32 devices in a mesh: dp: 8 (over z, y), pipe: 4 (over x, core).
Axes of the slice: x: 2, y: 2, z: 4, core: 2. Of those that a mesh axis runs over, the one named last changes fastest.
Arguments:
- numeric: float32 [8192, 128], P('dp'), may hold values from -6 to 6
- categories: int32 [8192, 24], P('dp'), may hold values from 0 to 255, as said below
- cardinalities: int32 [24], replicated, may hold values from 64 to 256, as said below
- embed_table: bfloat16 [24, 256, 16], replicated, may hold values from -6 to 6
- bn_gain: float32 [2, 512], replicated, may hold values from 0.25 to 1.75
- bn_bias: float32 [2, 512], replicated, may hold values from -3 to 3
- mask_logits: float32 [12, 512], P('pipe'), may hold values from -5 to 5
- feature_allow: int32 [12, 512], P('pipe'), may hold values from 0 to 1, as said below
- gate_weight: bfloat16 [12, 1024, 1024], P('pipe'), may hold values from -0.1875 to 0.1875
- gate_bias: float32 [12, 1024], P('pipe'), may hold values from -3 to 3
- cand_weight: bfloat16 [12, 1024, 512], P('pipe'), may hold values from -0.1875 to 0.1875
- cand_bias: float32 [12, 512], P('pipe'), may hold values from -3 to 3
- out_grad: float32 [8192, 512], P('dp'), may hold values from -6 to 6
Outputs:
- block_out: float32 [8192, 512], P('dp', 'pipe')
- numeric_grad: float32 [8192, 128], P('dp', 'pipe')
- table_grad: float32 [24, 256, 16], replicated
- gain_grad: float32 [2, 512], replicated
- bias_grad: float32 [2, 512], replicated
- logit_grad: float32 [12, 512], P('pipe')
- gate_weight_grad: float32 [12, 1024, 1024], P('pipe')
- gate_bias_grad: float32 [12, 1024], P('pipe')
- cand_weight_grad: float32 [12, 1024, 512], P('pipe')
- cand_bias_grad: float32 [12, 512], P('pipe')
The draws below stay inside these ranges and needn't reach their ends.
Inputs may be any that keep to these rules, and one draw needn't show every extreme that they name: categories[r, c] is below cardinalities[c]. `cardinalities`: some column has exactly 256 categories. `feature_allow`: every segment allows at least one feature.
All inputs are finite; a program needn't handle non-finite values.
Results may differ from the reference program's by a relative error of at most 0.0128.
The reference program's roundings to bfloat16 on the way count: a program that leaves them out, or rounds other values in their place, can miss the bound.
Values may be sent and summed in bfloat16 or wider, within the bound.
No kernel may reach another device: no remote copies, remote signals or barrier semaphores. Data moves between devices by JAX's collectives and lax.ppermute only.
A program may use at most 192 MiB of HBM per device.

```python
import jax
import jax.numpy as jnp
from jax import lax

F = 512
NUM = 128
NCAT = 24
EDIM = 16
CARD = 256
SECTION = 3
MB = 8
ROWS_MB = 128
SEGMENTS = 12
ROWS = 8192
N_DP = 8


def column_levels(key):
    first_key = jax.random.fold_in(key, 101)
    second_key = jax.random.fold_in(key, 102)
    levels = jax.random.randint(first_key, (NCAT,), CARD // 4, CARD + 1)
    chosen = jax.random.randint(second_key, (), 0, NCAT)
    return jnp.where(jnp.arange(NCAT) == chosen, CARD, levels).astype(jnp.int32)


def draw_cardinalities(key, part):
    return column_levels(key)


def draw_categories(key, part):
    levels = column_levels(key)
    key = jax.random.fold_in(key, 3)
    return jax.random.randint(key, (ROWS, NCAT), 0, levels[None, :]).astype(jnp.int32)


def draw_feature_allow(key, part):
    key = jax.random.fold_in(key, 5)
    first_key, second_key = jax.random.split(key)
    tosses = jax.random.randint(first_key, (SEGMENTS, F), 0, 4)
    forced = jax.random.randint(second_key, (SEGMENTS, 1), 0, F)
    allowed = (tosses > 0) | (jnp.arange(F)[None, :] == forced)
    return allowed.astype(jnp.int32)


def steps_of(own_key, dims, cuts, low, high):
    def one(position, parts):
        draws = jax.random.uniform(jax.random.fold_in(jax.random.fold_in(own_key, 6), position), (parts,), jnp.float32, low / len(cuts), high / len(cuts))
        return jnp.repeat(jnp.exp(draws), dims[position] // parts).reshape((-1,) + (1,) * (len(dims) - position - 1))

    level = one(*cuts[0])
    for cut in cuts[1:]:
        level = level * one(*cut)
    return level


def scatter_about(own_key, shape, width, limit, cuts=(), held_as=jnp.bfloat16):
    drawn = width * jax.random.normal(own_key, shape, jnp.float32)
    if cuts:
        drawn = drawn * steps_of(own_key, shape, cuts, -0.22, 0.18)
    return jnp.clip(drawn, -limit, limit).astype(held_as)


def setup_inputs(seed: int = 0) -> dict:
    key_list = jax.random.split(jax.random.key(seed), 14)
    return {
        "numeric": scatter_about(key_list[0], (ROWS, NUM), 1.0, 6.0, ((0, 8),), jnp.float32),
        "categories": draw_categories(jax.random.fold_in(key_list[13], 71), 0),
        "cardinalities": draw_cardinalities(jax.random.fold_in(key_list[13], 71), 0),
        "embed_table": scatter_about(key_list[3], (NCAT, CARD, EDIM), 1.0, 6.0),
        "bn_gain": jnp.clip(1.0 + 0.15 * jax.random.normal(key_list[4], (2, F), jnp.float32), 0.25, 1.75),
        "bn_bias": scatter_about(key_list[5], (2, F), 0.5, 3.0, (), jnp.float32),
        "mask_logits": scatter_about(key_list[6], (SEGMENTS, F), 1.0, 5.0, ((0, 4),), jnp.float32),
        "feature_allow": draw_feature_allow(jax.random.fold_in(key_list[13], 71), 0),
        "gate_weight": scatter_about(key_list[8], (SEGMENTS, 2 * F, 2 * F), (2 * F) ** -0.5, 0.1875, ((0, 4),)),
        "gate_bias": scatter_about(key_list[9], (SEGMENTS, 2 * F), 0.5, 3.0, ((0, 4),), jnp.float32),
        "cand_weight": scatter_about(key_list[10], (SEGMENTS, 2 * F, F), (2 * F) ** -0.5, 0.1875, ((0, 4),)),
        "cand_bias": scatter_about(key_list[11], (SEGMENTS, F), 0.5, 3.0, ((0, 4),), jnp.float32),
        "out_grad": scatter_about(key_list[12], (ROWS, F), 1.0, 6.0, ((0, 8),), jnp.float32),
    }


@jax.custom_vjp
def low(v):
    return lax.optimization_barrier(v.astype(jnp.bfloat16)).astype(jnp.float32)

@jax.custom_vjp
def low_back(v):
    return v

def low_keep(v):
    return (low(v), None)

def low_pass(kept, grad):
    return (grad,)

def back_keep(v):
    return (v, None)

def back_low(kept, grad):
    return (low(grad),)
low.defvjp(low_keep, low_pass)
low_back.defvjp(back_keep, back_low)
eps_norm = 1e-05
highest = lax.Precision.HIGHEST

def sent(value):
    return low_back(low(value))

def feature_scale(logits, allow):
    allowed = allow > 0
    largest = lax.optimization_barrier(jnp.max(jnp.where(allowed, logits, -1e+30), axis=-1, keepdims=True))
    raised = jnp.where(allowed, jnp.exp(jnp.where(allowed, logits - largest, 0.0)), 0.0)
    return F * raised / lax.optimization_barrier(jnp.sum(raised, axis=-1, keepdims=True))

def batch_norm(values, norm_gain, norm_bias):
    average = lax.optimization_barrier(jnp.mean(values, axis=0))
    centred = values - average
    variance = lax.optimization_barrier(jnp.mean(centred * centred, axis=0))
    return centred * lax.rsqrt(variance + eps_norm) * norm_gain + norm_bias

def embed(category_rows, column_sizes, table):
    levels = jnp.arange(CARD, dtype=jnp.int32)
    matches = (category_rows[:, :, None] == levels) & (levels < column_sizes[:, None])
    onehot = matches.astype(jnp.float32)
    embedded = jnp.einsum('rcv,cve->rce', onehot, table, precision=highest)
    return low_back(embedded.reshape(category_rows.shape[0], NCAT * EDIM))

def gated_segment(hidden, inputs, scale, w_gate, b_gate, w_cand, b_cand):
    hidden_width = hidden.shape[1]
    masked = low(inputs * scale)
    gate_input = jnp.concatenate([low(hidden), masked], axis=1)
    gate_pre = low_back(jnp.dot(gate_input, w_gate, precision=highest) + b_gate)
    update_gate = jax.nn.sigmoid(gate_pre[:, :hidden_width])
    reset_gate = jax.nn.sigmoid(gate_pre[:, hidden_width:])
    cand_input = jnp.concatenate([low(reset_gate * hidden), masked], axis=1)
    candidate = jnp.tanh(low_back(jnp.dot(cand_input, w_cand, precision=highest) + b_cand))
    return (1.0 - update_gate) * hidden + update_gate * candidate

def forward(numeric_rows, table, norm_gain, norm_bias, logits, w_gate, b_gate, w_cand, b_cand, category_rows, column_sizes, allow):
    features = jnp.concatenate([numeric_rows, embed(category_rows, column_sizes, table)], axis=1)
    scales = feature_scale(logits, allow)
    layer_span = SEGMENTS // 2
    segment_step = jax.checkpoint(gated_segment)
    hidden = features
    inputs = features
    for s in range(SEGMENTS):
        if s % layer_span == 0:
            source = features if s == 0 else sent(hidden)
            inputs = batch_norm(source, norm_gain[s // layer_span], norm_bias[s // layer_span])
            hidden = jnp.zeros_like(inputs)
        elif s % SECTION == 0:
            hidden = sent(hidden)
            inputs = sent(inputs)
        hidden = segment_step(hidden, inputs, scales[s], w_gate[s], b_gate[s], w_cand[s], b_cand[s])
    return hidden

def reference(numeric, categories, cardinalities, embed_table, bn_gain, bn_bias, mask_logits, feature_allow, gate_weight, gate_bias, cand_weight, cand_bias, out_grad):

    def by_batch(array):
        shaped = array.reshape((N_DP, MB, ROWS_MB) + array.shape[1:])
        return jnp.swapaxes(shaped, 0, 1).reshape((MB, N_DP * ROWS_MB) + array.shape[1:])

    def by_rows(array):
        shaped = array.reshape((MB, N_DP, ROWS_MB) + array.shape[2:])
        return jnp.swapaxes(shaped, 0, 1).reshape((N_DP * MB * ROWS_MB,) + array.shape[2:])
    params = (embed_table.astype(jnp.float32), bn_gain, bn_bias, mask_logits, gate_weight.astype(jnp.float32), gate_bias, cand_weight.astype(jnp.float32), cand_bias)
    zero_grads = jax.tree.map(jnp.zeros_like, params)

    def one_batch(running, pieces):
        numeric_part, category_part, cotangent = pieces

        def run_layers(numeric_rows, *weights):
            return forward(numeric_rows, *weights, category_part, cardinalities, feature_allow)
        result, pullback = jax.vjp(run_layers, numeric_part, *params)
        gradients = pullback(cotangent)
        running = jax.tree.map(jnp.add, running, tuple(gradients[1:]))
        return (running, (result, gradients[0]))
    totals, (results, numeric_grads) = lax.scan(one_batch, zero_grads, (by_batch(numeric), by_batch(categories), by_batch(out_grad)))
    return (by_rows(results), by_rows(numeric_grads), totals[0], totals[1], totals[2], totals[3], totals[4], totals[5], totals[6], totals[7])
```

```python
import jax
import jax.numpy as jnp
from jax import lax
from jax.sharding import PartitionSpec as P

MB = 8
ROWS_MB = 128
EPS = 1e-05
BF = jnp.bfloat16
F32 = jnp.float32


def feature_share(logits, allow):
    allowed = allow > 0
    largest = jnp.max(jnp.where(allowed, logits, -1e30), axis=-1, keepdims=True)
    raised = jnp.where(allowed, jnp.exp(jnp.where(allowed, logits - largest, 0.0)), 0.0)
    return raised / jnp.sum(raised, axis=-1, keepdims=True)


def core_swap(value):
    return lax.ppermute(value, "pipe", [(i, i ^ 1) for i in range(lax.axis_size("pipe"))])


def to_layer(value, up):
    half = lax.axis_size("pipe") // 2
    pairs = [(i, i + half) if up else (i + half, i) for i in range(half)]
    return lax.ppermute(value, "pipe", pairs)


def dp_swap(value, step):
    return lax.ppermute(value, "dp", [(i, i ^ step) for i in range(lax.axis_size("dp"))])


def dp_moments(source, count):
    mean = jnp.mean(source, axis=1)
    centred = source - mean[:, None, :]
    spread = jnp.sum(centred * centred, axis=1)
    step, held = 1, count
    while step < lax.axis_size("dp"):
        other_mean, other_spread = dp_swap((mean, spread), step)
        gap = mean - other_mean
        spread = spread + other_spread + gap * gap * (0.5 * held)
        mean = 0.5 * (mean + other_mean)
        held, step = held * 2, step * 2
    return mean, lax.rsqrt(spread / held + EPS)


def dp_total(value):
    step = 1
    while step < lax.axis_size("dp"):
        value = value + dp_swap(value, step)
        step *= 2
    return value


def rounded(value):
    return lax.reduce_precision(value, 8, 7)


def dot(a, b, dims):
    return lax.dot_general(a, b, ((dims[0], dims[1]), ((), ())), preferred_element_type=F32)


def layer_forward(x, scales, wg, bg, wc, bc):
    width = x.shape[1]
    h = jnp.zeros_like(x)
    kept = []
    for k in range(wg.shape[0]):
        if k == wg.shape[0] // 2:
            h, x = rounded(h), rounded(x)
        m = (x * scales[k]).astype(BF)
        hb = h.astype(BF)
        pre = dot(jnp.concatenate([hb, m], 1), wg[k], ((1,), (0,))) + bg[k]
        z, r = jax.nn.sigmoid(pre[:, :width]), jax.nn.sigmoid(pre[:, width:])
        rh = (r * h).astype(BF)
        c = jnp.tanh(dot(jnp.concatenate([rh, m], 1), wc[k], ((1,), (0,))) + bc[k])
        kept.append((h, z, r, c, hb, m, rh, x))
        h = (1.0 - z) * h + z * c
    return h, kept


def layer_backward(g, kept, scales, wg, wc):
    width = g.shape[1]
    gx = jnp.zeros_like(g)
    gates, cands, gscales = [], [], []
    count = wg.shape[0]
    for k in reversed(range(count)):
        h, z, r, c, hb, m, rh, x = kept[k]
        gc = (g * z * (1.0 - c * c)).astype(BF)
        back_c = dot(gc, wc[k], ((1,), (1,)))
        reset_h = back_c[:, :width]
        gg = jnp.concatenate([g * (c - h) * z * (1.0 - z), reset_h * h * r * (1.0 - r)], 1).astype(BF)
        back_g = dot(gg, wg[k], ((1,), (1,)))
        g = g * (1.0 - z) + reset_h * r + back_g[:, :width]
        gm = back_c[:, width:] + back_g[:, width:]
        gscales.append(jnp.sum(gm * x, axis=0))
        gx = gx + gm * scales[k]
        if k == count // 2:
            g, gx = rounded(g), rounded(gx)
        gates.append(gg)
        cands.append(gc)
    return gx, gates[::-1], cands[::-1], jnp.stack(gscales[::-1])


def on_device(numeric, categories, cardinalities, embed_table, bn_gain, bn_bias, mask_logits,
              feature_allow, gate_weight, gate_bias, cand_weight, cand_bias, out_grad):
    rank = lax.axis_index("pipe")
    core = rank % 2
    first_core = core == 0
    top = rank >= lax.axis_size("pipe") // 2
    width = out_grad.shape[1]
    numeric_width = numeric.shape[1]
    columns, levels, embed_width = embed_table.shape
    batches = MB // 2
    rows = batches * ROWS_MB
    counted = ROWS_MB * lax.axis_size("dp")

    def my_rows(array):
        return lax.dynamic_slice_in_dim(array, core * rows, rows, 0)

    def by_batch(array):
        return array.reshape(batches, ROWS_MB, array.shape[-1])

    shares = feature_share(mask_logits, feature_allow)
    own = (width * shares, gate_weight, gate_bias, cand_weight, cand_bias)
    others = core_swap(own)
    low = [jnp.where(first_core, a, b) for a, b in zip(own, others)]
    high = [jnp.where(first_core, b, a) for a, b in zip(own, others)]
    scales, wg, bg, wc, bc = [jnp.concatenate([a, b], 0) for a, b in zip(low, high)]

    cats = my_rows(categories)
    onehot = (cats[:, :, None] == jnp.arange(levels, dtype=jnp.int32)) & (
        jnp.arange(levels, dtype=jnp.int32) < cardinalities[:, None])
    onehot = onehot.astype(BF)
    embedded = jnp.einsum("rcv,cve->rce", onehot, embed_table, preferred_element_type=F32)
    source1 = jnp.concatenate([my_rows(numeric), embedded.reshape(rows, columns * embed_width)], 1)

    def norm(source, layer):
        mean, spread = dp_moments(by_batch(source), ROWS_MB)
        xhat = (by_batch(source) - mean[:, None]) * spread[:, None]
        return xhat, spread, (xhat * bn_gain[layer] + bn_bias[layer]).reshape(rows, width)

    def norm_back(g, xhat, spread, layer):
        g = by_batch(g)
        sums = jnp.stack([jnp.sum(g, axis=1), jnp.sum(g * xhat, axis=1)])
        totals = dp_total(sums) / counted
        back = bn_gain[layer] * spread[:, None] * (g - totals[0][:, None] - xhat * totals[1][:, None])
        return back.reshape(rows, width), jnp.sum(sums, axis=1)

    xhat1, spread1, x1 = norm(source1, 0)
    h1, kept1 = layer_forward(x1, scales, wg, bg, wc, bc)
    source2 = to_layer(h1.astype(BF), True).astype(F32)
    xhat2, spread2, x2 = norm(source2, 1)
    h2, kept2 = layer_forward(x2, scales, wg, bg, wc, bc)
    gx2, gates2, cands2, gscale2 = layer_backward(my_rows(out_grad), kept2, scales, wg, wc)
    back2, sums2 = norm_back(gx2, xhat2, spread2, 1)
    g1 = to_layer(back2.astype(BF), False).astype(F32)
    gx1, gates1, cands1, gscale1 = layer_backward(g1, kept1, scales, wg, wc)
    back1, sums1 = norm_back(gx1, xhat1, spread1, 0)

    def pick(a, b):
        return jnp.where(top, a, b)

    gate_grads, cand_grads, gate_sums, cand_sums = [], [], [], []
    for k in range(wg.shape[0]):
        gg, gc = pick(gates2[k], gates1[k]), pick(cands2[k], cands1[k])
        hb, m, rh = [pick(kept2[k][i], kept1[k][i]) for i in (4, 5, 6)]
        gate_grads.append(dot(jnp.concatenate([hb, m], 1), gg, ((0,), (0,))))
        cand_grads.append(dot(jnp.concatenate([rh, m], 1), gc, ((0,), (0,))))
        gate_sums.append(jnp.sum(gg.astype(F32), axis=0))
        cand_sums.append(jnp.sum(gc.astype(F32), axis=0))

    def to_owner(stacked, dtype):
        half = len(stacked) // 2
        a, b = jnp.stack(stacked[:half]), jnp.stack(stacked[half:])
        sent = jnp.where(first_core, b, a).astype(dtype)
        return jnp.where(first_core, a, b) + core_swap(sent).astype(F32)

    gate_w = to_owner(gate_grads, BF).astype(BF)
    cand_w = to_owner(cand_grads, BF).astype(BF)
    gate_b, cand_b = to_owner(gate_sums, F32), to_owner(cand_sums, F32)
    gscale = pick(gscale2, gscale1)
    gscale = to_owner([gscale[k] for k in range(gscale.shape[0])], F32)
    gate_w, cand_w = lax.psum((gate_w, cand_w), "dp")
    gate_b, cand_b, gscale = lax.psum((gate_b, cand_b, gscale), "dp")
    scaled = width * gscale
    logit = shares * (scaled - jnp.sum(shares * scaled, axis=-1, keepdims=True))

    gemb = back1[:, numeric_width:].astype(BF).reshape(rows, columns, embed_width)
    table = jnp.einsum("rcv,rce->cve", onehot, gemb, preferred_element_type=F32)
    table = jnp.where(top, 0.0, table)
    sums = jnp.stack([jnp.where(top, 0.0, sums1), jnp.where(top, sums2, 0.0)], axis=1)
    table, sums = lax.psum((table, sums), ("dp", "pipe"))

    def to_columns(mine, source_top):
        half = mine.shape[1] // 2
        share = half // 2
        pieces = mine.reshape(rows, 2, 2, share)
        kept = jnp.where(first_core, pieces[:, :, 0], pieces[:, :, 1])
        sent = jnp.where(first_core, pieces[:, :, 1], pieces[:, :, 0])
        got = core_swap(sent)
        both = jnp.where(first_core, jnp.stack([kept, got]), jnp.stack([got, kept]))
        both = both.reshape(2 * rows, 2, share)
        if source_top:
            return jnp.where(top, both[:, 1], to_layer(both[:, 0], False))
        return jnp.where(top, to_layer(both[:, 1], True), both[:, 0])

    block_out = to_columns(h2, True)
    numeric_grad = to_columns(back1[:, :numeric_width], False)
    return (block_out, numeric_grad, table, sums[1], sums[0], logit,
            gate_w.astype(F32), gate_b, cand_w.astype(F32), cand_b)


def solution(mesh):
    in_specs = (P("dp", None), P("dp", None), P(), P(), P(), P(), P("pipe", None), P("pipe", None),
                P("pipe", None, None), P("pipe", None), P("pipe", None, None), P("pipe", None),
                P("dp", None))
    out_specs = (P("dp", "pipe"), P("dp", "pipe"), P(), P(), P(), P("pipe", None),
                 P("pipe", None, None), P("pipe", None), P("pipe", None, None), P("pipe", None))
    return jax.shard_map(on_device, mesh=mesh, in_specs=in_specs, out_specs=out_specs, check_vma=False)
```

```python
import functools

import jax
import jax.numpy as jnp
from jax import lax
from jax.experimental import pallas as pl
from jax.experimental.pallas import tpu as pltpu
from jax.sharding import PartitionSpec as P

MB = 8
ROWS_MB = 128
BLOCK = 256
EPS = 1e-05
BF = jnp.bfloat16
F32 = jnp.float32


def feature_share(logits, allow):
    allowed = allow > 0
    largest = jnp.max(jnp.where(allowed, logits, -1e30), axis=-1, keepdims=True)
    raised = jnp.where(allowed, jnp.exp(jnp.where(allowed, logits - largest, 0.0)), 0.0)
    return raised / jnp.sum(raised, axis=-1, keepdims=True)


def core_swap(value):
    return lax.ppermute(value, "pipe", [(i, i ^ 1) for i in range(lax.axis_size("pipe"))])


def to_layer(value, up):
    half = lax.axis_size("pipe") // 2
    pairs = [(i, i + half) if up else (i + half, i) for i in range(half)]
    return lax.ppermute(value, "pipe", pairs)


def dp_swap(value, step):
    return lax.ppermute(value, "dp", [(i, i ^ step) for i in range(lax.axis_size("dp"))])


def dp_moments(both, count):
    step, held = 1, count
    while step < lax.axis_size("dp"):
        other = dp_swap(both, step)
        gap = both[0] - other[0]
        both = jnp.stack([0.5 * (both[0] + other[0]), both[1] + other[1] + gap * gap * (0.5 * held)])
        held, step = held * 2, step * 2
    return jnp.stack([both[0], lax.rsqrt(both[1] / held + EPS)])


def dp_total(value):
    step = 1
    while step < lax.axis_size("dp"):
        value = value + dp_swap(value, step)
        step *= 2
    return value


def plus(a, b):
    return lax.reduce_precision(a.astype(F32) + b.astype(F32), 8, 7).astype(BF)


def halves(value, second):
    mid = value.shape[0] // 2
    a, b = value[:mid], value[mid:]
    return jnp.where(second, b, a), jnp.where(second, a, b)


def joined(kept, got, second):
    return jnp.where(second, jnp.concatenate([got, kept]), jnp.concatenate([kept, got]))


def rounded(value):
    return lax.reduce_precision(value, 8, 7)


def dot(a, b, dims):
    return lax.dot_general(a, b, ((dims[0], dims[1]), ((), ())), preferred_element_type=F32)


def sigmoid(v):
    return 0.5 * jnp.tanh(0.5 * v) + 0.5


def low(v):
    return v.astype(BF).astype(F32)


def nn(a, b):
    return lax.dot_general(a, b, (((1,), (0,)), ((), ())), preferred_element_type=F32)


def nt(a, b):
    return lax.dot_general(a, b, (((1,), (1,)), ((), ())), preferred_element_type=F32)


def column_sum(v):
    return jnp.sum(v, axis=0, keepdims=True)


def batch_rows(i):
    return slice(i * ROWS_MB, (i + 1) * ROWS_MB)


def when_active(layer):
    rank = lax.axis_index("pipe")
    return rank // (lax.axis_size("pipe") // 2) == layer


class Weights:
    def __init__(self, refs, scratch, segments):
        self.own_gate, self.other_gate, self.own_cand, self.other_cand = refs
        self.gate, self.cand, self.sems = scratch
        self.segments = list(segments)
        self.base = min(self.segments)

    def start(self):
        core = lax.axis_index("pipe") % 2
        per_core = self.own_gate.shape[0]
        for k in self.segments:
            i, slot = k % per_core, k - self.base

            def begin(gate, cand):
                pltpu.make_async_copy(gate.at[i], self.gate.at[slot], self.sems.at[0, slot]).start()
                pltpu.make_async_copy(cand.at[i], self.cand.at[slot], self.sems.at[1, slot]).start()

            pl.when(core == k // per_core)(functools.partial(begin, self.own_gate, self.own_cand))
            pl.when(core != k // per_core)(functools.partial(begin, self.other_gate, self.other_cand))

    def wait(self, k):
        slot = k - self.base
        pltpu.make_async_copy(self.own_gate.at[0], self.gate.at[slot], self.sems.at[0, slot]).wait()
        pltpu.make_async_copy(self.own_cand.at[0], self.cand.at[slot], self.sems.at[1, slot]).wait()


def normalise(source, moments, affine, x):
    for i in range(source.shape[0] // ROWS_MB):
        at = batch_rows(i)
        xhat = (source[at, :].astype(F32) - moments[0, i : i + 1, :]) * moments[1, i : i + 1, :]
        x[at, :] = xhat * affine[0:1, :] + affine[1:2, :]


def run_forward(x, scales, gate_bias, cand_bias, weights, h, keep=None, after=None):
    rows, width = x.shape
    count = scales.shape[0]
    section = count // 2
    blocks = [slice(i, i + BLOCK) for i in range(0, rows, BLOCK)]

    def spot(k):
        return k if keep else k % 2

    weights.wait(0)
    for at in blocks:
        m = (x[at, :] * scales[0:1, :]).astype(BF)
        zz = sigmoid(nn(m, weights.gate[0, width:, :width]) + gate_bias[0:1, :width])
        cc = jnp.tanh(nn(m, weights.cand[0, width:, :]) + cand_bias[0:1, :])
        h[1, at, :] = zz * cc
        if keep:
            z, r, c, operands = keep
            z[0, at, :], c[0, at, :] = zz, cc
            operands[0, at, width : 2 * width] = m
    if keep:
        after(0)

    def segment(k, _):
        weights.wait(k)
        if keep:
            after.before(k)

        @pl.when(k == section)
        def _():
            x[...] = low(x[...])
            h[spot(k)] = low(h[spot(k)])

        for at in blocks:
            hh = h[spot(k), at, :]
            hb = hh.astype(BF)
            m = (x[at, :] * scales[pl.ds(k, 1), :]).astype(BF)
            pre = nn(jnp.concatenate([hb, m], 1), weights.gate[k]) + gate_bias[pl.ds(k, 1), :]
            rr = sigmoid(pre[:, width:])
            rh = (rr * hh).astype(BF)
            zz = sigmoid(pre[:, :width])
            cc = jnp.tanh(nn(jnp.concatenate([rh, m], 1), weights.cand[k]) + cand_bias[pl.ds(k, 1), :])
            if keep:
                z[k, at, :], r[k, at, :], c[k, at, :] = zz, rr, cc
                slot = k % 2
                operands[slot, at, :width] = hb
                operands[slot, at, width : 2 * width] = m
                operands[slot, at, 2 * width :] = rh
            h[spot(k + 1), at, :] = (1.0 - zz) * hh + zz * cc
        if keep:
            after(k)
        return 0

    lax.fori_loop(1, count, segment, 0)


class Out:
    def __init__(self, slotted, sems, kept=(), kept_sems=None):
        self.slotted, self.sems, self.kept, self.kept_sems = slotted, sems, kept, kept_sems

    def slot_copy(self, k):
        source, target = self.slotted
        return pltpu.make_async_copy(source.at[k % 2], target.at[k], self.sems.at[k % 2])

    def kept_copies(self, k):
        return [
            pltpu.make_async_copy(source.at[k], target.at[k], self.kept_sems.at[i, k])
            for i, (source, target) in enumerate(self.kept)
        ]

    def before(self, k):
        @pl.when(k >= 2)
        def _():
            self.slot_copy(k - 2).wait()

    def __call__(self, k):
        self.slot_copy(k).start()
        for copy in self.kept_copies(k):
            copy.start()

    def finish(self, count):
        self.slot_copy(count - 2).wait()
        self.slot_copy(count - 1).wait()
        if self.kept:
            def wait(k, _):
                for copy in self.kept_copies(k):
                    copy.wait()
                return 0
            lax.fori_loop(0, count, wait, 0)


def run_backward(segments, base, g, gx, x, scales, weights, h, z, r, c, grads, sums, out, arrive, terms=None):
    rows, width = g.shape
    blocks = [slice(i, i + BLOCK) for i in range(0, rows, BLOCK)]
    high = max(segments)

    def segment(i, _):
        k = high - i
        s = k - base
        arrive(k)

        @pl.when(i >= 2)
        def _():
            out(k + 2).wait()

        totals = None
        for at in blocks:
            gg, hh, zz, rr, cc = g[at, :], h[s, at, :], z[s, at, :], r[s, at, :], c[s, at, :]
            gc = (gg * zz * (1.0 - cc * cc)).astype(BF)
            back_c = nt(gc, weights.cand[s])
            reset_h = back_c[:, :width]
            gate_z = (gg * (cc - hh) * zz * (1.0 - zz)).astype(BF)
            gate_r = (reset_h * hh * rr * (1.0 - rr)).astype(BF)
            gates = jnp.concatenate([gate_z, gate_r], 1)
            back_g = nt(gates, weights.gate[s])
            g[at, :] = gg * (1.0 - zz) + reset_h * rr + back_g[:, :width]
            gm = back_c[:, width:] + back_g[:, width:]
            gx[at, :] = gx[at, :] + gm * scales[pl.ds(k, 1), :]
            grads[k % 2, at, : 2 * width] = gates
            grads[k % 2, at, 2 * width :] = gc
            part = jnp.concatenate([column_sum(gates.astype(F32)), column_sum(gc.astype(F32)),
                                    column_sum(gm * x[at, :])], 1)
            totals = part if totals is None else totals + part
            if terms:
                terms.stage(at, (x[at, :] * scales[pl.ds(k, 1), :]).astype(BF), hh.astype(BF), (rr * hh).astype(BF))
        sums[pl.ds(s, 1), :] = totals
        out(k).start()
        if terms:
            terms.add(s, grads.at[k % 2])
        return 0

    full = [k for k in segments if k > 0]
    lax.fori_loop(0, len(full), segment, 0)
    if min(segments) == 0:
        arrive(0)
        if len(full) >= 2:
            out(2).wait()
        totals = None
        for at in blocks:
            gg, zz, cc = g[at, :], z[0, at, :], c[0, at, :]
            gc = (gg * zz * (1.0 - cc * cc)).astype(BF)
            gate_z = (gg * cc * zz * (1.0 - zz)).astype(BF)
            gm = nt(gc, weights.cand[0, width:, :]) + nt(gate_z, weights.gate[0, width:, :width])
            gx[at, :] = gx[at, :] + gm * scales[0:1, :]
            grads[0, at, :width] = gate_z
            grads[0, at, width : 2 * width] = gc
            part = jnp.concatenate([column_sum(gate_z.astype(F32)), jnp.zeros((1, width), F32),
                                    column_sum(gc.astype(F32)), column_sum(gm * x[at, :])], 1)
            totals = part if totals is None else totals + part
            if terms:
                terms.stage(at, (x[at, :] * scales[0:1, :]).astype(BF), None, None)
        sums[0:1, :] = totals
        out(0).start()
        if terms:
            terms.add_first(grads.at[0])
        out(1).wait()
        out(0).wait()
    else:
        out(min(segments) + 1).wait()
        out(min(segments)).wait()


def tn(a, b):
    return lax.dot_general(a, b, (((0,), (0,)), ((), ())), preferred_element_type=F32)


class Terms:
    def __init__(self, keep, a, b, result):
        self.upper = (lax.axis_index("pipe") % 2 == 0) == keep
        self.a, self.b, self.result = a, b, result
        self.width = a.shape[-1]

    def stage(self, at, m, hb, rh):
        self.a[at, :] = m if hb is None else jnp.where(self.upper, hb, m)
        if rh is not None:
            self.b[at, :] = jnp.where(self.upper, rh, m)

    def add(self, slot, grads, per_section=3):
        w = self.width
        gates = tn(self.a[...], grads[:, : 2 * w]).astype(BF)
        cands = tn(self.b[...], grads[:, 2 * w :]).astype(BF)
        if isinstance(slot, int):
            start = (per_section - 1 - slot) * 3 * w
            self.result[:, start : start + 2 * w] = gates
            self.result[:, start + 2 * w : start + 3 * w] = cands
            return
        start = pl.multiple_of((per_section - 1 - slot) * 3 * w, w)
        self.result[:, pl.ds(start, 2 * w)] = gates
        self.result[:, pl.ds(pl.multiple_of(start + 2 * w, w), w)] = cands

    def add_first(self, grads, per_section=3):
        w = self.width
        start = (per_section - 1) * 3 * w
        at = pl.multiple_of(jnp.where(self.upper, 0, w), w)
        self.result[:, start : start + w] = tn(self.a[...], grads[:, pl.ds(at, w)]).astype(BF)


def terms_of_section(section, keep, operands, grads, buffers, sems, result):
    a, b, g = buffers
    per_section, rows, columns = grads.shape
    width = columns // 3
    upper = (lax.axis_index("pipe") % 2 == 0) == keep
    at_a = pl.multiple_of(jnp.where(upper, 0, width), width)
    at_b = pl.multiple_of(jnp.where(upper, 2 * width, width), width)
    loads = []
    for i in range(per_section - 1, -1, -1):
        k = section * per_section + i
        if k == 0:
            loads.append([(operands.at[0, :, pl.ds(width, width)], a.at[0]), (grads.at[0], g.at[0])])
        else:
            loads.append([(operands.at[k, :, pl.ds(at_a, width)], a.at[i]), (grads.at[i], g.at[i]),
                          (operands.at[k, :, pl.ds(at_b, width)], b.at[i])])
    loads = [[pltpu.make_async_copy(x, y, sems.at[i, j]) for j, (x, y) in enumerate(group)]
             for i, group in enumerate(loads)]
    for group in loads:
        for load in group:
            load.start()
    for i, group in zip(range(per_section - 1, -1, -1), loads):
        for load in group:
            load.wait()
        terms = Terms(keep, a.at[i], b.at[i], result)
        if section * per_section + i == 0:
            terms.add_first(g.at[0], per_section)
        else:
            terms.add(i, g.at[i], per_section)


def terms_scratch(per_section, rows, width):
    return [pltpu.VMEM((per_section, rows, width), BF), pltpu.VMEM((per_section, rows, width), BF),
            pltpu.VMEM((per_section, rows, 3 * width), BF), pltpu.SemaphoreType.DMA((per_section, 3))]


def section_columns(section, per_section, width):
    return (3 * per_section - (0 if section else 2)) * width


def kept_terms(section, operands, grads):
    per_section, rows, width = grads.shape
    width //= 3

    def kernel(operands, grads, result, a, b, g, sems):
        terms_of_section(section, True, operands, grads, (a, b, g), sems, result)

    return pl.pallas_call(
        kernel,
        out_shape=jax.ShapeDtypeStruct((width, section_columns(section, per_section, width)), BF),
        in_specs=[ANY, ANY],
        out_specs=VM,
        scratch_shapes=terms_scratch(per_section, rows, width),
        compiler_params=pltpu.CompilerParams(vmem_limit_bytes=LIMIT),
        name=f"kept_terms_{section}",
    )(operands, grads)


def norm_sums(gx, xhat_of, sums):
    for i in range(gx.shape[0] // ROWS_MB):
        part = gx[batch_rows(i), :]
        sums[0, i : i + 1, :] = column_sum(part)
        sums[1, i : i + 1, :] = column_sum(part * xhat_of(i))


def xhat_rows(source, moments, i):
    return (source[batch_rows(i), :].astype(F32) - moments[0, i : i + 1, :]) * moments[1, i : i + 1, :]


ANY = pl.BlockSpec(memory_space=pl.ANY)
VM = pl.BlockSpec(memory_space=pltpu.VMEM)
LIMIT = 62 * 1024 * 1024


def layer1_forward(source, moments, affine, scales, gate_bias, cand_bias, weights, keep):
    rows, width = source.shape
    count = scales.shape[0]

    def kernel(source, moments, affine, scales, gate_bias, cand_bias, w0, w1, w2, w3, *refs):
        if keep:
            kept_h, kept_z, kept_r, kept_c, operands_out = refs[:5]
            x, gate, cand, wsems, h, z, r, c, operands, osems, ksems = refs[5:]
        else:
            last, local = refs[:2]
            x, gate, cand, wsems, h = refs[2:]

        @pl.when(when_active(0))
        def _():
            held = Weights((w0, w1, w2, w3), (gate, cand, wsems), range(count))
            held.start()
            normalise(source, moments, affine, x)
            if keep:
                out = Out((operands, operands_out), osems,
                          ((h, kept_h), (z, kept_z), (r, kept_r), (c, kept_c)), ksems)
                run_forward(x, scales, gate_bias, cand_bias, held, h, (z, r, c, operands), out)
                out.finish(count)
                return
            run_forward(x, scales, gate_bias, cand_bias, held, h)
            final = h.at[count % 2]
            last[...] = final[...].astype(BF)
            for i in range(rows // ROWS_MB):
                part = low(final[batch_rows(i), :])
                mean = column_sum(part) * (1.0 / ROWS_MB)
                local[0, i : i + 1, :] = mean
                local[1, i : i + 1, :] = column_sum((part - mean) * (part - mean))

    state = jax.ShapeDtypeStruct((count, rows, width), F32)
    scratch = [pltpu.VMEM((rows, width), F32),
               pltpu.VMEM((count, 2 * width, 2 * width), BF),
               pltpu.VMEM((count, 2 * width, width), BF),
               pltpu.SemaphoreType.DMA((2, count))]
    if keep:
        out_shape = (state,) * 4 + (jax.ShapeDtypeStruct((count, rows, 3 * width), BF),)
        out_specs = (ANY,) * 5
        scratch += [pltpu.VMEM((count + 1, rows, width), F32)] + [pltpu.VMEM((count, rows, width), F32)] * 3
        scratch += [pltpu.VMEM((2, rows, 3 * width), BF), pltpu.SemaphoreType.DMA((2,)),
                    pltpu.SemaphoreType.DMA((4, count))]
    else:
        out_shape = (jax.ShapeDtypeStruct((rows, width), BF),
                     jax.ShapeDtypeStruct((2, rows // ROWS_MB, width), F32))
        out_specs = (VM, VM)
        scratch += [pltpu.VMEM((2, rows, width), F32)]
    return pl.pallas_call(
        kernel,
        out_shape=out_shape,
        in_specs=[VM] * 6 + [ANY] * 4,
        out_specs=out_specs,
        scratch_shapes=scratch,
        compiler_params=pltpu.CompilerParams(vmem_limit_bytes=LIMIT),
        name="layer1_states" if keep else "layer1_forward",
    )(source, moments, affine, scales, gate_bias, cand_bias, *weights)


def layer2_both(source, moments, affine, scales, gate_bias, cand_bias, weights, cotangent, operands_in):
    rows, width = source.shape
    count = scales.shape[0]

    def kernel(source, moments, affine, scales, gate_bias, cand_bias, w0, w1, w2, w3, cotangent, unused,
               last, gx_out, nsums, sums, operands_out, grads_high, grads_low,
               x, gate, cand, wsems, h, z, r, c, operands, osems, g, gx, gsem):
        @pl.when(when_active(1))
        def _():
            held = Weights((w0, w1, w2, w3), (gate, cand, wsems), range(count))
            held.start()
            core = lax.axis_index("pipe") % 2
            first = pl.multiple_of(core * rows, rows)
            load_g = pltpu.make_async_copy(cotangent.at[pl.ds(first, rows), :], g, gsem.at[0])
            load_g.start()
            normalise(source, moments, affine, x)
            out = Out((operands, operands_out), osems)
            run_forward(x, scales, gate_bias, cand_bias, held, h, (z, r, c, operands), out)
            last[...] = h[count]
            out.finish(count)
            load_g.wait()
            gx[...] = jnp.zeros_like(gx)

            section = count // 2

            def copy_high(k):
                return pltpu.make_async_copy(operands.at[k % 2], grads_high.at[k - section], osems.at[k % 2])

            def copy_low(k):
                return pltpu.make_async_copy(operands.at[k % 2], grads_low.at[k], osems.at[k % 2])

            def none(k):
                pass

            run_backward(range(section, count), 0, g, gx, x, scales, held, h, z, r, c, operands, sums,
                         copy_high, none)
            g[...] = low(g[...])
            gx[...] = low(gx[...])
            normalise(source, moments, affine, x)
            run_backward(range(section), 0, g, gx, x, scales, held, h, z, r, c, operands, sums,
                         copy_low, none)
            gx_out[...] = gx[...].astype(BF)
            norm_sums(gx, lambda i: xhat_rows(source, moments, i), nsums)

    state = pltpu.VMEM((count, rows, width), F32)
    half = jax.ShapeDtypeStruct((count // 2, rows, 3 * width), BF)
    return pl.pallas_call(
        kernel,
        out_shape=(jax.ShapeDtypeStruct((rows, width), F32),
                   jax.ShapeDtypeStruct((rows, width), BF),
                   jax.ShapeDtypeStruct((2, rows // ROWS_MB, width), F32),
                   jax.ShapeDtypeStruct((count, 4 * width), F32),
                   jax.ShapeDtypeStruct((count, rows, 3 * width), BF), half, half),
        in_specs=[VM] * 6 + [ANY] * 6,
        out_specs=(VM, VM, VM, VM, ANY, ANY, ANY),
        input_output_aliases={11: 4},
        scratch_shapes=[pltpu.VMEM((rows, width), F32),
                        pltpu.VMEM((count, 2 * width, 2 * width), BF),
                        pltpu.VMEM((count, 2 * width, width), BF),
                        pltpu.SemaphoreType.DMA((2, count)),
                        pltpu.VMEM((count + 1, rows, width), F32), state, state, state,
                        pltpu.VMEM((2, rows, 3 * width), BF),
                        pltpu.SemaphoreType.DMA((2,)),
                        pltpu.VMEM((rows, width), F32),
                        pltpu.VMEM((rows, width), F32),
                        pltpu.SemaphoreType.DMA((1,))],
        compiler_params=pltpu.CompilerParams(vmem_limit_bytes=LIMIT),
        name="layer2_both",
    )(source, moments, affine, scales, gate_bias, cand_bias, *weights, cotangent, operands_in)


def layer1_backward(section, carried, source, moments, affine, scales, weights, kept, operands, grads_in):
    upper = section == 1
    rows, width = source.shape
    count = scales.shape[0]
    half = count // 2
    base = half if upper else 0
    segments = range(base, base + half)

    def kernel(*refs):
        carried, refs = refs[: 5 if upper else 2], refs[5 if upper else 2 :]
        (source, moments, affine, scales, w0, w1, w2, w3, kept_h, kept_z, kept_r, kept_c, operands,
         grads_in) = refs[:14]
        refs = refs[14:]
        if upper:
            g, gx, sums, sent, grads_out = refs[:5]
        else:
            gx, nsums, sums, sent, grads_out = refs[:5]
        x, gate, cand, wsems, h, z, r, c, grads, osems, ksems, a, b, loaded, lsems = refs[5:20]
        if not upper:
            g = refs[20]

        @pl.when(when_active(1))
        def _():
            terms_of_section(section, False, operands, grads_in, (a, b, loaded), lsems, sent)

        @pl.when(when_active(0))
        def _():
            held = Weights((w0, w1, w2, w3), (gate, cand, wsems), list(segments)[::-1])
            states = ((kept_h, h), (kept_z, z), (kept_r, r), (kept_c, c))

            def copies(k):
                return [pltpu.make_async_copy(a.at[k], b.at[k - base], ksems.at[i, k - base])
                        for i, (a, b) in enumerate(states)]

            def arrive(k):
                held.wait(k)
                for copy in copies(k):
                    copy.wait()

            for k in list(segments)[::-1]:
                for copy in copies(k):
                    copy.start()
            held.start()
            normalise(source, moments, affine, x)
            if upper:
                x[...] = low(x[...])
                gxr, hb, moments2, totals, gain2 = carried
                for i in range(rows // ROWS_MB):
                    at = batch_rows(i)
                    back = (gxr[at, :].astype(F32) - totals[0, i : i + 1, :]
                            - xhat_rows(hb, moments2, i) * totals[1, i : i + 1, :])
                    g[at, :] = low(gain2[...] * moments2[1, i : i + 1, :] * back)
                gx[...] = jnp.zeros_like(gx)
            else:
                g[...] = carried[0][...]
                gx[...] = carried[1][...]

            def out(k):
                return pltpu.make_async_copy(grads.at[k % 2], grads_out.at[k - base], osems.at[k % 2])

            run_backward(segments, base, g, gx, x, scales, held, h, z, r, c, grads, sums, out, arrive,
                         Terms(False, a.at[0], b.at[0], sent))
            if upper:
                g[...] = low(g[...])
                gx[...] = low(gx[...])
            else:
                norm_sums(gx, lambda i: xhat_rows(source, moments, i), nsums)

    full = jax.ShapeDtypeStruct((rows, width), F32)
    rows_sums = jax.ShapeDtypeStruct((half, 4 * width), F32)
    outs = [full, full if upper else jax.ShapeDtypeStruct((2, rows // ROWS_MB, width), F32), rows_sums,
            jax.ShapeDtypeStruct((width, section_columns(section, half, width)), BF),
            jax.ShapeDtypeStruct((half, rows, 3 * width), BF)]
    state = pltpu.VMEM((half, rows, width), F32)
    args = list(carried) + [source, moments, affine, scales, *weights, *kept, operands, grads_in]
    return pl.pallas_call(
        kernel,
        out_shape=tuple(outs),
        in_specs=[VM] * (len(carried) + 4) + [ANY] * 10,
        out_specs=(VM, VM, VM, VM, ANY),
        input_output_aliases={len(args) - 1: 4},
        scratch_shapes=[pltpu.VMEM((rows, width), F32),
                        pltpu.VMEM((half, 2 * width, 2 * width), BF),
                        pltpu.VMEM((half, 2 * width, width), BF),
                        pltpu.SemaphoreType.DMA((2, half)),
                        state, state, state, state,
                        pltpu.VMEM((2, rows, 3 * width), BF),
                        pltpu.SemaphoreType.DMA((2,)),
                        pltpu.SemaphoreType.DMA((4, half))]
        + terms_scratch(half, rows, width)
        + ([] if upper else [pltpu.VMEM((rows, width), F32)]),
        compiler_params=pltpu.CompilerParams(vmem_limit_bytes=LIMIT),
        name="layer1_backward_upper" if upper else "layer1_backward_lower",
    )(*args)


def hot_rows(cats, c, levels):
    level = lax.broadcasted_iota(jnp.int32, (levels, cats.shape[1]), 0)
    return jnp.where(cats[c : c + 1, :] == level, 1.0, 0.0).astype(BF)


def load_columns(categories, cats, sem, rows):
    first = pl.multiple_of((lax.axis_index("pipe") % 2) * rows, rows)
    return pltpu.make_async_copy(categories.at[:, pl.ds(first, rows)], cats, sem)


def embed(numeric, categories, table, rows):
    numeric_width, columns = numeric.shape[1], categories.shape[0]
    embedded, levels = table.shape
    each = embedded // columns
    packed = 128 // each
    width = numeric_width + embedded

    def kernel(numeric, categories, table, source, local, cats, nums, sems):
        first = pl.multiple_of((lax.axis_index("pipe") % 2) * rows, rows)
        load = load_columns(categories, cats, sems.at[0], rows)
        load_numeric = pltpu.make_async_copy(numeric.at[pl.ds(first, rows), :], nums, sems.at[1])
        load.start()
        load_numeric.start()
        load.wait()
        row = lax.broadcasted_iota(jnp.int32, (128, levels), 0) // each
        for group in range(columns // packed):
            part = table[group * 128 : (group + 1) * 128, :]
            weights = jnp.concatenate([jnp.where(row == i, part, jnp.zeros_like(part)) for i in range(packed)], 1)
            hot = jnp.concatenate([hot_rows(cats, group * packed + i, levels) for i in range(packed)], 0)
            start = numeric_width + group * 128
            source[:, start : start + 128] = nn(weights, hot).T
        load_numeric.wait()
        source[:, :numeric_width] = nums[...]
        for i in range(rows // ROWS_MB):
            part = source[batch_rows(i), :]
            mean = column_sum(part) * (1.0 / ROWS_MB)
            local[0, i : i + 1, :] = mean
            local[1, i : i + 1, :] = column_sum((part - mean) * (part - mean))

    return pl.pallas_call(
        kernel,
        out_shape=(jax.ShapeDtypeStruct((rows, width), F32),
                   jax.ShapeDtypeStruct((2, rows // ROWS_MB, width), F32)),
        in_specs=[ANY, ANY, VM],
        out_specs=(VM, VM),
        scratch_shapes=[pltpu.VMEM((columns, rows), jnp.int32), pltpu.VMEM((rows, numeric_width), F32),
                        pltpu.SemaphoreType.DMA((2,))],
        compiler_params=pltpu.CompilerParams(vmem_limit_bytes=LIMIT),
        name="embed",
    )(numeric, categories, table)


def feature_grads(gx, source, moments, totals, gain, categories, table_shape):
    rows, width = gx.shape
    embedded, levels = table_shape
    columns = categories.shape[0]
    each = embedded // columns
    numeric_width = width - embedded

    def kernel(gx, source, moments, totals, gain, categories, numeric, table, cats, back, sem):
        load = load_columns(categories, cats, sem.at[0], rows)
        load.start()
        for i in range(rows // ROWS_MB):
            at = batch_rows(i)
            part = gx[at, :] - totals[0, i : i + 1, :] - xhat_rows(source, moments, i) * totals[1, i : i + 1, :]
            back[at, :] = gain[...] * moments[1, i : i + 1, :] * part
        numeric[...] = back[:, :numeric_width]
        load.wait()
        for group in range(embedded // 128):
            start = numeric_width + group * 128
            turned = back[:, start : start + 128].T.astype(BF)
            for i in range(128 // each):
                c = group * (128 // each) + i
                table[c * each : (c + 1) * each, :] = nt(turned[i * each : (i + 1) * each, :], hot_rows(cats, c, levels))

    return pl.pallas_call(
        kernel,
        out_shape=(jax.ShapeDtypeStruct((rows, numeric_width), F32), jax.ShapeDtypeStruct(table_shape, F32)),
        in_specs=[VM] * 5 + [ANY],
        out_specs=(VM, VM),
        scratch_shapes=[pltpu.VMEM((columns, rows), jnp.int32), pltpu.VMEM((rows, width), F32),
                        pltpu.SemaphoreType.DMA((1,))],
        compiler_params=pltpu.CompilerParams(vmem_limit_bytes=LIMIT),
        name="feature_grads",
    )(gx, source, moments, totals, gain, categories)


def ring_place(places):
    place = lax.axis_index("dp")
    spot = jnp.where(place % 2 == 0, place // 2, places - 1 - place // 2)
    return jnp.where(lax.axis_index("pipe") % 2 == 0, spot, places - 1 - spot)


def blank_outputs(per_core, width):
    def kernel(gate, cand, zeros, sems):
        @pl.when(lax.axis_index("pipe") % 2 == 0)
        def _():
            zeros[...] = jnp.zeros_like(zeros)
            copies = [
                pltpu.make_async_copy(zeros, gate.at[0, pl.ds(0, width), :], sems.at[0]),
                pltpu.make_async_copy(zeros.at[:, pl.ds(0, width)],
                                      gate.at[0, pl.ds(width, width), pl.ds(width, width)], sems.at[1]),
                pltpu.make_async_copy(zeros.at[:, pl.ds(0, width)], cand.at[0, pl.ds(0, width), :], sems.at[2])]
            for copy in copies:
                copy.start()
            for copy in copies:
                copy.wait()

    return pl.pallas_call(
        kernel,
        out_shape=(jax.ShapeDtypeStruct((per_core, 2 * width, 2 * width), F32),
                   jax.ShapeDtypeStruct((per_core, 2 * width, width), F32)),
        out_specs=(ANY, ANY),
        scratch_shapes=[pltpu.VMEM((width, 2 * width), F32), pltpu.SemaphoreType.DMA((3,))],
        name="blank_outputs",
    )()


def place_blocks(steps, blocks, mine, others, gate, cand):
    count = len(steps)
    rows = mine[0].shape[0]
    per_core, width = gate.shape[0], cand.shape[2]

    def kernel(*refs):
        mine, others = refs[:count], refs[count : 2 * count]
        gate, cand, full, sems = refs[2 * count + 2 :]
        spot = ring_place(blocks)

        def put(own_half, first_layer):
            copies = []
            for i, step in enumerate(steps):
                own_block = lax.rem(spot + 1 - step + blocks, blocks)
                others_block = lax.rem(2 * blocks - spot + step, blocks)
                for piece, half, block in ((mine[i], own_half, own_block), (others[i], 1 - own_half, others_block)):
                    full[i, half] = piece[...].astype(F32)
                    at = pl.multiple_of(block * rows, rows)
                    for j in range(per_core):
                        start = (per_core - 1 - j) * 3 * width
                        if first_layer and j == 0:
                            cuts = [(cand if half else gate, width + at, start, width)]
                        else:
                            cuts = [(gate, half * width + at, start, 2 * width),
                                    (cand, half * width + at, start + 2 * width, width)]
                        for target, row, column, size in cuts:
                            copies.append(pltpu.make_async_copy(
                                full.at[i, half, :, pl.ds(column, size)],
                                target.at[j, pl.ds(row, rows), pl.ds(0, size)], sems.at[len(copies)]))
                            copies[-1].start()
            for copy in copies:
                copy.wait()

        core = lax.axis_index("pipe") % 2
        pl.when(core == 0)(functools.partial(put, 0, True))
        pl.when(core == 1)(functools.partial(put, 1, False))

    return pl.pallas_call(
        kernel,
        out_shape=(jax.ShapeDtypeStruct(gate.shape, F32), jax.ShapeDtypeStruct(cand.shape, F32)),
        in_specs=[VM] * (2 * count) + [ANY] * 2,
        out_specs=(ANY, ANY),
        input_output_aliases={2 * count: 0, 2 * count + 1: 1},
        scratch_shapes=[pltpu.VMEM((count, 2) + mine[0].shape, F32),
                        pltpu.SemaphoreType.DMA((count * 4 * per_core,))],
        compiler_params=pltpu.CompilerParams(vmem_limit_bytes=LIMIT),
        name=f"place_blocks_{steps[0]}",
    )(*mine, *others, gate, cand)


def tied(*values):
    return lax.optimization_barrier(values)


class Ring:
    def __init__(self, parts=None, held=None):
        self.places = lax.axis_size("dp")
        order = list(range(0, self.places, 2)) + list(range(1, self.places, 2))[::-1]
        lanes = lax.axis_size("pipe")
        self.pairs = []
        for lane in range(lanes):
            way = order if lane % 2 == 0 else order[::-1]
            self.pairs += [(way[i] * lanes + lane, way[(i + 1) % self.places] * lanes + lane)
                           for i in range(self.places)]
        self.spot = ring_place(self.places)
        self.parts = parts
        self.done = 0
        self.held = held
        if parts:
            self.rows = parts[0].shape[0] // self.places
            self.held = lax.reduce_precision(self.block(self.spot), 8, 7).astype(BF)

    def block(self, number):
        at = lax.rem(number + self.places, self.places) * self.rows
        a, b = [lax.dynamic_slice_in_dim(part, at, self.rows, 0) for part in self.parts]
        return a.astype(F32) + b.astype(F32)

    def step(self, sends=(), work=None):
        self.done += 1
        inputs = tuple(work[1]) if work else ()
        tied_in = tied(self.held, *[value for _, value in sends], *inputs)
        held, values, inputs = tied_in[0], tied_in[1 : 1 + len(sends)], tied_in[1 + len(sends) :]
        got = lax.ppermute(held, ("dp", "pipe"), self.pairs)
        outs = [send(value) for (send, _), value in zip(sends, values)]
        if work:
            result = work[0](*inputs)
            outs += list(result) if isinstance(result, (tuple, list)) else [result]
        got, *outs = tied(got, *outs)
        if self.parts:
            got = lax.reduce_precision(self.block(self.spot - self.done) + got.astype(F32), 8, 7).astype(BF)
        self.held = got
        return outs


def on_device(numeric, categories, cardinalities, embed_table, bn_gain, bn_bias, mask_logits,
              feature_allow, gate_weight, gate_bias, cand_weight, cand_bias, out_grad):
    rank = lax.axis_index("pipe")
    core = rank % 2
    first_core = core == 0
    top = rank >= lax.axis_size("pipe") // 2
    width = out_grad.shape[1]
    numeric_width = numeric.shape[1]
    columns, levels, embed_width = embed_table.shape
    batches = MB // 2
    rows = batches * ROWS_MB
    counted = ROWS_MB * lax.axis_size("dp")

    def my_rows(array):
        return lax.dynamic_slice_in_dim(array, core * rows, rows, 0)

    def by_batch(array):
        return array.reshape(batches, ROWS_MB, array.shape[-1])

    flat_table = jnp.swapaxes(embed_table, 1, 2).reshape(columns * embed_width, levels)
    category_columns = categories.T
    source1, local1 = embed(numeric, category_columns, flat_table, rows)
    local1, mask_logits = lax.optimization_barrier((local1, mask_logits))
    shares = feature_share(mask_logits, feature_allow)
    other_gate, other_cand = core_swap(gate_weight), core_swap(cand_weight)
    weights = (gate_weight, other_gate, cand_weight, other_cand)
    own = jnp.concatenate([width * shares, gate_bias.reshape(-1, width), cand_bias])
    other = core_swap(own)
    low_part, high_part = jnp.where(first_core, own, other), jnp.where(first_core, other, own)
    half = gate_weight.shape[0]
    count = 2 * half
    scales = jnp.concatenate([low_part[:half], high_part[:half]])
    gate_b = jnp.concatenate([low_part[half : 3 * half], high_part[half : 3 * half]]).reshape(count, 2 * width)
    cand_b = jnp.concatenate([low_part[3 * half :], high_part[3 * half :]])

    moments1 = dp_moments(local1, ROWS_MB)
    affine1, affine2 = [jnp.stack([bn_gain[i], bn_bias[i]]) for i in range(2)]
    h1, local2 = layer1_forward(source1, moments1, affine1, scales, gate_b, cand_b, weights, False)
    source2 = to_layer(h1, True)
    moments2 = dp_moments(local2, ROWS_MB)
    moments2, source1 = lax.optimization_barrier((moments2, source1))
    kept_h, kept_z, kept_r, kept_c, operands = layer1_forward(
        source1, moments1, affine1, scales, gate_b, cand_b, weights, True)
    h2, gx2, nsums2, sums2, operands, grads_high, grads_low = layer2_both(
        source2, to_layer(moments2, True), affine2, scales, gate_b, cand_b, weights, out_grad, operands)
    received = to_layer(gx2, False)

    def layer_columns(value):
        share = value.shape[1] // 4
        pieces = value.reshape(rows, 2, 2, share)
        kept = jnp.where(first_core, pieces[:, :, 0], pieces[:, :, 1])
        got = core_swap(jnp.where(first_core, pieces[:, :, 1], pieces[:, :, 0]))
        both = jnp.where(first_core, jnp.stack([kept, got]), jnp.stack([got, kept]))
        return both.reshape(2 * rows, 2, share)

    totals2 = to_layer(dp_total(nsums2), False) / counted

    def pick(a, b):
        return jnp.where(top, a, b)

    kept_states = (kept_h, kept_z, kept_r, kept_c)
    g, gx1, sums1h, sent, grads_high = layer1_backward(
        1, (received, h1, moments2, totals2, bn_gain[1:2]), source1, moments1, affine1, scales, weights,
        kept_states, operands, grads_high)
    upper = Ring((kept_terms(1, operands, grads_high), core_swap(sent)))
    places = upper.places
    pipes = lax.axis_size("pipe")

    def lower_section(g, gx1):
        return layer1_backward(
            0, (g, gx1), source1, moments1, affine1, scales, weights, kept_states, operands, grads_low)

    gx1, nsums1, sums1l, sent, grads_low = upper.step(work=(lower_section, (g, gx1)))

    swapped = core_swap(sent)
    levels_of_dp = [1 << i for i in range(places.bit_length() - 1)]

    def over_layers(value):
        return lax.ppermute(value, "pipe", [(i, (i + pipes // 2) % pipes) for i in range(pipes)])

    def small_sums(sums1h, sums1l, sums2, nsums1, nsums2):
        small = pick(sums2, jnp.concatenate([sums1l, sums1h])).reshape(count, 4 * width)
        kept, sent_sums = halves(small, ~first_core)
        sums = [nsums.sum(axis=1) for nsums in (nsums1, nsums2)]
        sums = jnp.stack([jnp.where(top, 0.0, sums[0]), jnp.where(top, sums[1], 0.0)], axis=1).reshape(-1, 4 * width)
        return jnp.concatenate([kept, sums]) + core_swap(jnp.concatenate([sent_sums, sums]))

    def features(gx1, totals1):
        return feature_grads(gx1, source1, moments1, totals1, bn_gain[:1], category_columns, flat_table.shape)

    def table_halves(table):
        kept, sent = halves(table.astype(BF), ~first_core)
        return kept, core_swap(sent)

    got, kept = upper.step(sends=((functools.partial(dp_swap, step=1), nsums1),),
                           work=(functools.partial(kept_terms, 0), (operands, grads_low)))
    totals1 = nsums1 + got
    lower = Ring((kept, swapped))
    lower.held, upper.held = tied(lower.held, upper.held)
    small, = lower.step(work=(small_sums, (sums1h, sums1l, sums2, nsums1, nsums2)))
    for level in levels_of_dp[1:]:
        got, = upper.step(sends=((functools.partial(dp_swap, step=level), totals1),))
        totals1 = totals1 + got
    for level in levels_of_dp:
        got, = lower.step(sends=((functools.partial(dp_swap, step=level), small),))
        small = small + got
    numeric_back, table = upper.step(work=(features, (gx1, totals1 / counted)))
    table_kept, table_got = upper.step(work=(table_halves, (table,)))
    table = plus(table_kept, table_got)
    got, = lower.step(sends=((over_layers, small[half:]),))
    sums = (small[half:] + got).reshape(2, 2, width)
    block, = lower.step(work=(layer_columns, (h2,)))
    gate_w, cand_w = lower.step(work=(lambda: blank_outputs(half, width), ()))
    for level in levels_of_dp[: places - 1 - upper.done]:
        got, = upper.step(sends=((functools.partial(dp_swap, step=level), table),))
        table = plus(table, got)
        levels_left = levels_of_dp[levels_of_dp.index(level) + 1 :]
    while upper.done < places - 1:
        upper.step()
    while lower.done < places - 1:
        lower.step()

    pad = ((0, 0), (0, upper.held.shape[1] - lower.held.shape[1]))
    total_upper, total_lower = upper.held, jnp.pad(lower.held, pad)
    own = Ring(held=jnp.where(first_core, total_lower, total_upper))
    other = Ring(held=core_swap(jnp.where(first_core, total_upper, total_lower)))

    def table_side(s):
        if s < len(levels_left):
            return dict(sends=((functools.partial(dp_swap, step=levels_left[s]), table),))
        if s == len(levels_left):
            return dict(work=(core_swap, (table,)))
        if s == len(levels_left) + 1:
            return dict(sends=((functools.partial(to_layer, up=True), table),))
        return {}

    mine, others = [], []
    placed = 0
    for s in range(places):
        mine.append(own.held)
        others.append(other.held)
        if s == places - 1:
            break
        got = own.step(**table_side(s))
        if s < len(levels_left):
            table = plus(table, got[0])
        elif s == len(levels_left):
            table = joined(table, got[0], ~first_core)
        elif got:
            table_got = got[0]
        if s == 0:
            got_block, = other.step(sends=((functools.partial(to_layer, up=False), block[:, 0]),))
        elif s == 1:
            numeric_part, = other.step(work=(layer_columns, (numeric_back,)))
        elif s == 2:
            got_numeric, = other.step(sends=((functools.partial(to_layer, up=True), numeric_part[:, 1]),))
        elif s % 3 == 0:
            steps = range(placed, s)
            n = len(steps)

            def place(gate_w, cand_w, *flat):
                return place_blocks(steps, places, flat[:n], flat[n:], gate_w, cand_w)

            gate_w, cand_w = other.step(work=(place, (gate_w, cand_w, *mine[placed:s], *others[placed:s])))
            placed = s
        else:
            other.step()
    gate_w, cand_w = place_blocks(range(placed, places), places, mine[placed:], others[placed:], gate_w, cand_w)

    small = small[:half].reshape(half, 4, width)
    gate_b = small[:, :2].reshape(half, 2 * width)
    cand_b = small[:, 2]
    scaled = width * small[:, 3]
    logit = shares * (scaled - jnp.sum(shares * scaled, axis=-1, keepdims=True))
    table = pick(table_got, table).astype(F32)
    table = jnp.swapaxes(table.reshape(columns, embed_width, levels), 1, 2)
    block_out = pick(block[:, 1], got_block)
    numeric_grad = pick(got_numeric, numeric_part[:, 0])
    return (block_out, numeric_grad, table, sums[1], sums[0], logit,
            gate_w, gate_b, cand_w, cand_b)


def solution(mesh):
    in_specs = (P("dp", None), P("dp", None), P(), P(), P(), P(), P("pipe", None), P("pipe", None),
                P("pipe", None, None), P("pipe", None), P("pipe", None, None), P("pipe", None),
                P("dp", None))
    out_specs = (P("dp", "pipe"), P("dp", "pipe"), P(), P(), P(), P("pipe", None),
                 P("pipe", None, None), P("pipe", None), P("pipe", None, None), P("pipe", None))
    return jax.shard_map(on_device, mesh=mesh, in_specs=in_specs, out_specs=out_specs, check_vma=False)
```

```python
import functools

import jax
import jax.numpy as jnp
from jax import lax
from jax.experimental import pallas as pl
from jax.experimental.pallas import tpu as pltpu
from jax.sharding import PartitionSpec as P

MB = 8
ROWS_MB = 128
BLOCK = 512
EPS = 1e-05
BF = jnp.bfloat16
F32 = jnp.float32


def feature_share(logits, allow):
    allowed = allow > 0
    largest = jnp.max(jnp.where(allowed, logits, -1e30), axis=-1, keepdims=True)
    raised = jnp.where(allowed, jnp.exp(jnp.where(allowed, logits - largest, 0.0)), 0.0)
    return raised / jnp.sum(raised, axis=-1, keepdims=True)


def core_swap(value):
    return lax.ppermute(value, "pipe", [(i, i ^ 1) for i in range(lax.axis_size("pipe"))])


def to_layer(value, up):
    half = lax.axis_size("pipe") // 2
    pairs = [(i, i + half) if up else (i + half, i) for i in range(half)]
    return lax.ppermute(value, "pipe", pairs)


def dp_swap(value, step):
    return lax.ppermute(value, "dp", [(i, i ^ step) for i in range(lax.axis_size("dp"))])


def merged(a, b, held):
    gap = a[0] - b[0]
    return 0.5 * (a[0] + b[0]), a[1] + b[1] + gap * gap * (0.5 * held)


def dp_levels():
    return [1 << i for i in range(lax.axis_size("dp").bit_length() - 1)]


def dp_moments(both, count):
    held = count
    for step in dp_levels()[1:]:
        both = jnp.stack(merged(both, dp_swap(both, step), held))
        held *= 2
    return both


def last_pair(both):
    return both, dp_swap(both, dp_levels()[0])


def last_pair_to_layer(both, up):
    lanes = lax.axis_size("pipe")
    half = lanes // 2
    pairs = []
    for place in range(lax.axis_size("dp")):
        for lane in range(half):
            low, high = lane, lane + half
            start, end = (low, high) if up else (high, low)
            pairs.append((place * lanes + start, (place ^ dp_levels()[0]) * lanes + end))
    return to_layer(both, up), lax.ppermute(both, ("dp", "pipe"), pairs)


def partial_total(value):
    for step in dp_levels()[1:]:
        value = value + dp_swap(value, step)
    return value


def dp_total(value):
    step = 1
    while step < lax.axis_size("dp"):
        value = value + dp_swap(value, step)
        step *= 2
    return value


def plus(a, b):
    return lax.reduce_precision(a.astype(F32) + b.astype(F32), 8, 7).astype(BF)


def halves(value, second):
    mid = value.shape[0] // 2
    a, b = value[:mid], value[mid:]
    return jnp.where(second, b, a), jnp.where(second, a, b)


def joined(kept, got, second):
    return jnp.where(second, jnp.concatenate([got, kept]), jnp.concatenate([kept, got]))


def rounded(value):
    return lax.reduce_precision(value, 8, 7)


def dot(a, b, dims):
    return lax.dot_general(a, b, ((dims[0], dims[1]), ((), ())), preferred_element_type=F32)


def sigmoid(v):
    return 0.5 * jnp.tanh(0.5 * v) + 0.5


def low(v):
    return v.astype(BF).astype(F32)


def nn(a, b):
    return lax.dot_general(a, b, (((1,), (0,)), ((), ())), preferred_element_type=F32)


def nt(a, b):
    return lax.dot_general(a, b, (((1,), (1,)), ((), ())), preferred_element_type=F32)


def column_sum(v):
    return jnp.sum(v, axis=0, keepdims=True)


def batch_rows(i):
    return slice(i * ROWS_MB, (i + 1) * ROWS_MB)


def when_active(layer):
    rank = lax.axis_index("pipe")
    return rank // (lax.axis_size("pipe") // 2) == layer


class Weights:
    def __init__(self, refs, scratch):
        self.own_gate, self.other_gate, self.own_cand, self.other_cand = refs
        self.gate, self.cand, self.sems = scratch
        self.slots = self.gate.shape[0]

    def start(self, k):
        core = lax.axis_index("pipe") % 2
        per_core = self.own_gate.shape[0]
        i, slot = k % per_core, k % self.slots

        def begin(gate, cand):
            pltpu.make_async_copy(gate.at[i], self.gate.at[slot], self.sems.at[0, slot]).start()
            pltpu.make_async_copy(cand.at[i], self.cand.at[slot], self.sems.at[1, slot]).start()

        pl.when(core == k // per_core)(functools.partial(begin, self.own_gate, self.own_cand))
        pl.when(core != k // per_core)(functools.partial(begin, self.other_gate, self.other_cand))

    def wait(self, k):
        slot = k % self.slots
        pltpu.make_async_copy(self.own_gate.at[0], self.gate.at[slot], self.sems.at[0, slot]).wait()
        pltpu.make_async_copy(self.own_cand.at[0], self.cand.at[slot], self.sems.at[1, slot]).wait()


def finish_moments(a, b, moments, held):
    mean, spread = merged(a[...], b[...], held)
    moments[0] = mean
    moments[1] = lax.rsqrt(spread / (2 * held) + EPS)


def normalise(source, moments, affine, x):
    for i in range(source.shape[0] // ROWS_MB):
        at = batch_rows(i)
        xhat = (source[at, :].astype(F32) - moments[0, i : i + 1, :]) * moments[1, i : i + 1, :]
        x[at, :] = xhat * affine[0:1, :] + affine[1:2, :]


def run_forward(x, scales, gate_bias, cand_bias, weights, h, keep=None, after=None):
    rows, width = x.shape
    count = scales.shape[0]
    section = count // 2
    blocks = [slice(i, i + BLOCK) for i in range(0, rows, BLOCK)]

    def spot(k):
        return k if keep else k % 2

    weights.wait(0)
    for at in blocks:
        m = (x[at, :] * scales[0:1, :]).astype(BF)
        zz = sigmoid(nn(m, weights.gate[0, width:, :width]) + gate_bias[0:1, :width])
        cc = jnp.tanh(nn(m, weights.cand[0, width:, :]) + cand_bias[0:1, :])
        h[1, at, :] = zz * cc
        if keep:
            z, r, c, operands = keep
            z[0, at, :], c[0, at, :] = zz, cc
            if operands is not None:
                operands[0, at, width : 2 * width] = m
    if keep:
        after(0)

    def segment(k, _):
        weights.wait(k)
        if keep:
            after.before(k)

        @pl.when(k == section)
        def _():
            x[...] = low(x[...])
            h[spot(k)] = low(h[spot(k)])

        for at in blocks:
            hh = h[spot(k), at, :]
            hb = hh.astype(BF)
            m = (x[at, :] * scales[pl.ds(k, 1), :]).astype(BF)
            both = jnp.concatenate([hb, m], 1)
            bias = gate_bias[pl.ds(k, 1), :]
            rr = sigmoid(nn(both, weights.gate[k, :, width:]) + bias[:, width:])
            zz = sigmoid(nn(both, weights.gate[k, :, :width]) + bias[:, :width])
            rh = (rr * hh).astype(BF)
            cc = jnp.tanh(nn(jnp.concatenate([rh, m], 1), weights.cand[k]) + cand_bias[pl.ds(k, 1), :])
            if keep:
                z[k, at, :], r[k, at, :], c[k, at, :] = zz, rr, cc
                if operands is not None:
                    slot = k % 2
                    operands[slot, at, :width] = hb
                    operands[slot, at, width : 2 * width] = m
                    operands[slot, at, 2 * width :] = rh
            h[spot(k + 1), at, :] = (1.0 - zz) * hh + zz * cc
        if keep:
            after(k)
        return 0

    lax.fori_loop(1, count, segment, 0)


class Out:
    def __init__(self, slotted, sems, kept=(), kept_sems=None):
        self.slotted, self.sems, self.kept, self.kept_sems = slotted, sems, kept, kept_sems

    def slot_copy(self, k):
        source, target = self.slotted
        return pltpu.make_async_copy(source.at[k % 2], target.at[k], self.sems.at[k % 2])

    def kept_copies(self, k):
        return [
            pltpu.make_async_copy(source.at[k], target.at[k], self.kept_sems.at[i, k])
            for i, (source, target) in enumerate(self.kept)
        ]

    def before(self, k):
        if not self.slotted:
            return

        @pl.when(k >= 2)
        def _():
            self.slot_copy(k - 2).wait()

    def __call__(self, k):
        if self.slotted:
            self.slot_copy(k).start()
        for copy in self.kept_copies(k):
            copy.start()

    def finish(self, count):
        if self.slotted:
            self.slot_copy(count - 2).wait()
            self.slot_copy(count - 1).wait()
        if self.kept:
            def wait(k, _):
                for copy in self.kept_copies(k):
                    copy.wait()
                return 0
            lax.fori_loop(0, count, wait, 0)


def run_backward(segments, g, gx, x, scales, weights, states, slots, grads, sums, arrive, done):
    h, z, r, c = states
    rows, width = g.shape
    blocks = [slice(i, i + BLOCK) for i in range(0, rows, BLOCK)]
    high = max(segments)

    def segment(i, _):
        k = high - i
        s = k % slots
        arrive(k)
        totals = None
        for at in blocks:
            gg, hh, zz, rr, cc = g[at, :], h[s, at, :], z[s, at, :], r[s, at, :], c[s, at, :]
            gc = (gg * zz * (1.0 - cc * cc)).astype(BF)
            reset_h = nt(gc, weights.cand[k % weights.slots, :width, :])
            gate_z = (gg * (cc - hh) * zz * (1.0 - zz)).astype(BF)
            gm = nt(gc, weights.cand[k % weights.slots, width:, :])
            gate_r = (reset_h * hh * rr * (1.0 - rr)).astype(BF)
            gates = jnp.concatenate([gate_z, gate_r], 1)
            g[at, :] = gg * (1.0 - zz) + reset_h * rr + nt(gates, weights.gate[k % weights.slots, :width, :])
            gm = gm + nt(gates, weights.gate[k % weights.slots, width:, :])
            gx[at, :] = gx[at, :] + gm * scales[pl.ds(k, 1), :]
            grads[k % 2, at, : 2 * width] = gates
            grads[k % 2, at, 2 * width :] = gc
            part = jnp.concatenate([column_sum(gates.astype(F32)), column_sum(gc.astype(F32)),
                                    column_sum(gm * x[at, :])], 1)
            totals = part if totals is None else totals + part
            done.stage(k, at, lambda: ((x[at, :] * scales[pl.ds(k, 1), :]).astype(BF), hh.astype(BF),
                                       (rr * hh).astype(BF)))
        sums[pl.ds(k, 1), :] = totals
        done(k)
        return 0

    full = [k for k in segments if k > 0]
    lax.fori_loop(0, len(full), segment, 0)
    if min(segments) == 0:
        arrive(0)
        totals = None
        for at in blocks:
            gg, zz, cc = g[at, :], z[0, at, :], c[0, at, :]
            gc = (gg * zz * (1.0 - cc * cc)).astype(BF)
            gate_z = (gg * cc * zz * (1.0 - zz)).astype(BF)
            gm = nt(gc, weights.cand[0, width:, :]) + nt(gate_z, weights.gate[0, width:, :width])
            gx[at, :] = gx[at, :] + gm * scales[0:1, :]
            grads[0, at, :width] = gate_z
            grads[0, at, width : 2 * width] = gc
            part = jnp.concatenate([column_sum(gate_z.astype(F32)), jnp.zeros((1, width), F32),
                                    column_sum(gc.astype(F32)), column_sum(gm * x[at, :])], 1)
            totals = part if totals is None else totals + part
            done.stage(0, at, lambda: ((x[at, :] * scales[0:1, :]).astype(BF),))
        sums[0:1, :] = totals
        done.first()


def tn(a, b):
    return lax.dot_general(a, b, (((0,), (0,)), ((), ())), preferred_element_type=F32)


class Terms:
    def __init__(self, count, a, b, grads, made, sems, arrays, after=None):
        self.first_core = lax.axis_index("pipe") % 2 == 0
        self.count, self.a, self.b, self.grads, self.made, self.sems = count, a, b, grads, made, sems
        self.arrays, self.after = arrays, after
        self.width = a.shape[-1]

    def slot(self, k):
        return (self.count - 1 - k) % 2

    def copies(self, k):
        w, part, slot = self.width, self.arrays[0][0].shape[1], self.slot(k)
        start, size = (self.count - 1 - k) * 3 * w, w if k == 0 else 3 * w
        cuts = [(0, start, size)]
        if start < part < start + size:
            cuts = [(0, start, part - start), (part - start, part, start + size - part)]
        return [pltpu.make_async_copy(self.made.at[slot, i, :, pl.ds(at, n)],
                                      self.arrays[i][to // part].at[:, pl.ds(to % part, n)], self.sems.at[slot, i, j])
                for i in range(2) for j, (at, to, n) in enumerate(cuts)]

    def each(self, k, function):
        if isinstance(k, int):
            function(k)
            return
        for known in range(1, self.count):
            pl.when(k == known)(functools.partial(function, known))

    def start(self, k):
        for copy in self.copies(k):
            copy.start()

    def wait(self, k):
        if k < self.count:
            for copy in self.copies(k):
                copy.wait()

    def stage(self, k, at, operands):
        m, *others = operands()
        if not others:
            self.a[0, at, :] = m
            return
        for i, upper in enumerate((~self.first_core, self.first_core)):
            self.a[i, at, :] = jnp.where(upper, others[0], m)
            self.b[i, at, :] = jnp.where(upper, others[1], m)

    def __call__(self, k, source=0, a=None, b=None, grads=None):
        w = self.width
        a, b = (self.a, self.b) if a is None else (a, b)
        grads = self.grads.at[k % 2] if grads is None else grads
        self.each(k, lambda k: self.wait(k + 2))
        for i in range(2):
            self.made[self.slot(k), i, :, : 2 * w] = tn(a[i], grads[:, : 2 * w]).astype(BF)
            self.made[self.slot(k), i, :, 2 * w :] = tn(b[i], grads[:, 2 * w :]).astype(BF)
        self.each(k, self.start)
        if self.after:
            self.after(k)

    def first(self, a=None, grads=None):
        w = self.width
        a = self.a if a is None else a
        grads = self.grads.at[0] if grads is None else grads
        self.wait(2)
        for i, upper in enumerate((~self.first_core, self.first_core)):
            at = pl.multiple_of(jnp.where(upper, 0, w), w)
            self.made[self.slot(0), i, :, :w] = tn(a[0], grads[:, pl.ds(at, w)]).astype(BF)
        self.start(0)
        self.wait(1)
        self.wait(0)


def terms_from_hbm(terms, operands, grads, buffers, sems):
    a, b, g = buffers
    count = terms.count
    width = terms.width

    def copies(k):
        slot = k % 2
        pieces = []
        if k == 0:
            pieces = [(operands.at[0, :, pl.ds(width, width)], a.at[2 * slot])]
        else:
            for j, upper in enumerate((~terms.first_core, terms.first_core)):
                at_a = pl.multiple_of(jnp.where(upper, 0, width), width)
                at_b = pl.multiple_of(jnp.where(upper, 2 * width, width), width)
                pieces += [(operands.at[k, :, pl.ds(at_a, width)], a.at[2 * slot + j]),
                           (operands.at[k, :, pl.ds(at_b, width)], b.at[2 * slot + j])]
        pieces.append((grads.at[k], g.at[slot]))
        return [pltpu.make_async_copy(x, y, sems.at[slot, j]) for j, (x, y) in enumerate(pieces)]

    for copy in copies(count - 1):
        copy.start()
    for k in range(count - 1, -1, -1):
        slot = k % 2
        if k:
            for copy in copies(k - 1):
                copy.start()
        for copy in copies(k):
            copy.wait()
        if k:
            terms(k, a=a.at[pl.ds(2 * slot, 2)], b=b.at[pl.ds(2 * slot, 2)], grads=g.at[slot])
        else:
            terms.first(a=a.at[pl.ds(2 * slot, 2)], grads=g.at[slot])


def norm_sums(gx, xhat_of, sums):
    for i in range(gx.shape[0] // ROWS_MB):
        part = gx[batch_rows(i), :]
        sums[0, i : i + 1, :] = column_sum(part)
        sums[1, i : i + 1, :] = column_sum(part * xhat_of(i))


def xhat_rows(source, moments, i):
    return (source[batch_rows(i), :].astype(F32) - moments[0, i : i + 1, :]) * moments[1, i : i + 1, :]


ANY = pl.BlockSpec(memory_space=pl.ANY)
VM = pl.BlockSpec(memory_space=pltpu.VMEM)
LIMIT = 62 * 1024 * 1024


def layer_cost(segments, rows, width, passes):
    return pl.CostEstimate(flops=segments * passes * rows * 12 * width * width, transcendentals=0,
                           bytes_accessed=segments * (12 * width * width + 16 * rows * width))


def layer1_forward(source, moments, affine, scales, gate_bias, cand_bias, weights, keep):
    rows, width = source.shape
    count = scales.shape[0]

    dp_half = ROWS_MB * lax.axis_size("dp") // 2

    def kernel(*refs):
        if keep:
            source, moments = refs[:2]
            refs = refs[2:]
        else:
            source, first_half, second_half = refs[:3]
            refs = refs[3:]
        affine, scales, gate_bias, cand_bias, w0, w1, w2, w3 = refs[:8]
        refs = refs[8:]
        if keep:
            kept_h, kept_z, kept_r, kept_c = refs[:4]
            x, gate, cand, wsems, h, z, r, c, ksems = refs[4:]
        else:
            last, local, moments = refs[:3]
            x, gate, cand, wsems, h = refs[3:]

        @pl.when(when_active(0))
        def _():
            held = Weights((w0, w1, w2, w3), (gate, cand, wsems))
            for k in range(count):
                held.start(k)
            if not keep:
                finish_moments(first_half, second_half, moments, dp_half)
            normalise(source, moments, affine.at[0], x)
            if keep:
                out = Out(None, None, ((h, kept_h), (z, kept_z), (r, kept_r), (c, kept_c)), ksems)
                run_forward(x, scales, gate_bias, cand_bias, held, h, (z, r, c, None), out)
                out.finish(count)
                return
            run_forward(x, scales, gate_bias, cand_bias, held, h)
            final = h.at[count % 2]
            last[...] = final[...].astype(BF)
            for i in range(rows // ROWS_MB):
                part = low(final[batch_rows(i), :])
                mean = column_sum(part) * (1.0 / ROWS_MB)
                local[0, i : i + 1, :] = mean
                local[1, i : i + 1, :] = column_sum((part - mean) * (part - mean))

    state = jax.ShapeDtypeStruct((count, rows, width), F32)
    by_batch = jax.ShapeDtypeStruct((2, rows // ROWS_MB, width), F32)
    scratch = [pltpu.VMEM((rows, width), F32),
               pltpu.VMEM((count, 2 * width, 2 * width), BF),
               pltpu.VMEM((count, 2 * width, width), BF),
               pltpu.SemaphoreType.DMA((2, count))]
    if keep:
        out_shape = (state,) * 4
        out_specs = (ANY,) * 4
        scratch += [pltpu.VMEM((count + 1, rows, width), F32)] + [pltpu.VMEM((count, rows, width), F32)] * 3
        scratch += [pltpu.SemaphoreType.DMA((4, count))]
    else:
        out_shape = (jax.ShapeDtypeStruct((rows, width), BF), by_batch, by_batch)
        out_specs = (VM, VM, VM)
        scratch += [pltpu.VMEM((2, rows, width), F32)]
    args = (source,) + (moments if isinstance(moments, tuple) else (moments,))
    args += (affine, scales, gate_bias, cand_bias)
    return pl.pallas_call(
        kernel,
        out_shape=out_shape,
        in_specs=[VM] * len(args) + [ANY] * 4,
        out_specs=out_specs,
        scratch_shapes=scratch,
        compiler_params=pltpu.CompilerParams(vmem_limit_bytes=LIMIT),
        cost_estimate=layer_cost(count, rows, width, 1),
        name="layer1_states" if keep else "layer1_forward",
    )(*args, *weights)


def layer2_both(source, halves_of_moments, affine, scales, gate_bias, cand_bias, weights, cotangent):
    rows, width = source.shape
    count = scales.shape[0]

    dp_half = ROWS_MB * lax.axis_size("dp") // 2

    def kernel(source, first_half, second_half, affine, scales, gate_bias, cand_bias, w0, w1, w2, w3, cotangent,
               last, gx_out, nsums, sums, operands_out, grads_out,
               x, gate, cand, wsems, h, z, r, c, operands, osems, g, gx, gsem, moments):
        @pl.when(when_active(1))
        def _():
            held = Weights((w0, w1, w2, w3), (gate, cand, wsems))
            for k in range(count):
                held.start(k)
            core = lax.axis_index("pipe") % 2
            first = pl.multiple_of(core * rows, rows)
            load_g = pltpu.make_async_copy(cotangent.at[pl.ds(first, rows), :], g, gsem.at[0])
            load_g.start()
            finish_moments(first_half, second_half, moments, dp_half)
            normalise(source, moments, affine.at[1], x)
            out = Out((operands, operands_out), osems)
            run_forward(x, scales, gate_bias, cand_bias, held, h, (z, r, c, operands), out)
            last[...] = h[count]
            out.finish(count)
            load_g.wait()
            gx[...] = jnp.zeros_like(gx)

            section = count // 2

            class Left:
                def stage(self, k, at, operands):
                    pass

                def copy(self, k):
                    return pltpu.make_async_copy(operands.at[k % 2], grads_out.at[k], osems.at[k % 2])

                def __call__(self, k):
                    self.copy(k).start()

                def first(self):
                    self.copy(0).start()
                    self.copy(1).wait()
                    self.copy(0).wait()

            left = Left()

            def free(k):
                @pl.when(k <= count - 3)
                def _():
                    left.copy(k + 2).wait()

            run_backward(range(section, count), g, gx, x, scales, held, (h, z, r, c), count, operands, sums, free, left)
            g[...] = low(g[...])
            gx[...] = low(gx[...])
            normalise(source, moments, affine.at[1], x)
            run_backward(range(section), g, gx, x, scales, held, (h, z, r, c), count, operands, sums, free, left)
            gx_out[...] = gx[...].astype(BF)
            norm_sums(gx, lambda i: xhat_rows(source, moments, i), nsums)

    state = pltpu.VMEM((count, rows, width), F32)
    left_out = jax.ShapeDtypeStruct((count, rows, 3 * width), BF)
    return pl.pallas_call(
        kernel,
        out_shape=(jax.ShapeDtypeStruct((rows, width), F32),
                   jax.ShapeDtypeStruct((rows, width), BF),
                   jax.ShapeDtypeStruct((2, rows // ROWS_MB, width), F32),
                   jax.ShapeDtypeStruct((count, 4 * width), F32),
                   left_out, left_out),
        in_specs=[VM] * 7 + [ANY] * 5,
        out_specs=(VM, VM, VM, VM, ANY, ANY),
        scratch_shapes=[pltpu.VMEM((rows, width), F32),
                        pltpu.VMEM((count, 2 * width, 2 * width), BF),
                        pltpu.VMEM((count, 2 * width, width), BF),
                        pltpu.SemaphoreType.DMA((2, count)),
                        pltpu.VMEM((count + 1, rows, width), F32), state, state, state,
                        pltpu.VMEM((2, rows, 3 * width), BF),
                        pltpu.SemaphoreType.DMA((2,)),
                        pltpu.VMEM((rows, width), F32),
                        pltpu.VMEM((rows, width), F32),
                        pltpu.SemaphoreType.DMA((1,)),
                        pltpu.VMEM((2, rows // ROWS_MB, width), F32)],
        compiler_params=pltpu.CompilerParams(vmem_limit_bytes=LIMIT),
        cost_estimate=layer_cost(count, rows, width, 2),
        name="layer2_both",
    )(source, *halves_of_moments, affine, scales, gate_bias, cand_bias, *weights, cotangent)


def layer1_backward(carried, source, moments, affine, scales, weights, kept, operands, grads):
    rows, width = source.shape
    count = scales.shape[0]
    section = count // 2
    slots = 3
    counted = ROWS_MB * lax.axis_size("dp")
    part = (3 * count - 2) * width // 2

    def kernel(gxr, hb, moments2, total_a, total_b, source, moments, affine, scales, w0, w1, w2, w3,
               kept_h, kept_z, kept_r, kept_c, operands_in, grads_in,
               gx, nsums, sums, sent_a, sent_b, mine_a, mine_b,
               x, gate, cand, wsems, h, z, r, c, ksems, g, loaded, a, b, lsems, made, msems):
        held = Weights((w0, w1, w2, w3), (gate, cand, wsems))
        states = ((kept_h, h), (kept_z, z), (kept_r, r), (kept_c, c))

        def copies(k):
            return [pltpu.make_async_copy(x.at[k], y.at[k % slots], ksems.at[i, k % slots])
                    for i, (x, y) in enumerate(states)]

        def arrive(k):
            held.wait(k)
            for copy in copies(k):
                copy.wait()

        def load(k):
            for copy in copies(k):
                copy.start()
            held.start(k)

        def after(k):
            @pl.when(k >= slots)
            def _():
                load(k - slots)

        terms = Terms(count, a, b, loaded, made, msems, ((sent_a, sent_b), (mine_a, mine_b)), after)

        @pl.when(when_active(1))
        def _():
            terms.after = None
            terms_from_hbm(terms, operands_in, grads_in, (a, b, loaded), lsems)

        @pl.when(when_active(0))
        def _():
            terms.after = after
            for k in range(count - 1, count - 1 - slots, -1):
                load(k)
            normalise(source, moments, affine.at[0], x)
            x[...] = low(x[...])
            for i in range(rows // ROWS_MB):
                at = batch_rows(i)
                mean_g, mean_gx = [(total_a[j, i : i + 1, :] + total_b[j, i : i + 1, :]) / counted for j in (0, 1)]
                back = gxr[at, :].astype(F32) - mean_g - xhat_rows(hb, moments2, i) * mean_gx
                g[at, :] = low(affine[1, 0:1, :] * moments2[1, i : i + 1, :] * back)
            gx[...] = jnp.zeros_like(gx)
            run_backward(range(section, count), g, gx, x, scales, held, (h, z, r, c), slots, loaded, sums, arrive, terms)
            g[...] = low(g[...])
            gx[...] = low(gx[...])
            normalise(source, moments, affine.at[0], x)
            run_backward(range(section), g, gx, x, scales, held, (h, z, r, c), slots, loaded, sums, arrive, terms)
            norm_sums(gx, lambda i: xhat_rows(source, moments, i), nsums)

    state = pltpu.VMEM((slots, rows, width), F32)
    terms = jax.ShapeDtypeStruct((width, part), BF)
    args = [*carried, source, moments, affine, scales, *weights, *kept, operands, grads]
    return pl.pallas_call(
        kernel,
        out_shape=(jax.ShapeDtypeStruct((rows, width), F32),
                   jax.ShapeDtypeStruct((2, rows // ROWS_MB, width), F32),
                   jax.ShapeDtypeStruct((count, 4 * width), F32), terms, terms, terms, terms),
        in_specs=[VM] * 9 + [ANY] * 10,
        out_specs=(VM,) * 3 + (ANY,) * 4,
        scratch_shapes=[pltpu.VMEM((rows, width), F32),
                        pltpu.VMEM((slots, 2 * width, 2 * width), BF),
                        pltpu.VMEM((slots, 2 * width, width), BF),
                        pltpu.SemaphoreType.DMA((2, slots)),
                        state, state, state, state,
                        pltpu.SemaphoreType.DMA((4, slots)),
                        pltpu.VMEM((rows, width), F32),
                        pltpu.VMEM((2, rows, 3 * width), BF),
                        pltpu.VMEM((4, rows, width), BF), pltpu.VMEM((4, rows, width), BF),
                        pltpu.SemaphoreType.DMA((2, 5)),
                        pltpu.VMEM((2, 2, width, 3 * width), BF),
                        pltpu.SemaphoreType.DMA((2, 2, 2))],
        compiler_params=pltpu.CompilerParams(vmem_limit_bytes=LIMIT),
        cost_estimate=layer_cost(count, rows, width, 2),
        name="layer1_backward",
    )(*args)


def hot_rows(cats, c, levels):
    level = lax.broadcasted_iota(jnp.int32, (levels, cats.shape[1]), 0)
    return jnp.where(cats[c : c + 1, :] == level, 1.0, 0.0).astype(BF)


def load_columns(categories, cats, sem, rows):
    first = pl.multiple_of((lax.axis_index("pipe") % 2) * rows, rows)
    return pltpu.make_async_copy(categories.at[:, pl.ds(first, rows)], cats, sem)


def embed(numeric, categories, table, rows, own, other, affine):
    numeric_width, columns = numeric.shape[1], categories.shape[0]
    embedded, levels = table.shape
    each = embedded // columns
    packed = 128 // each
    width = numeric_width + embedded

    half = own[0].shape[0]

    def kernel(numeric, categories, table, *refs):
        own, other, (bn_gain, bn_bias) = refs[:4], refs[4:8], refs[8:10]
        source, local, scales, gate_bias, cand_bias, affine, cats, nums, sems = refs[10:]
        core = lax.axis_index("pipe") % 2

        def put(logits, allow, gates, cands, at):
            scales[at : at + half, :] = width * feature_share(logits[...], allow[...])
            gate_bias[at : at + half, :] = gates[...]
            cand_bias[at : at + half, :] = cands[...]

        for at, owner in ((0, 0), (half, 1)):
            pl.when(core == owner)(functools.partial(put, *own, at))
            pl.when(core != owner)(functools.partial(put, *other, at))
        for layer in range(2):
            affine[layer, 0:1, :] = bn_gain[layer : layer + 1, :]
            affine[layer, 1:2, :] = bn_bias[layer : layer + 1, :]
        first = pl.multiple_of((lax.axis_index("pipe") % 2) * rows, rows)
        load = load_columns(categories, cats, sems.at[0], rows)
        load_numeric = pltpu.make_async_copy(numeric.at[pl.ds(first, rows), :], nums, sems.at[1])
        load.start()
        load_numeric.start()
        load.wait()
        row = lax.broadcasted_iota(jnp.int32, (128, levels), 0) // each
        for group in range(columns // packed):
            part = table[group * 128 : (group + 1) * 128, :]
            weights = jnp.concatenate([jnp.where(row == i, part, jnp.zeros_like(part)) for i in range(packed)], 1)
            hot = jnp.concatenate([hot_rows(cats, group * packed + i, levels) for i in range(packed)], 0)
            start = numeric_width + group * 128
            source[:, start : start + 128] = nn(weights, hot).T
        load_numeric.wait()
        source[:, :numeric_width] = nums[...]
        for i in range(rows // ROWS_MB):
            part = source[batch_rows(i), :]
            mean = column_sum(part) * (1.0 / ROWS_MB)
            local[0, i : i + 1, :] = mean
            local[1, i : i + 1, :] = column_sum((part - mean) * (part - mean))

    return pl.pallas_call(
        kernel,
        out_shape=(jax.ShapeDtypeStruct((rows, width), F32),
                   jax.ShapeDtypeStruct((2, rows // ROWS_MB, width), F32),
                   jax.ShapeDtypeStruct((2 * half, width), F32),
                   jax.ShapeDtypeStruct((2 * half, 2 * width), F32),
                   jax.ShapeDtypeStruct((2 * half, width), F32),
                   jax.ShapeDtypeStruct((2, 2, width), F32)),
        in_specs=[ANY, ANY] + [VM] * 11,
        out_specs=(VM,) * 6,
        scratch_shapes=[pltpu.VMEM((columns, rows), jnp.int32), pltpu.VMEM((rows, numeric_width), F32),
                        pltpu.SemaphoreType.DMA((2,))],
        compiler_params=pltpu.CompilerParams(vmem_limit_bytes=LIMIT),
        cost_estimate=pl.CostEstimate(flops=8 * rows * width * levels, transcendentals=0, bytes_accessed=8 * rows * width),
        name="embed",
    )(numeric, categories, table, *own, *other, *affine)


def feature_grads(gx, source, moments, totals, gain, categories, table_shape):
    rows, width = gx.shape
    embedded, levels = table_shape
    columns = categories.shape[0]
    each = embedded // columns
    numeric_width = width - embedded
    half = columns // 2

    def kernel(gx, source, moments, totals, gain, categories, numeric, sent, mine, cats, back, table, sem):
        load = load_columns(categories, cats, sem.at[0], rows)
        load.start()
        for i in range(rows // ROWS_MB):
            at = batch_rows(i)
            part = gx[at, :] - totals[0, i : i + 1, :] - xhat_rows(source, moments, i) * totals[1, i : i + 1, :]
            back[at, :] = gain[...] * moments[1, i : i + 1, :] * part
        numeric[...] = back[:, :numeric_width]
        load.wait()
        table[...] = jnp.zeros_like(table)
        for group in range(embedded // 128):
            start = numeric_width + group * 128
            grads = back[:, start : start + 128].astype(BF)
            lane = lax.broadcasted_iota(jnp.int32, (levels, 128), 1) // each
            blocks = jnp.zeros((levels, 128), F32)
            for i in range(128 // each):
                c = group * (128 // each) + i
                blocks = jnp.where(lane == i, nn(hot_rows(cats, c, levels), grads), blocks)
            turned = blocks.T
            for i in range(128 // each):
                c = group * (128 // each) + i
                for e in range(each):
                    at = i * each + e
                    table[c // half, c % half : c % half + 1, e * levels : (e + 1) * levels] = turned[at : at + 1, :]
        core = lax.axis_index("pipe") % 2
        sent[...] = table[1 - core].astype(BF)
        mine[...] = table[core].astype(BF)

    part = jax.ShapeDtypeStruct((16, each * levels), BF)
    return pl.pallas_call(
        kernel,
        out_shape=(jax.ShapeDtypeStruct((rows, numeric_width), F32), part, part),
        in_specs=[VM] * 5 + [ANY],
        out_specs=(VM, VM, VM),
        scratch_shapes=[pltpu.VMEM((columns, rows), jnp.int32), pltpu.VMEM((rows, width), F32),
                        pltpu.VMEM((2, 16, each * levels), F32), pltpu.SemaphoreType.DMA((1,))],
        compiler_params=pltpu.CompilerParams(vmem_limit_bytes=LIMIT),
        cost_estimate=pl.CostEstimate(flops=8 * rows * width * levels, transcendentals=0, bytes_accessed=16 * rows * width),
        name="feature_grads",
    )(gx, source, moments, totals, gain, categories)


def spare_totals(pieces, rows, used, logits, allow):
    count = len(pieces)
    spare, columns = pieces[0].shape[0] - rows, pieces[0].shape[1]
    half, width = logits.shape

    def kernel(logits, allow, *refs):
        pieces, (table, gate_b, cand_b, logit, gain, bias, parts, sems) = refs[:count], refs[count:]
        copies = [pltpu.make_async_copy(piece.at[pl.ds(rows, spare), :], parts.at[i], sems.at[i])
                  for i, piece in enumerate(pieces)]
        for copy in copies:
            copy.start()
        shares = feature_share(logits[...], allow[...])
        for copy in copies:
            copy.wait()
        spot = ring_place(count)
        added = jnp.zeros((spare, columns), F32)
        for place in range(count):
            added = added + parts[lax.rem(spot - place + count, count)].astype(F32)
        table[...] = added[:used, :]
        small = added[used:, : columns // 2] + added[used:, columns // 2 :]
        gate_b[...] = small[:half, : 2 * width]
        cand_b[...] = small[:half, 2 * width : 3 * width]
        scaled = width * small[:half, 3 * width :]
        logit[...] = shares * (scaled - jnp.sum(shares * scaled, axis=-1, keepdims=True))
        for layer in range(2):
            at = layer * width
            bias[layer : layer + 1, :] = small[half : half + 1, at : at + width]
            gain[layer : layer + 1, :] = small[half : half + 1, 2 * width + at : 3 * width + at]

    def out(*shape):
        return jax.ShapeDtypeStruct(shape, F32)

    return pl.pallas_call(
        kernel,
        out_shape=(out(used, columns), out(half, 2 * width), out(half, width), out(half, width), out(2, width),
                   out(2, width)),
        in_specs=[VM, VM] + [ANY] * count,
        out_specs=(VM,) * 6,
        scratch_shapes=[pltpu.VMEM((count, spare, columns), BF), pltpu.SemaphoreType.DMA((count,))],
        compiler_params=pltpu.CompilerParams(vmem_limit_bytes=LIMIT),
        name="spare_totals",
    )(logits, allow, *pieces)


def ring_place(places):
    place = lax.axis_index("dp")
    spot = jnp.where(place % 2 == 0, place // 2, places - 1 - place // 2)
    return jnp.where(lax.axis_index("pipe") % 2 == 0, spot, places - 1 - spot)


def blank_outputs(per_core, width):
    def kernel(gate, cand, zeros, sems):
        @pl.when(lax.axis_index("pipe") % 2 == 0)
        def _():
            zeros[...] = jnp.zeros_like(zeros)
            copies = [
                pltpu.make_async_copy(zeros, gate.at[0, pl.ds(0, width), :], sems.at[0]),
                pltpu.make_async_copy(zeros.at[:, pl.ds(0, width)],
                                      gate.at[0, pl.ds(width, width), pl.ds(width, width)], sems.at[1]),
                pltpu.make_async_copy(zeros.at[:, pl.ds(0, width)], cand.at[0, pl.ds(0, width), :], sems.at[2])]
            for copy in copies:
                copy.start()
            for copy in copies:
                copy.wait()

    return pl.pallas_call(
        kernel,
        out_shape=(jax.ShapeDtypeStruct((per_core, 2 * width, 2 * width), F32),
                   jax.ShapeDtypeStruct((per_core, 2 * width, width), F32)),
        out_specs=(ANY, ANY),
        scratch_shapes=[pltpu.VMEM((width, 2 * width), F32), pltpu.SemaphoreType.DMA((3,))],
        name="blank_outputs",
    )()


def place_block(step, blocks, mine, other, extra, gate, cand):
    rows, columns = other.shape
    per_core, width = gate.shape[0], cand.shape[2]
    given = () if extra is None else (extra,)

    def kernel(*refs):
        mine, other = refs[:2]
        extra = refs[2] if given else None
        gate, cand, onward, full, tail, sems = refs[4 + len(given) :]
        spot = ring_place(blocks)
        copies = []

        def copy(source, target, j, row, size):
            copies.append(pltpu.make_async_copy(
                source, target.at[j, pl.ds(row, rows), pl.ds(0, size)], sems.at[len(copies)]))
            copies[-1].start()

        def at(block):
            return pl.multiple_of(block * rows, rows)

        def put(own_half, first_layer):
            del copies[:]
            own_block = lax.rem(spot + 1 - step + blocks, blocks)
            other_block = lax.rem(2 * blocks - spot + step, blocks)
            if not first_layer and given:
                put_extra(spot, step - 1, blocks, extra, tail, cand, copies, sems)
            for piece, half, block in ((mine, own_half, own_block), (other, 1 - own_half, other_block)):
                full[half] = piece[:rows, :].astype(F32)
                for j in range(per_core):
                    start = (per_core - 1 - j) * 3 * width + (width if first_layer else 0)
                    source = full.at[half]
                    if first_layer and j == 0:
                        copy(source.at[:, pl.ds(start, width)], cand if half else gate, 0, width + at(block), width)
                        continue
                    copy(source.at[:, pl.ds(start, 2 * width)], gate, j, half * width + at(block), 2 * width)
                    if j or first_layer:
                        copy(source.at[:, pl.ds(start + 2 * width, width)], cand, j, half * width + at(block), width)
            if first_layer:
                onward[:rows, :] = mine[:rows, :width]
                onward[rows:, :] = other[:, :width]
            for item in copies:
                item.wait()

        core = lax.axis_index("pipe") % 2
        pl.when(core == 0)(functools.partial(put, 0, True))
        pl.when(core == 1)(functools.partial(put, 1, False))

    args = (mine, other, *given, gate, cand)
    return pl.pallas_call(
        kernel,
        out_shape=(jax.ShapeDtypeStruct(gate.shape, F32), jax.ShapeDtypeStruct(cand.shape, F32),
                   jax.ShapeDtypeStruct((2 * rows, width), BF)),
        in_specs=[VM] * (len(args) - 2) + [ANY] * 2,
        out_specs=(ANY, ANY, VM),
        input_output_aliases={len(args) - 2: 0, len(args) - 1: 1},
        scratch_shapes=[pltpu.VMEM((2, rows, columns), F32), pltpu.VMEM((2, rows, width), F32),
                        pltpu.SemaphoreType.DMA((4 * per_core,))],
        compiler_params=pltpu.CompilerParams(vmem_limit_bytes=LIMIT),
        name=f"place_block_{step}",
    )(*args)


def put_extra(spot, step, blocks, extra, tail, cand, copies, sems):
    rows, width = tail.shape[1:]
    for half, block in ((0, lax.rem(2 * blocks - spot - step, blocks)), (1, lax.rem(spot + 1 + step, blocks))):
        tail[half] = extra[half * rows : (half + 1) * rows, :].astype(F32)
        row = half * width + pl.multiple_of(block * rows, rows)
        copies.append(pltpu.make_async_copy(tail.at[half], cand.at[0, pl.ds(row, rows), :], sems.at[len(copies)]))
        copies[-1].start()


def place_extra(step, blocks, extra, cand):
    width = cand.shape[2]
    rows = extra.shape[0] // 2

    def kernel(extra, unused, cand, tail, sems):
        @pl.when(lax.axis_index("pipe") % 2 == 1)
        def _():
            copies = []
            put_extra(ring_place(blocks), step, blocks, extra, tail, cand, copies, sems)
            for item in copies:
                item.wait()

    return pl.pallas_call(
        kernel,
        out_shape=jax.ShapeDtypeStruct(cand.shape, F32),
        in_specs=[VM, ANY],
        out_specs=ANY,
        input_output_aliases={1: 0},
        scratch_shapes=[pltpu.VMEM((2, rows, width), F32), pltpu.SemaphoreType.DMA((2,))],
        compiler_params=pltpu.CompilerParams(vmem_limit_bytes=LIMIT),
        name="place_extra",
    )(extra, cand)


def tied(*values):
    return lax.optimization_barrier(values)


class Ring:
    def __init__(self, parts=None, held=None, unit=None, turn=None):
        self.turn = turn
        self.unit = unit
        self.places = lax.axis_size("dp")
        order = list(range(0, self.places, 2)) + list(range(1, self.places, 2))[::-1]
        lanes = lax.axis_size("pipe")
        self.pairs = []
        for lane in range(lanes):
            way = order if lane % 2 == 0 else order[::-1]
            self.pairs += [(way[i] * lanes + lane, way[(i + 1) % self.places] * lanes + lane)
                           for i in range(self.places)]
        self.spot = ring_place(self.places)
        self.parts = ()
        self.done = 0
        self.held = held
        if held is None:
            mine, received, first = parts
            self.rows = mine.shape[0] // self.places
            self.parts = (mine, received)
            self.held = (self.rows_of(mine, self.spot).astype(F32) + first.astype(F32)).astype(BF)

    def rows_of(self, part, number):
        at = lax.rem(number + self.places, self.places) * self.rows
        return lax.dynamic_slice_in_dim(part, at, self.rows, 0)

    def block(self, number):
        a, b = [self.rows_of(part, number) for part in self.parts]
        return a.astype(F32) + b.astype(F32)

    def step(self, sends=(), work=None, ends=None, wait=True):
        self.done += 1
        sent = len(sends)
        works = work if isinstance(work, list) else [work] if work else []
        held, *values = tied(self.held, *[value for _, value in sends], *[value for _, given in works for value in given])
        got = lax.ppermute(held, ("dp", "pipe"), self.pairs)
        given = [send(value) for (send, _), value in zip(sends, values)]
        outs, values = [], values[sent:]
        for function, arguments in works + ([ends] if ends else []):
            if function is not (ends or [None])[0]:
                arguments, values = values[: len(arguments)], values[len(arguments) :]
            result = function(*arguments)
            outs += list(result) if isinstance(result, (tuple, list)) else [result]
        if self.turn is not None:
            got, *_ = tied(got, *self.turn)
            self.turn[:] = [got]
        got, *outs = tied(got, *outs, *(given if wait else ()))
        if wait:
            given, outs = outs[len(outs) - sent :], outs[: len(outs) - sent]
        if self.unit is not None and self.done < self.places - 1:
            got = got * self.unit
        if self.parts:
            got = (self.block(self.spot - self.done) + got.astype(F32)).astype(BF)
        self.held = got
        return list(given) + outs


def on_device(numeric, categories, cardinalities, embed_table, bn_gain, bn_bias, mask_logits,
              feature_allow, gate_weight, gate_bias, cand_weight, cand_bias, out_grad):
    rank = lax.axis_index("pipe")
    core = rank % 2
    first_core = core == 0
    top = rank >= lax.axis_size("pipe") // 2
    width = out_grad.shape[1]
    numeric_width = numeric.shape[1]
    columns, levels, embed_width = embed_table.shape
    batches = MB // 2
    rows = batches * ROWS_MB
    counted = ROWS_MB * lax.axis_size("dp")

    def my_rows(array):
        return lax.dynamic_slice_in_dim(array, core * rows, rows, 0)

    def by_batch(array):
        return array.reshape(batches, ROWS_MB, array.shape[-1])

    half = gate_weight.shape[0]
    count = 2 * half
    flat_table = jnp.swapaxes(embed_table, 1, 2).reshape(columns * embed_width, levels)
    category_columns = categories.T
    own_small = (mask_logits, feature_allow, gate_bias, cand_bias)
    other_small = tuple(core_swap(value) for value in own_small)
    *other_small, own_gate, own_cand = tied(*other_small, gate_weight, cand_weight)
    weights = (gate_weight, core_swap(own_gate), cand_weight, core_swap(own_cand))
    source1, local1, scales, gate_b, cand_b, affine = embed(
        numeric, category_columns, flat_table, rows, own_small, other_small, (bn_gain, bn_bias))
    h1, local2, moments1 = layer1_forward(
        source1, last_pair(dp_moments(local1, ROWS_MB)), affine, scales, gate_b, cand_b, weights, False)
    source2 = to_layer(h1, True)
    local2 = dp_moments(local2, ROWS_MB)
    halves2 = last_pair_to_layer(local2, True)
    local2, source1 = lax.optimization_barrier((local2, source1))
    kept_states = layer1_forward(source1, moments1, affine, scales, gate_b, cand_b, weights, True)
    mean2, spread2 = merged(*last_pair(local2), counted // 2)
    moments2 = jnp.stack([mean2, lax.rsqrt(spread2 / counted + EPS)])
    h2, gx2, nsums2, sums2, operands, grads = layer2_both(
        source2, halves2, affine, scales, gate_b, cand_b, weights, out_grad)
    received = to_layer(gx2, False)
    totals2 = last_pair_to_layer(partial_total(nsums2), False)

    def layer_columns(value):
        share = value.shape[1] // 4
        pieces = value.reshape(rows, 2, 2, share)
        kept = jnp.where(first_core, pieces[:, :, 0], pieces[:, :, 1])
        got = core_swap(jnp.where(first_core, pieces[:, :, 1], pieces[:, :, 0]))
        both = jnp.where(first_core, jnp.stack([kept, got]), jnp.stack([got, kept]))
        return both.reshape(2 * rows, 2, share)

    def pick(a, b):
        return jnp.where(top, a, b)

    gx1, nsums1, sums1, sent_a, sent_b, mine_a, mine_b = layer1_backward(
        (received, h1, moments2, *totals2), source1, moments1, affine, scales, weights, kept_states, operands, grads)
    places = lax.axis_size("dp")

    def first_block(sent):
        rows = sent.shape[0] // places
        return core_swap(lax.dynamic_slice_in_dim(sent, (places - 1 - ring_place(places)) * rows, rows, 0))

    first_a, first_b = first_block(sent_a), first_block(sent_b)
    first_a, first_b, sent_a, sent_b = tied(first_a, first_b, sent_a, sent_b)
    upper = Ring((mine_a, core_swap(sent_a), first_a))
    lower = Ring((mine_b, core_swap(sent_b), first_b))
    pipes = lax.axis_size("pipe")

    levels_of_dp = [1 << i for i in range(places.bit_length() - 1)]

    def over_layers(value):
        return lax.ppermute(value, "pipe", [(i, (i + pipes // 2) % pipes) for i in range(pipes)])

    def small_sums(sums1, sums2, nsums1, nsums2):
        small = pick(sums2, sums1).reshape(count, 4 * width)
        kept, sent_sums = halves(small, ~first_core)
        sums = [nsums.sum(axis=1) for nsums in (nsums1, nsums2)]
        sums = jnp.stack([jnp.where(top, 0.0, sums[0]), jnp.where(top, sums[1], 0.0)], axis=1).reshape(-1, 4 * width)
        small = jnp.concatenate([kept, sums]) + core_swap(jnp.concatenate([sent_sums, sums]))
        return small

    def features(gx1, totals1):
        return feature_grads(gx1, source1, moments1, totals1, bn_gain[:1], category_columns, flat_table.shape)

    totals1 = nsums1
    used = columns // 2
    chain = [("sum", level) for level in levels_of_dp] + [("features",), ("cores",), ("layers",)]
    while lower.done < places - 1:
        act = chain.pop(0) if chain else ("",)
        if act[0] == "sum":
            got, *_ = upper.step(((functools.partial(dp_swap, step=act[1]), totals1),),
                                 ends=None if lower.done else (lambda held: held, (lower.held,)))
            totals1 = totals1 + got
        elif act[0] == "features":
            numeric_back, table_sent, table = upper.step(work=(features, (gx1, totals1 / counted)))
        elif act[0] == "cores":
            got, = upper.step(((core_swap, table_sent),))
            table = plus(table, got)
        elif act[0] == "layers":
            got, got_sums = upper.step(((functools.partial(to_layer, up=True), table), (over_layers, small[half:])))
            high = lax.reduce_precision(jnp.concatenate([small[:half], small[half:] + got_sums]), 8, 7)
            low_part = jnp.concatenate([small[:half], small[half:] + got_sums]) - high
            table = jnp.concatenate([pick(got, table)[:used], jnp.concatenate([high, low_part], 1).astype(BF)])
        else:
            upper.step()
        if lower.done == 1:
            small, = lower.step(work=(small_sums, (sums1, sums2, nsums1, nsums2)))
        elif lower.done == 5:
            block, = lower.step(work=(layer_columns, (h2,)))
        elif lower.done == 2:
            gate_w, cand_w = lower.step(work=(lambda: blank_outputs(half, width), ()))
        else:
            lower.step()

    block_rows = upper.held.shape[0]
    unit = (1.0 + 0.0 * cardinalities[0].astype(F32)).astype(BF)
    turn = []
    own = Ring(held=jnp.concatenate([jnp.where(first_core, lower.held, upper.held), table]), unit=unit, turn=turn)
    other = Ring(held=core_swap(jnp.where(first_core, upper.held, lower.held)), unit=unit, turn=turn)
    mine, extra = [], None
    for s in range(places):
        mine.append(own.held)
        place = functools.partial(place_block, s, places)
        if extra is None:
            place = lambda a, b, *rest: place_block(0, places, a, b, None, *rest)
        values = (own.held, other.held, *(() if extra is None else (extra,)), gate_w, cand_w)
        if s == places - 1:
            gate_w, cand_w, extra = place(*values)
            break
        if s == places - 2:
            gate_w, cand_w, extra = own.step(ends=(place, values))
            extra = core_swap(extra)
            other.step()
            continue
        own.step()
        sends, ends, works = (), None, [(place, values)]
        if s == 1:
            sends = ((functools.partial(to_layer, up=False), block[:, 0]),)
        elif s == 2:
            ends = (layer_columns, (numeric_back,))
        elif s == 3:
            sends = ((functools.partial(to_layer, up=True), numeric_part[:, 1]),)
        elif s == 5:
            works.append((lambda a, b, c, d: (pick(a, b), pick(c, d)),
                          (block[:, 1], got_block, got_numeric, numeric_part[:, 0])))
        outs = other.step(sends, works, ends, wait=False)
        if s == 1:
            got_block = outs.pop(0)
        elif s == 3:
            got_numeric = outs.pop(0)
        gate_w, cand_w, extra, *outs = outs
        extra = core_swap(extra)
        if s == 2:
            numeric_part, = outs
        elif s == 5:
            block_out, numeric_grad = outs
    cand_w = place_extra(places - 1, places, core_swap(extra), cand_w)
    table, gate_b, cand_b, logit, gain, bias = spare_totals(mine, block_rows, used, mask_logits, feature_allow)
    table = joined(table, core_swap(table), ~first_core)
    table = jnp.swapaxes(table.reshape(columns, embed_width, levels), 1, 2)
    return (block_out, numeric_grad, table, gain, bias, logit,
            gate_w, gate_b, cand_w, cand_b)


def solution(mesh):
    in_specs = (P("dp", None), P("dp", None), P(), P(), P(), P(), P("pipe", None), P("pipe", None),
                P("pipe", None, None), P("pipe", None), P("pipe", None, None), P("pipe", None),
                P("dp", None))
    out_specs = (P("dp", "pipe"), P("dp", "pipe"), P(), P(), P(), P("pipe", None),
                 P("pipe", None, None), P("pipe", None), P("pipe", None, None), P("pipe", None))
    return jax.shard_map(on_device, mesh=mesh, in_specs=in_specs, out_specs=out_specs, check_vma=False)
```

```python
import functools

import jax
import jax.numpy as jnp
from jax import lax
from jax.experimental import pallas as pl
from jax.experimental.pallas import tpu as pltpu
from jax.sharding import PartitionSpec as P

MB = 8
ROWS_MB = 128
BLOCK = 512
EPS = 1e-05
BF = jnp.bfloat16
F32 = jnp.float32


def feature_share(logits, allow):
    allowed = allow > 0
    largest = jnp.max(jnp.where(allowed, logits, -1e30), axis=-1, keepdims=True)
    raised = jnp.where(allowed, jnp.exp(jnp.where(allowed, logits - largest, 0.0)), 0.0)
    return raised / jnp.sum(raised, axis=-1, keepdims=True)


def core_swap(value):
    return lax.ppermute(value, "pipe", [(i, i ^ 1) for i in range(lax.axis_size("pipe"))])


def to_layer(value, up):
    half = lax.axis_size("pipe") // 2
    pairs = [(i, i + half) if up else (i + half, i) for i in range(half)]
    return lax.ppermute(value, "pipe", pairs)


def dp_swap(value, step):
    return lax.ppermute(value, "dp", [(i, i ^ step) for i in range(lax.axis_size("dp"))])


def merged(a, b, held):
    gap = a[0] - b[0]
    return 0.5 * (a[0] + b[0]), a[1] + b[1] + gap * gap * (0.5 * held)


def dp_levels():
    return [1 << i for i in range(lax.axis_size("dp").bit_length() - 1)]


def dp_moments(both, count):
    held = count
    for step in dp_levels()[1:]:
        both = jnp.stack(merged(both, dp_swap(both, step), held))
        held *= 2
    return both


def last_pair(both):
    return both, dp_swap(both, dp_levels()[0])


def last_pair_to_layer(both, up):
    lanes = lax.axis_size("pipe")
    half = lanes // 2
    pairs = []
    for place in range(lax.axis_size("dp")):
        for lane in range(half):
            low, high = lane, lane + half
            start, end = (low, high) if up else (high, low)
            pairs.append((place * lanes + start, (place ^ dp_levels()[0]) * lanes + end))
    return to_layer(both, up), lax.ppermute(both, ("dp", "pipe"), pairs)


def partial_total(value):
    for step in dp_levels()[1:]:
        value = value + dp_swap(value, step)
    return value


def dp_total(value):
    step = 1
    while step < lax.axis_size("dp"):
        value = value + dp_swap(value, step)
        step *= 2
    return value


def plus(a, b):
    return lax.reduce_precision(a.astype(F32) + b.astype(F32), 8, 7).astype(BF)


def halves(value, second):
    mid = value.shape[0] // 2
    a, b = value[:mid], value[mid:]
    return jnp.where(second, b, a), jnp.where(second, a, b)


def joined(kept, got, second):
    return jnp.where(second, jnp.concatenate([got, kept]), jnp.concatenate([kept, got]))


def rounded(value):
    return lax.reduce_precision(value, 8, 7)


def dot(a, b, dims):
    return lax.dot_general(a, b, ((dims[0], dims[1]), ((), ())), preferred_element_type=F32)


def sigmoid(v):
    return 0.5 * jnp.tanh(0.5 * v) + 0.5


def low(v):
    return v.astype(BF).astype(F32)


def nn(a, b):
    return lax.dot_general(a, b, (((1,), (0,)), ((), ())), preferred_element_type=F32)


def nt(a, b):
    return lax.dot_general(a, b, (((1,), (1,)), ((), ())), preferred_element_type=F32)


def column_sum(v):
    return jnp.sum(v, axis=0, keepdims=True)


def batch_rows(i):
    return slice(i * ROWS_MB, (i + 1) * ROWS_MB)


def when_active(layer):
    rank = lax.axis_index("pipe")
    return rank // (lax.axis_size("pipe") // 2) == layer


class Weights:
    def __init__(self, refs, scratch):
        self.own_gate, self.other_gate, self.own_cand, self.other_cand = refs
        self.gate, self.cand, self.sems = scratch
        self.slots = self.gate.shape[0]

    def start(self, k):
        core = lax.axis_index("pipe") % 2
        per_core = self.own_gate.shape[0]
        i, slot = k % per_core, k % self.slots

        def begin(gate, cand):
            pltpu.make_async_copy(gate.at[i], self.gate.at[slot], self.sems.at[0, slot]).start()
            pltpu.make_async_copy(cand.at[i], self.cand.at[slot], self.sems.at[1, slot]).start()

        pl.when(core == k // per_core)(functools.partial(begin, self.own_gate, self.own_cand))
        pl.when(core != k // per_core)(functools.partial(begin, self.other_gate, self.other_cand))

    def wait(self, k):
        slot = k % self.slots
        pltpu.make_async_copy(self.own_gate.at[0], self.gate.at[slot], self.sems.at[0, slot]).wait()
        pltpu.make_async_copy(self.own_cand.at[0], self.cand.at[slot], self.sems.at[1, slot]).wait()


def finish_moments(a, b, moments, held):
    mean, spread = merged(a[...], b[...], held)
    moments[0] = mean
    moments[1] = lax.rsqrt(spread / (2 * held) + EPS)


def normalise(source, moments, affine, x):
    for i in range(source.shape[0] // ROWS_MB):
        at = batch_rows(i)
        xhat = (source[at, :].astype(F32) - moments[0, i : i + 1, :]) * moments[1, i : i + 1, :]
        x[at, :] = xhat * affine[0:1, :] + affine[1:2, :]


def run_forward(x, scales, gate_bias, cand_bias, weights, h, keep=None, after=None):
    rows, width = x.shape
    count = scales.shape[0]
    section = count // 2
    blocks = [slice(i, i + BLOCK) for i in range(0, rows, BLOCK)]

    def spot(k):
        return k if keep else k % 2

    weights.wait(0)
    for at in blocks:
        m = (x[at, :] * scales[0:1, :]).astype(BF)
        zz = sigmoid(nn(m, weights.gate[0, width:, :width]) + gate_bias[0:1, :width])
        cc = jnp.tanh(nn(m, weights.cand[0, width:, :]) + cand_bias[0:1, :])
        h[1, at, :] = zz * cc
        if keep:
            z, r, c, operands = keep
            z[0, at, :], c[0, at, :] = zz, cc
            if operands is not None:
                operands[0, at, width : 2 * width] = m
    if keep:
        after(0)

    def segment(k, _):
        weights.wait(k)
        if keep:
            after.before(k)

        @pl.when(k == section)
        def _():
            x[...] = low(x[...])
            h[spot(k)] = low(h[spot(k)])

        for at in blocks:
            hh = h[spot(k), at, :]
            hb = hh.astype(BF)
            m = (x[at, :] * scales[pl.ds(k, 1), :]).astype(BF)
            both = jnp.concatenate([hb, m], 1)
            bias = gate_bias[pl.ds(k, 1), :]
            rr = sigmoid(nn(both, weights.gate[k, :, width:]) + bias[:, width:])
            zz = sigmoid(nn(both, weights.gate[k, :, :width]) + bias[:, :width])
            rh = (rr * hh).astype(BF)
            cc = jnp.tanh(nn(jnp.concatenate([rh, m], 1), weights.cand[k]) + cand_bias[pl.ds(k, 1), :])
            if keep:
                z[k, at, :], r[k, at, :], c[k, at, :] = zz, rr, cc
                if operands is not None:
                    slot = k % 2
                    operands[slot, at, :width] = hb
                    operands[slot, at, width : 2 * width] = m
                    operands[slot, at, 2 * width :] = rh
            h[spot(k + 1), at, :] = (1.0 - zz) * hh + zz * cc
        if keep:
            after(k)
        return 0

    lax.fori_loop(1, count, segment, 0)


class Out:
    def __init__(self, slotted, sems, kept=(), kept_sems=None):
        self.slotted, self.sems, self.kept, self.kept_sems = slotted, sems, kept, kept_sems

    def slot_copy(self, k):
        source, target = self.slotted
        return pltpu.make_async_copy(source.at[k % 2], target.at[k], self.sems.at[k % 2])

    def kept_copies(self, k):
        return [
            pltpu.make_async_copy(source.at[k], target.at[k], self.kept_sems.at[i, k])
            for i, (source, target) in enumerate(self.kept)
        ]

    def before(self, k):
        if not self.slotted:
            return

        @pl.when(k >= 2)
        def _():
            self.slot_copy(k - 2).wait()

    def __call__(self, k):
        if self.slotted:
            self.slot_copy(k).start()
        for copy in self.kept_copies(k):
            copy.start()

    def finish(self, count):
        if self.slotted:
            self.slot_copy(count - 2).wait()
            self.slot_copy(count - 1).wait()
        if self.kept:
            def wait(k, _):
                for copy in self.kept_copies(k):
                    copy.wait()
                return 0
            lax.fori_loop(0, count, wait, 0)


def run_backward(segments, g, gx, x, scales, weights, states, slots, grads, sums, arrive, done):
    h, z, r, c = states
    rows, width = g.shape
    blocks = [slice(i, i + BLOCK) for i in range(0, rows, BLOCK)]
    high = max(segments)

    def segment(i, _):
        k = high - i
        s = k % slots
        arrive(k)
        totals = None
        for at in blocks:
            gg, hh, zz, rr, cc = g[at, :], h[s, at, :], z[s, at, :], r[s, at, :], c[s, at, :]
            gc = (gg * zz * (1.0 - cc * cc)).astype(BF)
            reset_h = nt(gc, weights.cand[k % weights.slots, :width, :])
            gate_z = (gg * (cc - hh) * zz * (1.0 - zz)).astype(BF)
            gm = nt(gc, weights.cand[k % weights.slots, width:, :])
            gate_r = (reset_h * hh * rr * (1.0 - rr)).astype(BF)
            gates = jnp.concatenate([gate_z, gate_r], 1)
            g[at, :] = gg * (1.0 - zz) + reset_h * rr + nt(gates, weights.gate[k % weights.slots, :width, :])
            gm = gm + nt(gates, weights.gate[k % weights.slots, width:, :])
            gx[at, :] = gx[at, :] + gm * scales[pl.ds(k, 1), :]
            grads[k % 2, at, : 2 * width] = gates
            grads[k % 2, at, 2 * width :] = gc
            part = jnp.concatenate([column_sum(gates.astype(F32)), column_sum(gc.astype(F32)),
                                    column_sum(gm * x[at, :])], 1)
            totals = part if totals is None else totals + part
            done.stage(k, at, lambda: ((x[at, :] * scales[pl.ds(k, 1), :]).astype(BF), hh.astype(BF),
                                       (rr * hh).astype(BF)))
        sums[pl.ds(k, 1), :] = totals
        done(k)
        return 0

    full = [k for k in segments if k > 0]
    lax.fori_loop(0, len(full), segment, 0)
    if min(segments) == 0:
        arrive(0)
        totals = None
        for at in blocks:
            gg, zz, cc = g[at, :], z[0, at, :], c[0, at, :]
            gc = (gg * zz * (1.0 - cc * cc)).astype(BF)
            gate_z = (gg * cc * zz * (1.0 - zz)).astype(BF)
            gm = nt(gc, weights.cand[0, width:, :]) + nt(gate_z, weights.gate[0, width:, :width])
            gx[at, :] = gx[at, :] + gm * scales[0:1, :]
            grads[0, at, :width] = gate_z
            grads[0, at, width : 2 * width] = gc
            part = jnp.concatenate([column_sum(gate_z.astype(F32)), jnp.zeros((1, width), F32),
                                    column_sum(gc.astype(F32)), column_sum(gm * x[at, :])], 1)
            totals = part if totals is None else totals + part
            done.stage(0, at, lambda: ((x[at, :] * scales[0:1, :]).astype(BF),))
        sums[0:1, :] = totals
        done.first()


def tn(a, b):
    return lax.dot_general(a, b, (((0,), (0,)), ((), ())), preferred_element_type=F32)


class Terms:
    def __init__(self, count, operands, grads, made, sems, arrays, after=None):
        self.hidden = 1 - lax.axis_index("pipe") % 2
        self.count, self.operands, self.grads, self.made, self.sems = count, operands, grads, made, sems
        self.arrays, self.after = arrays, after
        self.width = operands.shape[-1] // 3

    def slot(self, k):
        return (self.count - 1 - k) % 2

    def copies(self, k):
        w, part, slot = self.width, self.arrays[0][0].shape[1], self.slot(k)
        start, size = (self.count - 1 - k) * 3 * w, w if k == 0 else 3 * w
        cuts = [(0, start, size)]
        if start < part < start + size:
            cuts = [(0, start, part - start), (part - start, part, start + size - part)]
        return [pltpu.make_async_copy(self.made.at[slot, i, :, pl.ds(at, n)],
                                      self.arrays[i][to // part].at[:, pl.ds(to % part, n)], self.sems.at[slot, i, j])
                for i in range(2) for j, (at, to, n) in enumerate(cuts)]

    def each(self, k, function):
        if isinstance(k, int):
            function(k)
            return
        for known in range(1, self.count):
            pl.when(k == known)(functools.partial(function, known))

    def start(self, k):
        for copy in self.copies(k):
            copy.start()

    def wait(self, k):
        if k < self.count:
            for copy in self.copies(k):
                copy.wait()

    def stage(self, k, at, operands):
        m, *others = operands()
        w = self.width
        self.operands[0, at, w : 2 * w] = m
        if others:
            self.operands[0, at, :w] = others[0]
            self.operands[0, at, 2 * w :] = others[1]

    def __call__(self, k, operands=None, grads=None):
        w = self.width
        operands = self.operands.at[0] if operands is None else operands
        grads = self.grads.at[k % 2] if grads is None else grads
        self.each(k, lambda k: self.wait(k + 2))
        made = self.made.at[self.slot(k)]
        made[self.hidden, :, : 2 * w] = tn(operands[:, :w], grads[:, : 2 * w]).astype(BF)
        made[self.hidden, :, 2 * w :] = tn(operands[:, 2 * w :], grads[:, 2 * w :]).astype(BF)
        made[1 - self.hidden] = tn(operands[:, w : 2 * w], grads[...]).astype(BF)
        self.each(k, self.start)
        if self.after:
            self.after(k)

    def first(self, operands=None, grads=None):
        w = self.width
        operands = self.operands.at[0] if operands is None else operands
        grads = self.grads.at[0] if grads is None else grads
        self.wait(2)
        made = self.made.at[self.slot(0)]
        made[self.hidden, :, :w] = tn(operands[:, w : 2 * w], grads[:, :w]).astype(BF)
        made[1 - self.hidden, :, :w] = tn(operands[:, w : 2 * w], grads[:, w : 2 * w]).astype(BF)
        self.start(0)
        self.wait(1)
        self.wait(0)


def terms_from_hbm(terms, operands_in, grads_in, sems):
    count = terms.count

    def copies(k):
        slot = k % 2
        return [pltpu.make_async_copy(x.at[k], y.at[slot], sems.at[slot, j])
                for j, (x, y) in enumerate(((operands_in, terms.operands), (grads_in, terms.grads)))]

    for copy in copies(count - 1):
        copy.start()

    def segment(i, _):
        k = count - 1 - i
        for copy in copies(k - 1):
            copy.start()
        for copy in copies(k):
            copy.wait()
        terms(k, terms.operands.at[k % 2], terms.grads.at[k % 2])
        return 0

    lax.fori_loop(0, count - 1, segment, 0)
    for copy in copies(0):
        copy.wait()
    terms.first()


def norm_sums(gx, xhat_of, sums):
    for i in range(gx.shape[0] // ROWS_MB):
        part = gx[batch_rows(i), :]
        sums[0, i : i + 1, :] = column_sum(part)
        sums[1, i : i + 1, :] = column_sum(part * xhat_of(i))


def xhat_rows(source, moments, i):
    return (source[batch_rows(i), :].astype(F32) - moments[0, i : i + 1, :]) * moments[1, i : i + 1, :]


ANY = pl.BlockSpec(memory_space=pl.ANY)
VM = pl.BlockSpec(memory_space=pltpu.VMEM)
LIMIT = 62 * 1024 * 1024


def layer_cost(segments, rows, width, passes):
    return pl.CostEstimate(flops=segments * passes * rows * 12 * width * width, transcendentals=0,
                           bytes_accessed=segments * (12 * width * width + 16 * rows * width))


def layer1_forward(source, moments, affine, scales, gate_bias, cand_bias, weights, keep):
    rows, width = source.shape
    count = scales.shape[0]

    dp_half = ROWS_MB * lax.axis_size("dp") // 2

    def kernel(*refs):
        if keep:
            source, moments = refs[:2]
            refs = refs[2:]
        else:
            source, first_half, second_half = refs[:3]
            refs = refs[3:]
        affine, scales, gate_bias, cand_bias, w0, w1, w2, w3 = refs[:8]
        refs = refs[8:]
        if keep:
            kept_h, kept_z, kept_r, kept_c = refs[:4]
            x, gate, cand, wsems, h, z, r, c, ksems = refs[4:]
        else:
            last, local, moments = refs[:3]
            x, gate, cand, wsems, h = refs[3:]

        @pl.when(when_active(0))
        def _():
            held = Weights((w0, w1, w2, w3), (gate, cand, wsems))
            for k in range(count):
                held.start(k)
            if not keep:
                finish_moments(first_half, second_half, moments, dp_half)
            normalise(source, moments, affine.at[0], x)
            if keep:
                out = Out(None, None, ((h, kept_h), (z, kept_z), (r, kept_r), (c, kept_c)), ksems)
                run_forward(x, scales, gate_bias, cand_bias, held, h, (z, r, c, None), out)
                out.finish(count)
                return
            run_forward(x, scales, gate_bias, cand_bias, held, h)
            final = h.at[count % 2]
            last[...] = final[...].astype(BF)
            for i in range(rows // ROWS_MB):
                part = low(final[batch_rows(i), :])
                mean = column_sum(part) * (1.0 / ROWS_MB)
                local[0, i : i + 1, :] = mean
                local[1, i : i + 1, :] = column_sum((part - mean) * (part - mean))

    state = jax.ShapeDtypeStruct((count, rows, width), F32)
    by_batch = jax.ShapeDtypeStruct((2, rows // ROWS_MB, width), F32)
    scratch = [pltpu.VMEM((rows, width), F32),
               pltpu.VMEM((count, 2 * width, 2 * width), BF),
               pltpu.VMEM((count, 2 * width, width), BF),
               pltpu.SemaphoreType.DMA((2, count))]
    if keep:
        out_shape = (state,) * 4
        out_specs = (ANY,) * 4
        scratch += [pltpu.VMEM((count + 1, rows, width), F32)] + [pltpu.VMEM((count, rows, width), F32)] * 3
        scratch += [pltpu.SemaphoreType.DMA((4, count))]
    else:
        out_shape = (jax.ShapeDtypeStruct((rows, width), BF), by_batch, by_batch)
        out_specs = (VM, VM, VM)
        scratch += [pltpu.VMEM((2, rows, width), F32)]
    args = (source,) + (moments if isinstance(moments, tuple) else (moments,))
    args += (affine, scales, gate_bias, cand_bias)
    return pl.pallas_call(
        kernel,
        out_shape=out_shape,
        in_specs=[VM] * len(args) + [ANY] * 4,
        out_specs=out_specs,
        scratch_shapes=scratch,
        compiler_params=pltpu.CompilerParams(vmem_limit_bytes=LIMIT),
        cost_estimate=layer_cost(count, rows, width, 1),
        name="layer1_states" if keep else "layer1_forward",
    )(*args, *weights)


def layer2_both(source, halves_of_moments, affine, scales, gate_bias, cand_bias, weights, cotangent):
    rows, width = source.shape
    count = scales.shape[0]

    dp_half = ROWS_MB * lax.axis_size("dp") // 2

    def kernel(source, first_half, second_half, affine, scales, gate_bias, cand_bias, w0, w1, w2, w3, cotangent,
               last, gx_out, nsums, sums, operands_out, grads_out,
               x, gate, cand, wsems, h, z, r, c, operands, osems, g, gx, gsem, moments):
        @pl.when(when_active(1))
        def _():
            held = Weights((w0, w1, w2, w3), (gate, cand, wsems))
            for k in range(count):
                held.start(k)
            core = lax.axis_index("pipe") % 2
            first = pl.multiple_of(core * rows, rows)
            load_g = pltpu.make_async_copy(cotangent.at[pl.ds(first, rows), :], g, gsem.at[0])
            load_g.start()
            finish_moments(first_half, second_half, moments, dp_half)
            normalise(source, moments, affine.at[1], x)
            out = Out((operands, operands_out), osems)
            run_forward(x, scales, gate_bias, cand_bias, held, h, (z, r, c, operands), out)
            last[...] = h[count]
            out.finish(count)
            load_g.wait()
            gx[...] = jnp.zeros_like(gx)

            section = count // 2

            class Left:
                def stage(self, k, at, operands):
                    pass

                def copy(self, k):
                    return pltpu.make_async_copy(operands.at[k % 2], grads_out.at[k], osems.at[k % 2])

                def __call__(self, k):
                    self.copy(k).start()

                def first(self):
                    self.copy(0).start()
                    self.copy(1).wait()
                    self.copy(0).wait()

            left = Left()

            def free(k):
                @pl.when(k <= count - 3)
                def _():
                    left.copy(k + 2).wait()

            run_backward(range(section, count), g, gx, x, scales, held, (h, z, r, c), count, operands, sums, free, left)
            g[...] = low(g[...])
            gx[...] = low(gx[...])
            normalise(source, moments, affine.at[1], x)
            run_backward(range(section), g, gx, x, scales, held, (h, z, r, c), count, operands, sums, free, left)
            gx_out[...] = gx[...].astype(BF)
            norm_sums(gx, lambda i: xhat_rows(source, moments, i), nsums)

    state = pltpu.VMEM((count, rows, width), F32)
    left_out = jax.ShapeDtypeStruct((count, rows, 3 * width), BF)
    return pl.pallas_call(
        kernel,
        out_shape=(jax.ShapeDtypeStruct((rows, width), F32),
                   jax.ShapeDtypeStruct((rows, width), BF),
                   jax.ShapeDtypeStruct((2, rows // ROWS_MB, width), F32),
                   jax.ShapeDtypeStruct((count, 4 * width), F32),
                   left_out, left_out),
        in_specs=[VM] * 7 + [ANY] * 5,
        out_specs=(VM, VM, VM, VM, ANY, ANY),
        scratch_shapes=[pltpu.VMEM((rows, width), F32),
                        pltpu.VMEM((count, 2 * width, 2 * width), BF),
                        pltpu.VMEM((count, 2 * width, width), BF),
                        pltpu.SemaphoreType.DMA((2, count)),
                        pltpu.VMEM((count + 1, rows, width), F32), state, state, state,
                        pltpu.VMEM((2, rows, 3 * width), BF),
                        pltpu.SemaphoreType.DMA((2,)),
                        pltpu.VMEM((rows, width), F32),
                        pltpu.VMEM((rows, width), F32),
                        pltpu.SemaphoreType.DMA((1,)),
                        pltpu.VMEM((2, rows // ROWS_MB, width), F32)],
        compiler_params=pltpu.CompilerParams(vmem_limit_bytes=LIMIT),
        cost_estimate=layer_cost(count, rows, width, 2),
        name="layer2_both",
    )(source, *halves_of_moments, affine, scales, gate_bias, cand_bias, *weights, cotangent)


def layer1_backward(carried, source, moments, affine, scales, weights, kept, operands, grads):
    rows, width = source.shape
    count = scales.shape[0]
    section = count // 2
    slots = 3
    counted = ROWS_MB * lax.axis_size("dp")
    part = (3 * count - 2) * width // 2

    def kernel(gxr, hb, moments2, total_a, total_b, source, moments, affine, scales, w0, w1, w2, w3,
               kept_h, kept_z, kept_r, kept_c, operands_in, grads_in,
               gx, nsums, sums, sent_a, sent_b, mine_a, mine_b,
               x, gate, cand, wsems, h, z, r, c, ksems, g, loaded, staged, lsems, made, msems):
        held = Weights((w0, w1, w2, w3), (gate, cand, wsems))
        states = ((kept_h, h), (kept_z, z), (kept_r, r), (kept_c, c))

        def copies(k):
            return [pltpu.make_async_copy(x.at[k], y.at[k % slots], ksems.at[i, k % slots])
                    for i, (x, y) in enumerate(states)]

        def arrive(k):
            held.wait(k)
            for copy in copies(k):
                copy.wait()

        def load(k):
            for copy in copies(k):
                copy.start()
            held.start(k)

        def after(k):
            @pl.when(k >= slots)
            def _():
                load(k - slots)

        terms = Terms(count, staged, loaded, made, msems, ((sent_a, sent_b), (mine_a, mine_b)), after)

        @pl.when(when_active(1))
        def _():
            terms.after = None
            terms_from_hbm(terms, operands_in, grads_in, lsems)

        @pl.when(when_active(0))
        def _():
            terms.after = after
            for k in range(count - 1, count - 1 - slots, -1):
                load(k)
            normalise(source, moments, affine.at[0], x)
            x[...] = low(x[...])
            for i in range(rows // ROWS_MB):
                at = batch_rows(i)
                mean_g, mean_gx = [(total_a[j, i : i + 1, :] + total_b[j, i : i + 1, :]) / counted for j in (0, 1)]
                back = gxr[at, :].astype(F32) - mean_g - xhat_rows(hb, moments2, i) * mean_gx
                g[at, :] = low(affine[1, 0:1, :] * moments2[1, i : i + 1, :] * back)
            gx[...] = jnp.zeros_like(gx)
            run_backward(range(section, count), g, gx, x, scales, held, (h, z, r, c), slots, loaded, sums, arrive, terms)
            g[...] = low(g[...])
            gx[...] = low(gx[...])
            normalise(source, moments, affine.at[0], x)
            run_backward(range(section), g, gx, x, scales, held, (h, z, r, c), slots, loaded, sums, arrive, terms)
            norm_sums(gx, lambda i: xhat_rows(source, moments, i), nsums)

    state = pltpu.VMEM((slots, rows, width), F32)
    terms = jax.ShapeDtypeStruct((width, part), BF)
    args = [*carried, source, moments, affine, scales, *weights, *kept, operands, grads]
    return pl.pallas_call(
        kernel,
        out_shape=(jax.ShapeDtypeStruct((rows, width), F32),
                   jax.ShapeDtypeStruct((2, rows // ROWS_MB, width), F32),
                   jax.ShapeDtypeStruct((count, 4 * width), F32), terms, terms, terms, terms),
        in_specs=[VM] * 9 + [ANY] * 10,
        out_specs=(VM,) * 3 + (ANY,) * 4,
        scratch_shapes=[pltpu.VMEM((rows, width), F32),
                        pltpu.VMEM((slots, 2 * width, 2 * width), BF),
                        pltpu.VMEM((slots, 2 * width, width), BF),
                        pltpu.SemaphoreType.DMA((2, slots)),
                        state, state, state, state,
                        pltpu.SemaphoreType.DMA((4, slots)),
                        pltpu.VMEM((rows, width), F32),
                        pltpu.VMEM((2, rows, 3 * width), BF),
                        pltpu.VMEM((2, rows, 3 * width), BF),
                        pltpu.SemaphoreType.DMA((2, 2)),
                        pltpu.VMEM((2, 2, width, 3 * width), BF),
                        pltpu.SemaphoreType.DMA((2, 2, 2))],
        compiler_params=pltpu.CompilerParams(vmem_limit_bytes=LIMIT),
        cost_estimate=layer_cost(count, rows, width, 2),
        name="layer1_backward",
    )(*args)


def hot_rows(cats, c, levels):
    level = lax.broadcasted_iota(jnp.int32, (levels, cats.shape[1]), 0)
    return jnp.where(cats[c : c + 1, :] == level, 1.0, 0.0).astype(BF)


def load_columns(categories, cats, sem, rows):
    first = pl.multiple_of((lax.axis_index("pipe") % 2) * rows, rows)
    return pltpu.make_async_copy(categories.at[:, pl.ds(first, rows)], cats, sem)


def embed(numeric, categories, table, rows, own, other, affine):
    numeric_width, columns = numeric.shape[1], categories.shape[0]
    embedded, levels = table.shape
    each = embedded // columns
    packed = 128 // each
    width = numeric_width + embedded

    half = own[0].shape[0]

    def kernel(numeric, categories, table, *refs):
        own, other, (bn_gain, bn_bias) = refs[:4], refs[4:8], refs[8:10]
        source, local, scales, gate_bias, cand_bias, affine, cats, nums, sems = refs[10:]
        core = lax.axis_index("pipe") % 2

        def put(logits, allow, gates, cands, at):
            scales[at : at + half, :] = width * feature_share(logits[...], allow[...])
            gate_bias[at : at + half, :] = gates[...]
            cand_bias[at : at + half, :] = cands[...]

        for at, owner in ((0, 0), (half, 1)):
            pl.when(core == owner)(functools.partial(put, *own, at))
            pl.when(core != owner)(functools.partial(put, *other, at))
        for layer in range(2):
            affine[layer, 0:1, :] = bn_gain[layer : layer + 1, :]
            affine[layer, 1:2, :] = bn_bias[layer : layer + 1, :]
        first = pl.multiple_of((lax.axis_index("pipe") % 2) * rows, rows)
        load = load_columns(categories, cats, sems.at[0], rows)
        load_numeric = pltpu.make_async_copy(numeric.at[pl.ds(first, rows), :], nums, sems.at[1])
        load.start()
        load_numeric.start()
        load.wait()
        row = lax.broadcasted_iota(jnp.int32, (128, levels), 0) // each
        for group in range(columns // packed):
            part = table[group * 128 : (group + 1) * 128, :]
            weights = jnp.concatenate([jnp.where(row == i, part, jnp.zeros_like(part)) for i in range(packed)], 1)
            hot = jnp.concatenate([hot_rows(cats, group * packed + i, levels) for i in range(packed)], 0)
            start = numeric_width + group * 128
            source[:, start : start + 128] = nn(weights, hot).T
        load_numeric.wait()
        source[:, :numeric_width] = nums[...]
        for i in range(rows // ROWS_MB):
            part = source[batch_rows(i), :]
            mean = column_sum(part) * (1.0 / ROWS_MB)
            local[0, i : i + 1, :] = mean
            local[1, i : i + 1, :] = column_sum((part - mean) * (part - mean))

    return pl.pallas_call(
        kernel,
        out_shape=(jax.ShapeDtypeStruct((rows, width), F32),
                   jax.ShapeDtypeStruct((2, rows // ROWS_MB, width), F32),
                   jax.ShapeDtypeStruct((2 * half, width), F32),
                   jax.ShapeDtypeStruct((2 * half, 2 * width), F32),
                   jax.ShapeDtypeStruct((2 * half, width), F32),
                   jax.ShapeDtypeStruct((2, 2, width), F32)),
        in_specs=[ANY, ANY] + [VM] * 11,
        out_specs=(VM,) * 6,
        scratch_shapes=[pltpu.VMEM((columns, rows), jnp.int32), pltpu.VMEM((rows, numeric_width), F32),
                        pltpu.SemaphoreType.DMA((2,))],
        compiler_params=pltpu.CompilerParams(vmem_limit_bytes=LIMIT),
        cost_estimate=pl.CostEstimate(flops=8 * rows * width * levels, transcendentals=0, bytes_accessed=8 * rows * width),
        name="embed",
    )(numeric, categories, table, *own, *other, *affine)


def feature_grads(gx, source, moments, totals, gain, categories, table_shape):
    rows, width = gx.shape
    embedded, levels = table_shape
    columns = categories.shape[0]
    each = embedded // columns
    numeric_width = width - embedded
    half = columns // 2

    def kernel(gx, source, moments, totals, gain, categories, numeric, sent, mine, cats, back, table, sem):
        load = load_columns(categories, cats, sem.at[0], rows)
        load.start()
        for i in range(rows // ROWS_MB):
            at = batch_rows(i)
            part = gx[at, :] - totals[0, i : i + 1, :] - xhat_rows(source, moments, i) * totals[1, i : i + 1, :]
            back[at, :] = gain[...] * moments[1, i : i + 1, :] * part
        numeric[...] = back[:, :numeric_width]
        load.wait()
        table[...] = jnp.zeros_like(table)
        for group in range(embedded // 128):
            start = numeric_width + group * 128
            grads = back[:, start : start + 128].astype(BF)
            lane = lax.broadcasted_iota(jnp.int32, (levels, 128), 1) // each
            blocks = jnp.zeros((levels, 128), F32)
            for i in range(128 // each):
                c = group * (128 // each) + i
                blocks = jnp.where(lane == i, nn(hot_rows(cats, c, levels), grads), blocks)
            turned = blocks.T
            for i in range(128 // each):
                c = group * (128 // each) + i
                for e in range(each):
                    at = i * each + e
                    table[c // half, c % half : c % half + 1, e * levels : (e + 1) * levels] = turned[at : at + 1, :]
        core = lax.axis_index("pipe") % 2
        sent[...] = table[1 - core].astype(BF)
        mine[...] = table[core].astype(BF)

    part = jax.ShapeDtypeStruct((16, each * levels), BF)
    return pl.pallas_call(
        kernel,
        out_shape=(jax.ShapeDtypeStruct((rows, numeric_width), F32), part, part),
        in_specs=[VM] * 5 + [ANY],
        out_specs=(VM, VM, VM),
        scratch_shapes=[pltpu.VMEM((columns, rows), jnp.int32), pltpu.VMEM((rows, width), F32),
                        pltpu.VMEM((2, 16, each * levels), F32), pltpu.SemaphoreType.DMA((1,))],
        compiler_params=pltpu.CompilerParams(vmem_limit_bytes=LIMIT),
        cost_estimate=pl.CostEstimate(flops=8 * rows * width * levels, transcendentals=0, bytes_accessed=16 * rows * width),
        name="feature_grads",
    )(gx, source, moments, totals, gain, categories)


def spare_totals(pieces, rows, used, logits, allow):
    count = len(pieces)
    spare, columns = pieces[0].shape[0] - rows, pieces[0].shape[1]
    half, width = logits.shape

    def kernel(logits, allow, *refs):
        pieces, (table, gate_b, cand_b, logit, gain, bias, parts, sems) = refs[:count], refs[count:]
        copies = [pltpu.make_async_copy(piece.at[pl.ds(rows, spare), :], parts.at[i], sems.at[i])
                  for i, piece in enumerate(pieces)]
        for copy in copies:
            copy.start()
        shares = feature_share(logits[...], allow[...])
        for copy in copies:
            copy.wait()
        spot = ring_place(count)
        added = jnp.zeros((spare, columns), F32)
        for place in range(count):
            added = added + parts[lax.rem(spot - place + count, count)].astype(F32)
        table[...] = added[:used, :]
        small = added[used:, : columns // 2] + added[used:, columns // 2 :]
        gate_b[...] = small[:half, : 2 * width]
        cand_b[...] = small[:half, 2 * width : 3 * width]
        scaled = width * small[:half, 3 * width :]
        logit[...] = shares * (scaled - jnp.sum(shares * scaled, axis=-1, keepdims=True))
        for layer in range(2):
            at = layer * width
            bias[layer : layer + 1, :] = small[half : half + 1, at : at + width]
            gain[layer : layer + 1, :] = small[half : half + 1, 2 * width + at : 3 * width + at]

    def out(*shape):
        return jax.ShapeDtypeStruct(shape, F32)

    return pl.pallas_call(
        kernel,
        out_shape=(out(used, columns), out(half, 2 * width), out(half, width), out(half, width), out(2, width),
                   out(2, width)),
        in_specs=[VM, VM] + [ANY] * count,
        out_specs=(VM,) * 6,
        scratch_shapes=[pltpu.VMEM((count, spare, columns), BF), pltpu.SemaphoreType.DMA((count,))],
        compiler_params=pltpu.CompilerParams(vmem_limit_bytes=LIMIT),
        name="spare_totals",
    )(logits, allow, *pieces)


def ring_place(places):
    place = lax.axis_index("dp")
    spot = jnp.where(place % 2 == 0, place // 2, places - 1 - place // 2)
    return jnp.where(lax.axis_index("pipe") % 2 == 0, spot, places - 1 - spot)


def blank_outputs(per_core, width):
    def kernel(gate, cand, zeros, sems):
        @pl.when(lax.axis_index("pipe") % 2 == 0)
        def _():
            zeros[...] = jnp.zeros_like(zeros)
            copies = [
                pltpu.make_async_copy(zeros, gate.at[0, pl.ds(0, width), :], sems.at[0]),
                pltpu.make_async_copy(zeros.at[:, pl.ds(0, width)],
                                      gate.at[0, pl.ds(width, width), pl.ds(width, width)], sems.at[1]),
                pltpu.make_async_copy(zeros.at[:, pl.ds(0, width)], cand.at[0, pl.ds(0, width), :], sems.at[2])]
            for copy in copies:
                copy.start()
            for copy in copies:
                copy.wait()

    return pl.pallas_call(
        kernel,
        out_shape=(jax.ShapeDtypeStruct((per_core, 2 * width, 2 * width), F32),
                   jax.ShapeDtypeStruct((per_core, 2 * width, width), F32)),
        out_specs=(ANY, ANY),
        scratch_shapes=[pltpu.VMEM((width, 2 * width), F32), pltpu.SemaphoreType.DMA((3,))],
        name="blank_outputs",
    )()


def place_block(step, blocks, mine, other, extra, gate, cand):
    rows, columns = other.shape
    per_core, width = gate.shape[0], cand.shape[2]
    given = () if extra is None else (extra,)

    def kernel(*refs):
        mine, other = refs[:2]
        extra = refs[2] if given else None
        gate, cand, onward, full, tail, sems = refs[4 + len(given) :]
        spot = ring_place(blocks)
        copies = []

        def copy(source, target, j, row, size):
            copies.append(pltpu.make_async_copy(
                source, target.at[j, pl.ds(row, rows), pl.ds(0, size)], sems.at[len(copies)]))
            copies[-1].start()

        def at(block):
            return pl.multiple_of(block * rows, rows)

        def put(own_half, first_layer):
            del copies[:]
            own_block = lax.rem(spot + 1 - step + blocks, blocks)
            other_block = lax.rem(2 * blocks - spot + step, blocks)
            if not first_layer and given:
                put_extra(spot, step - 1, blocks, extra, tail, cand, copies, sems)
            for piece, half, block in ((mine, own_half, own_block), (other, 1 - own_half, other_block)):
                full[half] = piece[:rows, :].astype(F32)
                for j in range(per_core):
                    start = (per_core - 1 - j) * 3 * width + (width if first_layer else 0)
                    source = full.at[half]
                    if first_layer and j == 0:
                        copy(source.at[:, pl.ds(start, width)], cand if half else gate, 0, width + at(block), width)
                        continue
                    copy(source.at[:, pl.ds(start, 2 * width)], gate, j, half * width + at(block), 2 * width)
                    if j or first_layer:
                        copy(source.at[:, pl.ds(start + 2 * width, width)], cand, j, half * width + at(block), width)
            if first_layer:
                onward[:rows, :] = mine[:rows, :width]
                onward[rows:, :] = other[:, :width]
            for item in copies:
                item.wait()

        core = lax.axis_index("pipe") % 2
        pl.when(core == 0)(functools.partial(put, 0, True))
        pl.when(core == 1)(functools.partial(put, 1, False))

    args = (mine, other, *given, gate, cand)
    return pl.pallas_call(
        kernel,
        out_shape=(jax.ShapeDtypeStruct(gate.shape, F32), jax.ShapeDtypeStruct(cand.shape, F32),
                   jax.ShapeDtypeStruct((2 * rows, width), BF)),
        in_specs=[VM] * (len(args) - 2) + [ANY] * 2,
        out_specs=(ANY, ANY, VM),
        input_output_aliases={len(args) - 2: 0, len(args) - 1: 1},
        scratch_shapes=[pltpu.VMEM((2, rows, columns), F32), pltpu.VMEM((2, rows, width), F32),
                        pltpu.SemaphoreType.DMA((4 * per_core,))],
        compiler_params=pltpu.CompilerParams(vmem_limit_bytes=LIMIT),
        name=f"place_block_{step}",
    )(*args)


def put_extra(spot, step, blocks, extra, tail, cand, copies, sems):
    rows, width = tail.shape[1:]
    for half, block in ((0, lax.rem(2 * blocks - spot - step, blocks)), (1, lax.rem(spot + 1 + step, blocks))):
        tail[half] = extra[half * rows : (half + 1) * rows, :].astype(F32)
        row = half * width + pl.multiple_of(block * rows, rows)
        copies.append(pltpu.make_async_copy(tail.at[half], cand.at[0, pl.ds(row, rows), :], sems.at[len(copies)]))
        copies[-1].start()


def place_extra(step, blocks, extra, cand):
    width = cand.shape[2]
    rows = extra.shape[0] // 2

    def kernel(extra, unused, cand, tail, sems):
        @pl.when(lax.axis_index("pipe") % 2 == 1)
        def _():
            copies = []
            put_extra(ring_place(blocks), step, blocks, extra, tail, cand, copies, sems)
            for item in copies:
                item.wait()

    return pl.pallas_call(
        kernel,
        out_shape=jax.ShapeDtypeStruct(cand.shape, F32),
        in_specs=[VM, ANY],
        out_specs=ANY,
        input_output_aliases={1: 0},
        scratch_shapes=[pltpu.VMEM((2, rows, width), F32), pltpu.SemaphoreType.DMA((2,))],
        compiler_params=pltpu.CompilerParams(vmem_limit_bytes=LIMIT),
        name="place_extra",
    )(extra, cand)


def tied(*values):
    return lax.optimization_barrier(values)


class Ring:
    def __init__(self, parts=None, held=None, unit=None, turn=None):
        self.turn = turn
        self.unit = unit
        self.places = lax.axis_size("dp")
        order = list(range(0, self.places, 2)) + list(range(1, self.places, 2))[::-1]
        lanes = lax.axis_size("pipe")
        self.pairs = []
        for lane in range(lanes):
            way = order if lane % 2 == 0 else order[::-1]
            self.pairs += [(way[i] * lanes + lane, way[(i + 1) % self.places] * lanes + lane)
                           for i in range(self.places)]
        self.spot = ring_place(self.places)
        self.parts = ()
        self.done = 0
        self.held = held
        if held is None:
            mine, received, first = parts
            self.rows = mine.shape[0] // self.places
            self.parts = (mine, received)
            self.held = (self.rows_of(mine, self.spot).astype(F32) + first.astype(F32)).astype(BF)

    def rows_of(self, part, number):
        at = lax.rem(number + self.places, self.places) * self.rows
        return lax.dynamic_slice_in_dim(part, at, self.rows, 0)

    def block(self, number):
        a, b = [self.rows_of(part, number) for part in self.parts]
        return a.astype(F32) + b.astype(F32)

    def step(self, sends=(), work=None, ends=None, wait=True):
        self.done += 1
        sent = len(sends)
        works = work if isinstance(work, list) else [work] if work else []
        held, *values = tied(self.held, *[value for _, value in sends], *[value for _, given in works for value in given])
        got = lax.ppermute(held, ("dp", "pipe"), self.pairs)
        given = [send(value) for (send, _), value in zip(sends, values)]
        outs, values = [], values[sent:]
        for function, arguments in works + ([ends] if ends else []):
            if function is not (ends or [None])[0]:
                arguments, values = values[: len(arguments)], values[len(arguments) :]
            result = function(*arguments)
            outs += list(result) if isinstance(result, (tuple, list)) else [result]
        if self.turn is not None:
            got, *_ = tied(got, *self.turn)
            self.turn[:] = [got]
        got, *outs = tied(got, *outs, *(given if wait else ()))
        if wait:
            given, outs = outs[len(outs) - sent :], outs[: len(outs) - sent]
        if self.unit is not None and self.done < self.places - 1:
            got = got * self.unit
        if self.parts:
            got = (self.block(self.spot - self.done) + got.astype(F32)).astype(BF)
        self.held = got
        return list(given) + outs


def on_device(numeric, categories, cardinalities, embed_table, bn_gain, bn_bias, mask_logits,
              feature_allow, gate_weight, gate_bias, cand_weight, cand_bias, out_grad):
    rank = lax.axis_index("pipe")
    core = rank % 2
    first_core = core == 0
    top = rank >= lax.axis_size("pipe") // 2
    width = out_grad.shape[1]
    numeric_width = numeric.shape[1]
    columns, levels, embed_width = embed_table.shape
    batches = MB // 2
    rows = batches * ROWS_MB
    counted = ROWS_MB * lax.axis_size("dp")

    def my_rows(array):
        return lax.dynamic_slice_in_dim(array, core * rows, rows, 0)

    def by_batch(array):
        return array.reshape(batches, ROWS_MB, array.shape[-1])

    half = gate_weight.shape[0]
    count = 2 * half
    flat_table = jnp.swapaxes(embed_table, 1, 2).reshape(columns * embed_width, levels)
    category_columns = categories.T
    own_small = (mask_logits, feature_allow, gate_bias, cand_bias)
    other_small = tuple(core_swap(value) for value in own_small)
    *other_small, own_gate, own_cand = tied(*other_small, gate_weight, cand_weight)
    weights = (gate_weight, core_swap(own_gate), cand_weight, core_swap(own_cand))
    source1, local1, scales, gate_b, cand_b, affine = embed(
        numeric, category_columns, flat_table, rows, own_small, other_small, (bn_gain, bn_bias))
    h1, local2, moments1 = layer1_forward(
        source1, last_pair(dp_moments(local1, ROWS_MB)), affine, scales, gate_b, cand_b, weights, False)
    source2 = to_layer(h1, True)
    local2 = dp_moments(local2, ROWS_MB)
    halves2 = last_pair_to_layer(local2, True)
    local2, source1 = lax.optimization_barrier((local2, source1))
    kept_states = layer1_forward(source1, moments1, affine, scales, gate_b, cand_b, weights, True)
    mean2, spread2 = merged(*last_pair(local2), counted // 2)
    moments2 = jnp.stack([mean2, lax.rsqrt(spread2 / counted + EPS)])
    h2, gx2, nsums2, sums2, operands, grads = layer2_both(
        source2, halves2, affine, scales, gate_b, cand_b, weights, out_grad)
    received = to_layer(gx2, False)
    totals2 = last_pair_to_layer(partial_total(nsums2), False)

    def layer_columns(value):
        share = value.shape[1] // 4
        pieces = value.reshape(rows, 2, 2, share)
        kept = jnp.where(first_core, pieces[:, :, 0], pieces[:, :, 1])
        got = core_swap(jnp.where(first_core, pieces[:, :, 1], pieces[:, :, 0]))
        both = jnp.where(first_core, jnp.stack([kept, got]), jnp.stack([got, kept]))
        return both.reshape(2 * rows, 2, share)

    def pick(a, b):
        return jnp.where(top, a, b)

    gx1, nsums1, sums1, sent_a, sent_b, mine_a, mine_b = layer1_backward(
        (received, h1, moments2, *totals2), source1, moments1, affine, scales, weights, kept_states, operands, grads)
    places = lax.axis_size("dp")

    def first_block(sent):
        rows = sent.shape[0] // places
        return core_swap(lax.dynamic_slice_in_dim(sent, (places - 1 - ring_place(places)) * rows, rows, 0))

    first_a, first_b = first_block(sent_a), first_block(sent_b)
    first_a, first_b, sent_a, sent_b = tied(first_a, first_b, sent_a, sent_b)
    upper = Ring((mine_a, core_swap(sent_a), first_a))
    lower = Ring((mine_b, core_swap(sent_b), first_b))
    pipes = lax.axis_size("pipe")

    levels_of_dp = [1 << i for i in range(places.bit_length() - 1)]

    def over_layers(value):
        return lax.ppermute(value, "pipe", [(i, (i + pipes // 2) % pipes) for i in range(pipes)])

    def small_sums(sums1, sums2, nsums1, nsums2):
        small = pick(sums2, sums1).reshape(count, 4 * width)
        kept, sent_sums = halves(small, ~first_core)
        sums = [nsums.sum(axis=1) for nsums in (nsums1, nsums2)]
        sums = jnp.stack([jnp.where(top, 0.0, sums[0]), jnp.where(top, sums[1], 0.0)], axis=1).reshape(-1, 4 * width)
        small = jnp.concatenate([kept, sums]) + core_swap(jnp.concatenate([sent_sums, sums]))
        return small

    def features(gx1, totals1):
        return feature_grads(gx1, source1, moments1, totals1, bn_gain[:1], category_columns, flat_table.shape)

    totals1 = nsums1
    used = columns // 2
    chain = [("",)] + [("sum", level) for level in levels_of_dp] + [("features",), ("cores",), ("layers",)]
    while lower.done < places - 1:
        act = chain.pop(0) if chain else ("",)
        if act[0] == "sum":
            got, = upper.step(((functools.partial(dp_swap, step=act[1]), totals1),))
            totals1 = totals1 + got
        elif act[0] == "features":
            numeric_back, table_sent, table = upper.step(work=(features, (gx1, totals1 / counted)))
        elif act[0] == "cores":
            got, = upper.step(((core_swap, table_sent),))
            table = plus(table, got)
        elif act[0] == "layers":
            got, got_sums = upper.step(((functools.partial(to_layer, up=True), table), (over_layers, small[half:])))
            high = lax.reduce_precision(jnp.concatenate([small[:half], small[half:] + got_sums]), 8, 7)
            low_part = jnp.concatenate([small[:half], small[half:] + got_sums]) - high
            table = jnp.concatenate([pick(got, table)[:used], jnp.concatenate([high, low_part], 1).astype(BF)])
        else:
            upper.step(ends=None if lower.done else (lambda held: held, (lower.held,)))
        if lower.done == 1:
            small, = lower.step(work=(small_sums, (sums1, sums2, nsums1, nsums2)))
        elif lower.done == 5:
            block, = lower.step(work=(layer_columns, (h2,)))
        elif lower.done == 2:
            gate_w, cand_w = lower.step(work=(lambda: blank_outputs(half, width), ()))
        else:
            lower.step()

    block_rows = upper.held.shape[0]
    unit = (1.0 + 0.0 * cardinalities[0].astype(F32)).astype(BF)
    turn = []
    own = Ring(held=jnp.concatenate([jnp.where(first_core, lower.held, upper.held), table]), unit=unit, turn=turn)
    other = Ring(held=core_swap(jnp.where(first_core, upper.held, lower.held)), unit=unit, turn=turn)
    mine, extra = [], None
    for s in range(places):
        mine.append(own.held)
        place = functools.partial(place_block, s, places)
        if extra is None:
            place = lambda a, b, *rest: place_block(0, places, a, b, None, *rest)
        values = (own.held, other.held, *(() if extra is None else (extra,)), gate_w, cand_w)
        if s == places - 1:
            gate_w, cand_w, extra = place(*values)
            break
        if s == places - 2:
            gate_w, cand_w, extra = own.step(ends=(place, values))
            extra = core_swap(extra)
            other.step()
            continue
        own.step()
        sends, ends, works = (), None, [(place, values)]
        if s == 1:
            sends = ((functools.partial(to_layer, up=False), block[:, 0]),)
        elif s == 2:
            ends = (layer_columns, (numeric_back,))
        elif s == 3:
            sends = ((functools.partial(to_layer, up=True), numeric_part[:, 1]),)
        elif s == 5:
            works.append((lambda a, b, c, d: (pick(a, b), pick(c, d)),
                          (block[:, 1], got_block, got_numeric, numeric_part[:, 0])))
        outs = other.step(sends, works, ends, wait=False)
        if s == 1:
            got_block = outs.pop(0)
        elif s == 3:
            got_numeric = outs.pop(0)
        gate_w, cand_w, extra, *outs = outs
        extra = core_swap(extra)
        if s == 2:
            numeric_part, = outs
        elif s == 5:
            block_out, numeric_grad = outs
    cand_w = place_extra(places - 1, places, core_swap(extra), cand_w)
    table, gate_b, cand_b, logit, gain, bias = spare_totals(mine, block_rows, used, mask_logits, feature_allow)
    table = joined(table, core_swap(table), ~first_core)
    table = jnp.swapaxes(table.reshape(columns, embed_width, levels), 1, 2)
    return (block_out, numeric_grad, table, gain, bias, logit,
            gate_w, gate_b, cand_w, cand_b)


def solution(mesh):
    in_specs = (P("dp", None), P("dp", None), P(), P(), P(), P(), P("pipe", None), P("pipe", None),
                P("pipe", None, None), P("pipe", None), P("pipe", None, None), P("pipe", None),
                P("dp", None))
    out_specs = (P("dp", "pipe"), P("dp", "pipe"), P(), P(), P(), P("pipe", None),
                 P("pipe", None, None), P("pipe", None), P("pipe", None, None), P("pipe", None))
    return jax.shard_map(on_device, mesh=mesh, in_specs=in_specs, out_specs=out_specs, check_vma=False)
```

```python
import functools

import jax
import jax.numpy as jnp
from jax import lax
from jax.experimental import pallas as pl
from jax.experimental.pallas import tpu as pltpu
from jax.sharding import PartitionSpec as P

MB = 8
ROWS_MB = 128
BLOCK = 512
EPS = 1e-05
BF = jnp.bfloat16
F32 = jnp.float32


def feature_share(logits, allow):
    allowed = allow > 0
    largest = jnp.max(jnp.where(allowed, logits, -1e30), axis=-1, keepdims=True)
    raised = jnp.where(allowed, jnp.exp(jnp.where(allowed, logits - largest, 0.0)), 0.0)
    return raised / jnp.sum(raised, axis=-1, keepdims=True)


def core_swap(value):
    return lax.ppermute(value, "pipe", [(i, i ^ 1) for i in range(lax.axis_size("pipe"))])


def to_layer(value, up):
    half = lax.axis_size("pipe") // 2
    pairs = [(i, i + half) if up else (i + half, i) for i in range(half)]
    return lax.ppermute(value, "pipe", pairs)


def dp_swap(value, step):
    return lax.ppermute(value, "dp", [(i, i ^ step) for i in range(lax.axis_size("dp"))])


def merged(a, b, held):
    gap = a[0] - b[0]
    return 0.5 * (a[0] + b[0]), a[1] + b[1] + gap * gap * (0.5 * held)


def dp_levels():
    return [1 << i for i in range(lax.axis_size("dp").bit_length() - 1)]


def dp_moments(both, count):
    held = count
    for step in dp_levels()[1:]:
        both = jnp.stack(merged(both, dp_swap(both, step), held))
        held *= 2
    return both


def last_pair(both):
    return both, dp_swap(both, dp_levels()[0])


def last_pair_to_layer(both, up):
    lanes = lax.axis_size("pipe")
    half = lanes // 2
    pairs = []
    for place in range(lax.axis_size("dp")):
        for lane in range(half):
            low, high = lane, lane + half
            start, end = (low, high) if up else (high, low)
            pairs.append((place * lanes + start, (place ^ dp_levels()[0]) * lanes + end))
    return to_layer(both, up), lax.ppermute(both, ("dp", "pipe"), pairs)


def partial_total(value):
    for step in dp_levels()[1:]:
        value = value + dp_swap(value, step)
    return value


def dp_total(value):
    step = 1
    while step < lax.axis_size("dp"):
        value = value + dp_swap(value, step)
        step *= 2
    return value


def plus(a, b):
    return lax.reduce_precision(a.astype(F32) + b.astype(F32), 8, 7).astype(BF)


def halves(value, second):
    mid = value.shape[0] // 2
    a, b = value[:mid], value[mid:]
    return jnp.where(second, b, a), jnp.where(second, a, b)


def joined(kept, got, second):
    return jnp.where(second, jnp.concatenate([got, kept]), jnp.concatenate([kept, got]))


def rounded(value):
    return lax.reduce_precision(value, 8, 7)


def dot(a, b, dims):
    return lax.dot_general(a, b, ((dims[0], dims[1]), ((), ())), preferred_element_type=F32)


def sigmoid(v):
    return 0.5 * jnp.tanh(0.5 * v) + 0.5


def low(v):
    return v.astype(BF).astype(F32)


def nn(a, b):
    return lax.dot_general(a, b, (((1,), (0,)), ((), ())), preferred_element_type=F32)


def nt(a, b):
    return lax.dot_general(a, b, (((1,), (1,)), ((), ())), preferred_element_type=F32)


def column_sum(v):
    return jnp.sum(v, axis=0, keepdims=True)


def batch_rows(i):
    return slice(i * ROWS_MB, (i + 1) * ROWS_MB)


def when_active(layer):
    rank = lax.axis_index("pipe")
    return rank // (lax.axis_size("pipe") // 2) == layer


class Weights:
    def __init__(self, refs, scratch):
        self.own_gate, self.other_gate, self.own_cand, self.other_cand = refs
        self.gate, self.cand, self.sems = scratch
        self.slots = self.gate.shape[0]

    def start(self, k):
        core = lax.axis_index("pipe") % 2
        per_core = self.own_gate.shape[0]
        i, slot = k % per_core, k % self.slots

        def begin(gate, cand):
            pltpu.make_async_copy(gate.at[i], self.gate.at[slot], self.sems.at[0, slot]).start()
            pltpu.make_async_copy(cand.at[i], self.cand.at[slot], self.sems.at[1, slot]).start()

        pl.when(core == k // per_core)(functools.partial(begin, self.own_gate, self.own_cand))
        pl.when(core != k // per_core)(functools.partial(begin, self.other_gate, self.other_cand))

    def wait(self, k):
        slot = k % self.slots
        pltpu.make_async_copy(self.own_gate.at[0], self.gate.at[slot], self.sems.at[0, slot]).wait()
        pltpu.make_async_copy(self.own_cand.at[0], self.cand.at[slot], self.sems.at[1, slot]).wait()


def finish_moments(a, b, moments, held):
    mean, spread = merged(a[...], b[...], held)
    moments[0] = mean
    moments[1] = lax.rsqrt(spread / (2 * held) + EPS)


def normalise(source, moments, affine, x):
    for i in range(source.shape[0] // ROWS_MB):
        at = batch_rows(i)
        xhat = (source[at, :].astype(F32) - moments[0, i : i + 1, :]) * moments[1, i : i + 1, :]
        x[at, :] = xhat * affine[0:1, :] + affine[1:2, :]


def run_forward(x, scales, gate_bias, cand_bias, weights, h, keep=None, after=None):
    rows, width = x.shape
    count = scales.shape[0]
    section = count // 2
    blocks = [slice(i, i + BLOCK) for i in range(0, rows, BLOCK)]

    def spot(k):
        return k if keep else k % 2

    weights.wait(0)
    for at in blocks:
        m = (x[at, :] * scales[0:1, :]).astype(BF)
        zz = sigmoid(nn(m, weights.gate[0, width:, :width]) + gate_bias[0:1, :width])
        cc = jnp.tanh(nn(m, weights.cand[0, width:, :]) + cand_bias[0:1, :])
        h[1, at, :] = zz * cc
        if keep:
            z, r, c, operands = keep
            z[0, at, :], c[0, at, :] = zz, cc
            if operands is not None:
                operands[0, at, width : 2 * width] = m
    if keep:
        after(0)

    def segment(k, _):
        weights.wait(k)
        if keep:
            after.before(k)

        @pl.when(k == section)
        def _():
            x[...] = low(x[...])
            h[spot(k)] = low(h[spot(k)])

        for at in blocks:
            hh = h[spot(k), at, :]
            hb = hh.astype(BF)
            m = (x[at, :] * scales[pl.ds(k, 1), :]).astype(BF)
            both = jnp.concatenate([hb, m], 1)
            bias = gate_bias[pl.ds(k, 1), :]
            rr = sigmoid(nn(both, weights.gate[k, :, width:]) + bias[:, width:])
            zz = sigmoid(nn(both, weights.gate[k, :, :width]) + bias[:, :width])
            rh = (rr * hh).astype(BF)
            cc = jnp.tanh(nn(jnp.concatenate([rh, m], 1), weights.cand[k]) + cand_bias[pl.ds(k, 1), :])
            if keep:
                z[k, at, :], r[k, at, :], c[k, at, :] = zz, rr, cc
                if operands is not None:
                    slot = k % 2
                    operands[slot, at, :width] = hb
                    operands[slot, at, width : 2 * width] = m
                    operands[slot, at, 2 * width :] = rh
            h[spot(k + 1), at, :] = (1.0 - zz) * hh + zz * cc
        if keep:
            after(k)
        return 0

    lax.fori_loop(1, count, segment, 0)


class Out:
    def __init__(self, slotted, sems, kept=(), kept_sems=None):
        self.slotted, self.sems, self.kept, self.kept_sems = slotted, sems, kept, kept_sems

    def slot_copy(self, k):
        source, target = self.slotted
        return pltpu.make_async_copy(source.at[k % 2], target.at[k], self.sems.at[k % 2])

    def kept_copies(self, k):
        return [
            pltpu.make_async_copy(source.at[k], target.at[k], self.kept_sems.at[i, k])
            for i, (source, target) in enumerate(self.kept)
        ]

    def before(self, k):
        if not self.slotted:
            return

        @pl.when(k >= 2)
        def _():
            self.slot_copy(k - 2).wait()

    def __call__(self, k):
        if self.slotted:
            self.slot_copy(k).start()
        for copy in self.kept_copies(k):
            copy.start()

    def finish(self, count):
        if self.slotted:
            self.slot_copy(count - 2).wait()
            self.slot_copy(count - 1).wait()
        if self.kept:
            def wait(k, _):
                for copy in self.kept_copies(k):
                    copy.wait()
                return 0
            lax.fori_loop(0, count, wait, 0)


def run_backward(segments, g, gx, x, scales, weights, states, slots, grads, sums, arrive, done):
    h, z, r, c = states
    rows, width = g.shape
    blocks = [slice(i, i + BLOCK) for i in range(0, rows, BLOCK)]
    high = max(segments)

    def segment(i, _):
        k = high - i
        s = k % slots
        arrive(k)
        totals = None
        for at in blocks:
            gg, hh, zz, rr, cc = g[at, :], h[s, at, :], z[s, at, :], r[s, at, :], c[s, at, :]
            gc = (gg * zz * (1.0 - cc * cc)).astype(BF)
            reset_h = nt(gc, weights.cand[k % weights.slots, :width, :])
            gate_z = (gg * (cc - hh) * zz * (1.0 - zz)).astype(BF)
            gm = nt(gc, weights.cand[k % weights.slots, width:, :])
            gate_r = (reset_h * hh * rr * (1.0 - rr)).astype(BF)
            gates = jnp.concatenate([gate_z, gate_r], 1)
            g[at, :] = gg * (1.0 - zz) + reset_h * rr + nt(gates, weights.gate[k % weights.slots, :width, :])
            gm = gm + nt(gates, weights.gate[k % weights.slots, width:, :])
            gx[at, :] = gx[at, :] + gm * scales[pl.ds(k, 1), :]
            grads[k % 2, at, : 2 * width] = gates
            grads[k % 2, at, 2 * width :] = gc
            part = jnp.concatenate([column_sum(gates.astype(F32)), column_sum(gc.astype(F32)),
                                    column_sum(gm * x[at, :])], 1)
            totals = part if totals is None else totals + part
            done.stage(k, at, lambda: ((x[at, :] * scales[pl.ds(k, 1), :]).astype(BF), hh.astype(BF),
                                       (rr * hh).astype(BF)))
        sums[pl.ds(k, 1), :] = totals
        done(k)
        return 0

    full = [k for k in segments if k > 0]
    lax.fori_loop(0, len(full), segment, 0)
    if min(segments) == 0:
        arrive(0)
        totals = None
        for at in blocks:
            gg, zz, cc = g[at, :], z[0, at, :], c[0, at, :]
            gc = (gg * zz * (1.0 - cc * cc)).astype(BF)
            gate_z = (gg * cc * zz * (1.0 - zz)).astype(BF)
            gm = nt(gc, weights.cand[0, width:, :]) + nt(gate_z, weights.gate[0, width:, :width])
            gx[at, :] = gx[at, :] + gm * scales[0:1, :]
            grads[0, at, :width] = gate_z
            grads[0, at, width : 2 * width] = gc
            part = jnp.concatenate([column_sum(gate_z.astype(F32)), jnp.zeros((1, width), F32),
                                    column_sum(gc.astype(F32)), column_sum(gm * x[at, :])], 1)
            totals = part if totals is None else totals + part
            done.stage(0, at, lambda: ((x[at, :] * scales[0:1, :]).astype(BF),))
        sums[0:1, :] = totals
        done.first()


def tn(a, b):
    return lax.dot_general(a, b, (((0,), (0,)), ((), ())), preferred_element_type=F32)


class Terms:
    def __init__(self, count, operands, grads, made, sems, arrays, after=None):
        self.hidden = 1 - lax.axis_index("pipe") % 2
        self.count, self.operands, self.grads, self.made, self.sems = count, operands, grads, made, sems
        self.arrays, self.after = arrays, after
        self.width = operands.shape[-1] // 3

    def slot(self, k):
        return (self.count - 1 - k) % 2

    def copies(self, k):
        w, part, slot = self.width, self.arrays[0][0].shape[1], self.slot(k)
        start, size = (self.count - 1 - k) * 3 * w, w if k == 0 else 3 * w
        cuts = [(0, start, size)]
        if start < part < start + size:
            cuts = [(0, start, part - start), (part - start, part, start + size - part)]
        return [pltpu.make_async_copy(self.made.at[slot, i, :, pl.ds(at, n)],
                                      self.arrays[i][to // part].at[:, pl.ds(to % part, n)], self.sems.at[slot, i, j])
                for i in range(2) for j, (at, to, n) in enumerate(cuts)]

    def each(self, k, function):
        if isinstance(k, int):
            function(k)
            return
        for known in range(1, self.count):
            pl.when(k == known)(functools.partial(function, known))

    def start(self, k):
        for copy in self.copies(k):
            copy.start()

    def wait(self, k):
        if k < self.count:
            for copy in self.copies(k):
                copy.wait()

    def stage(self, k, at, operands):
        m, *others = operands()
        w = self.width
        self.operands[0, at, w : 2 * w] = m
        if others:
            self.operands[0, at, :w] = others[0]
            self.operands[0, at, 2 * w :] = others[1]

    def __call__(self, k, operands=None, grads=None):
        w = self.width
        operands = self.operands.at[0] if operands is None else operands
        grads = self.grads.at[k % 2] if grads is None else grads
        self.each(k, lambda k: self.wait(k + 2))
        made = self.made.at[self.slot(k)]
        made[self.hidden, :, : 2 * w] = tn(operands[:, :w], grads[:, : 2 * w]).astype(BF)
        made[self.hidden, :, 2 * w :] = tn(operands[:, 2 * w :], grads[:, 2 * w :]).astype(BF)
        made[1 - self.hidden] = tn(operands[:, w : 2 * w], grads[...]).astype(BF)
        self.each(k, self.start)
        if self.after:
            self.after(k)

    def first(self, operands=None, grads=None):
        w = self.width
        operands = self.operands.at[0] if operands is None else operands
        grads = self.grads.at[0] if grads is None else grads
        self.wait(2)
        made = self.made.at[self.slot(0)]
        made[self.hidden, :, :w] = tn(operands[:, w : 2 * w], grads[:, :w]).astype(BF)
        made[1 - self.hidden, :, :w] = tn(operands[:, w : 2 * w], grads[:, w : 2 * w]).astype(BF)
        self.start(0)
        self.wait(1)
        self.wait(0)


def terms_from_hbm(terms, operands_in, grads_in, sems):
    count = terms.count

    def copies(k):
        slot = k % 2
        return [pltpu.make_async_copy(x.at[k], y.at[slot], sems.at[slot, j])
                for j, (x, y) in enumerate(((operands_in, terms.operands), (grads_in, terms.grads)))]

    for copy in copies(count - 1):
        copy.start()

    def segment(i, _):
        k = count - 1 - i
        for copy in copies(k - 1):
            copy.start()
        for copy in copies(k):
            copy.wait()
        terms(k, terms.operands.at[k % 2], terms.grads.at[k % 2])
        return 0

    lax.fori_loop(0, count - 1, segment, 0)
    for copy in copies(0):
        copy.wait()
    terms.first()


def norm_sums(gx, xhat_of, sums):
    for i in range(gx.shape[0] // ROWS_MB):
        part = gx[batch_rows(i), :]
        sums[0, i : i + 1, :] = column_sum(part)
        sums[1, i : i + 1, :] = column_sum(part * xhat_of(i))


def xhat_rows(source, moments, i):
    return (source[batch_rows(i), :].astype(F32) - moments[0, i : i + 1, :]) * moments[1, i : i + 1, :]


ANY = pl.BlockSpec(memory_space=pl.ANY)
VM = pl.BlockSpec(memory_space=pltpu.VMEM)
LIMIT = 62 * 1024 * 1024


def layer_cost(segments, rows, width, passes):
    return pl.CostEstimate(flops=segments * passes * rows * 12 * width * width, transcendentals=0,
                           bytes_accessed=segments * (12 * width * width + 16 * rows * width))


def layer1_forward(source, moments, affine, scales, gate_bias, cand_bias, weights, keep):
    rows, width = source.shape
    count = scales.shape[0]

    dp_half = ROWS_MB * lax.axis_size("dp") // 2

    def kernel(*refs):
        if keep:
            source, moments = refs[:2]
            refs = refs[2:]
        else:
            source, first_half, second_half = refs[:3]
            refs = refs[3:]
        affine, scales, gate_bias, cand_bias, w0, w1, w2, w3 = refs[:8]
        refs = refs[8:]
        if keep:
            kept_h, kept_z, kept_r, kept_c = refs[:4]
            x, gate, cand, wsems, h, z, r, c, ksems = refs[4:]
        else:
            last, local, moments = refs[:3]
            x, gate, cand, wsems, h = refs[3:]

        @pl.when(when_active(0))
        def _():
            held = Weights((w0, w1, w2, w3), (gate, cand, wsems))
            for k in range(count):
                held.start(k)
            if not keep:
                finish_moments(first_half, second_half, moments, dp_half)
            normalise(source, moments, affine.at[0], x)
            if keep:
                out = Out(None, None, ((h, kept_h), (z, kept_z), (r, kept_r), (c, kept_c)), ksems)
                run_forward(x, scales, gate_bias, cand_bias, held, h, (z, r, c, None), out)
                out.finish(count)
                return
            run_forward(x, scales, gate_bias, cand_bias, held, h)
            final = h.at[count % 2]
            last[...] = final[...].astype(BF)
            for i in range(rows // ROWS_MB):
                part = low(final[batch_rows(i), :])
                mean = column_sum(part) * (1.0 / ROWS_MB)
                local[0, i : i + 1, :] = mean
                local[1, i : i + 1, :] = column_sum((part - mean) * (part - mean))

    state = jax.ShapeDtypeStruct((count, rows, width), F32)
    by_batch = jax.ShapeDtypeStruct((2, rows // ROWS_MB, width), F32)
    scratch = [pltpu.VMEM((rows, width), F32),
               pltpu.VMEM((count, 2 * width, 2 * width), BF),
               pltpu.VMEM((count, 2 * width, width), BF),
               pltpu.SemaphoreType.DMA((2, count))]
    if keep:
        out_shape = (state,) * 4
        out_specs = (ANY,) * 4
        scratch += [pltpu.VMEM((count + 1, rows, width), F32)] + [pltpu.VMEM((count, rows, width), F32)] * 3
        scratch += [pltpu.SemaphoreType.DMA((4, count))]
    else:
        out_shape = (jax.ShapeDtypeStruct((rows, width), BF), by_batch, by_batch)
        out_specs = (VM, VM, VM)
        scratch += [pltpu.VMEM((2, rows, width), F32)]
    args = (source,) + (moments if isinstance(moments, tuple) else (moments,))
    args += (affine, scales, gate_bias, cand_bias)
    return pl.pallas_call(
        kernel,
        out_shape=out_shape,
        in_specs=[VM] * len(args) + [ANY] * 4,
        out_specs=out_specs,
        scratch_shapes=scratch,
        compiler_params=pltpu.CompilerParams(vmem_limit_bytes=LIMIT),
        cost_estimate=layer_cost(count, rows, width, 1),
        name="layer1_states" if keep else "layer1_forward",
    )(*args, *weights)


def layer2_both(source, halves_of_moments, affine, scales, gate_bias, cand_bias, weights, cotangent):
    rows, width = source.shape
    count = scales.shape[0]

    dp_half = ROWS_MB * lax.axis_size("dp") // 2

    def kernel(source, first_half, second_half, affine, scales, gate_bias, cand_bias, w0, w1, w2, w3, cotangent,
               last, gx_out, nsums, sums, operands_out, grads_out,
               x, gate, cand, wsems, h, z, r, c, operands, osems, g, gx, gsem, moments):
        @pl.when(when_active(1))
        def _():
            held = Weights((w0, w1, w2, w3), (gate, cand, wsems))
            for k in range(count):
                held.start(k)
            core = lax.axis_index("pipe") % 2
            first = pl.multiple_of(core * rows, rows)
            load_g = pltpu.make_async_copy(cotangent.at[pl.ds(first, rows), :], g, gsem.at[0])
            load_g.start()
            finish_moments(first_half, second_half, moments, dp_half)
            normalise(source, moments, affine.at[1], x)
            out = Out((operands, operands_out), osems)
            run_forward(x, scales, gate_bias, cand_bias, held, h, (z, r, c, operands), out)
            last[...] = h[count]
            out.finish(count)
            load_g.wait()
            gx[...] = jnp.zeros_like(gx)

            section = count // 2

            class Left:
                def stage(self, k, at, operands):
                    pass

                def copy(self, k):
                    return pltpu.make_async_copy(operands.at[k % 2], grads_out.at[k], osems.at[k % 2])

                def __call__(self, k):
                    self.copy(k).start()

                def first(self):
                    self.copy(0).start()
                    self.copy(1).wait()
                    self.copy(0).wait()

            left = Left()

            def free(k):
                @pl.when(k <= count - 3)
                def _():
                    left.copy(k + 2).wait()

            run_backward(range(section, count), g, gx, x, scales, held, (h, z, r, c), count, operands, sums, free, left)
            g[...] = low(g[...])
            gx[...] = low(gx[...])
            normalise(source, moments, affine.at[1], x)
            run_backward(range(section), g, gx, x, scales, held, (h, z, r, c), count, operands, sums, free, left)
            gx_out[...] = gx[...].astype(BF)
            norm_sums(gx, lambda i: xhat_rows(source, moments, i), nsums)

    state = pltpu.VMEM((count, rows, width), F32)
    left_out = jax.ShapeDtypeStruct((count, rows, 3 * width), BF)
    return pl.pallas_call(
        kernel,
        out_shape=(jax.ShapeDtypeStruct((rows, width), F32),
                   jax.ShapeDtypeStruct((rows, width), BF),
                   jax.ShapeDtypeStruct((2, rows // ROWS_MB, width), F32),
                   jax.ShapeDtypeStruct((count, 4 * width), F32),
                   left_out, left_out),
        in_specs=[VM] * 7 + [ANY] * 5,
        out_specs=(VM, VM, VM, VM, ANY, ANY),
        scratch_shapes=[pltpu.VMEM((rows, width), F32),
                        pltpu.VMEM((count, 2 * width, 2 * width), BF),
                        pltpu.VMEM((count, 2 * width, width), BF),
                        pltpu.SemaphoreType.DMA((2, count)),
                        pltpu.VMEM((count + 1, rows, width), F32), state, state, state,
                        pltpu.VMEM((2, rows, 3 * width), BF),
                        pltpu.SemaphoreType.DMA((2,)),
                        pltpu.VMEM((rows, width), F32),
                        pltpu.VMEM((rows, width), F32),
                        pltpu.SemaphoreType.DMA((1,)),
                        pltpu.VMEM((2, rows // ROWS_MB, width), F32)],
        compiler_params=pltpu.CompilerParams(vmem_limit_bytes=LIMIT),
        cost_estimate=layer_cost(count, rows, width, 2),
        name="layer2_both",
    )(source, *halves_of_moments, affine, scales, gate_bias, cand_bias, *weights, cotangent)


def layer1_backward(carried, source, moments, affine, scales, weights, kept, operands, grads):
    rows, width = source.shape
    count = scales.shape[0]
    section = count // 2
    slots = 3
    counted = ROWS_MB * lax.axis_size("dp")
    part = (3 * count - 2) * width // 2

    def kernel(gxr, hb, moments2, total_a, total_b, source, moments, affine, scales, w0, w1, w2, w3,
               kept_h, kept_z, kept_r, kept_c, operands_in, grads_in,
               gx, nsums, sums, sent_a, sent_b, mine_a, mine_b,
               x, gate, cand, wsems, h, z, r, c, ksems, g, loaded, staged, lsems, made, msems):
        held = Weights((w0, w1, w2, w3), (gate, cand, wsems))
        states = ((kept_h, h), (kept_z, z), (kept_r, r), (kept_c, c))

        def copies(k):
            return [pltpu.make_async_copy(x.at[k], y.at[k % slots], ksems.at[i, k % slots])
                    for i, (x, y) in enumerate(states)]

        def arrive(k):
            held.wait(k)
            for copy in copies(k):
                copy.wait()

        def load(k):
            for copy in copies(k):
                copy.start()
            held.start(k)

        def after(k):
            @pl.when(k >= slots)
            def _():
                load(k - slots)

        terms = Terms(count, staged, loaded, made, msems, ((sent_a, sent_b), (mine_a, mine_b)), after)

        @pl.when(when_active(1))
        def _():
            terms.after = None
            terms_from_hbm(terms, operands_in, grads_in, lsems)

        @pl.when(when_active(0))
        def _():
            terms.after = after
            for k in range(count - 1, count - 1 - slots, -1):
                load(k)
            normalise(source, moments, affine.at[0], x)
            x[...] = low(x[...])
            for i in range(rows // ROWS_MB):
                at = batch_rows(i)
                mean_g, mean_gx = [(total_a[j, i : i + 1, :] + total_b[j, i : i + 1, :]) / counted for j in (0, 1)]
                back = gxr[at, :].astype(F32) - mean_g - xhat_rows(hb, moments2, i) * mean_gx
                g[at, :] = low(affine[1, 0:1, :] * moments2[1, i : i + 1, :] * back)
            gx[...] = jnp.zeros_like(gx)
            run_backward(range(section, count), g, gx, x, scales, held, (h, z, r, c), slots, loaded, sums, arrive, terms)
            g[...] = low(g[...])
            gx[...] = low(gx[...])
            normalise(source, moments, affine.at[0], x)
            run_backward(range(section), g, gx, x, scales, held, (h, z, r, c), slots, loaded, sums, arrive, terms)
            norm_sums(gx, lambda i: xhat_rows(source, moments, i), nsums)

    state = pltpu.VMEM((slots, rows, width), F32)
    terms = jax.ShapeDtypeStruct((width, part), BF)
    args = [*carried, source, moments, affine, scales, *weights, *kept, operands, grads]
    return pl.pallas_call(
        kernel,
        out_shape=(jax.ShapeDtypeStruct((rows, width), F32),
                   jax.ShapeDtypeStruct((2, rows // ROWS_MB, width), F32),
                   jax.ShapeDtypeStruct((count, 4 * width), F32), terms, terms, terms, terms),
        in_specs=[VM] * 9 + [ANY] * 10,
        out_specs=(VM,) * 3 + (ANY,) * 4,
        scratch_shapes=[pltpu.VMEM((rows, width), F32),
                        pltpu.VMEM((slots, 2 * width, 2 * width), BF),
                        pltpu.VMEM((slots, 2 * width, width), BF),
                        pltpu.SemaphoreType.DMA((2, slots)),
                        state, state, state, state,
                        pltpu.SemaphoreType.DMA((4, slots)),
                        pltpu.VMEM((rows, width), F32),
                        pltpu.VMEM((2, rows, 3 * width), BF),
                        pltpu.VMEM((2, rows, 3 * width), BF),
                        pltpu.SemaphoreType.DMA((2, 2)),
                        pltpu.VMEM((2, 2, width, 3 * width), BF),
                        pltpu.SemaphoreType.DMA((2, 2, 2))],
        compiler_params=pltpu.CompilerParams(vmem_limit_bytes=LIMIT),
        cost_estimate=layer_cost(count, rows, width, 2),
        name="layer1_backward",
    )(*args)


def hot_rows(cats, c, levels):
    level = lax.broadcasted_iota(jnp.int32, (levels, cats.shape[1]), 0)
    return jnp.where(cats[c : c + 1, :] == level, 1.0, 0.0).astype(BF)


def load_columns(categories, cats, sem, rows):
    first = pl.multiple_of((lax.axis_index("pipe") % 2) * rows, rows)
    return pltpu.make_async_copy(categories.at[:, pl.ds(first, rows)], cats, sem)


def embed(numeric, categories, table, rows, own, other, affine):
    numeric_width, columns = numeric.shape[1], categories.shape[0]
    embedded, levels = table.shape
    each = embedded // columns
    packed = 128 // each
    width = numeric_width + embedded

    half = own[0].shape[0]

    def kernel(numeric, categories, table, *refs):
        own, other, (bn_gain, bn_bias) = refs[:4], refs[4:8], refs[8:10]
        source, local, scales, gate_bias, cand_bias, affine, cats, nums, sems = refs[10:]
        core = lax.axis_index("pipe") % 2

        def put(logits, allow, gates, cands, at):
            scales[at : at + half, :] = width * feature_share(logits[...], allow[...])
            gate_bias[at : at + half, :] = gates[...]
            cand_bias[at : at + half, :] = cands[...]

        for at, owner in ((0, 0), (half, 1)):
            pl.when(core == owner)(functools.partial(put, *own, at))
            pl.when(core != owner)(functools.partial(put, *other, at))
        for layer in range(2):
            affine[layer, 0:1, :] = bn_gain[layer : layer + 1, :]
            affine[layer, 1:2, :] = bn_bias[layer : layer + 1, :]
        first = pl.multiple_of((lax.axis_index("pipe") % 2) * rows, rows)
        load = load_columns(categories, cats, sems.at[0], rows)
        load_numeric = pltpu.make_async_copy(numeric.at[pl.ds(first, rows), :], nums, sems.at[1])
        load.start()
        load_numeric.start()
        load.wait()
        row = lax.broadcasted_iota(jnp.int32, (128, levels), 0) // each
        for group in range(columns // packed):
            part = table[group * 128 : (group + 1) * 128, :]
            weights = jnp.concatenate([jnp.where(row == i, part, jnp.zeros_like(part)) for i in range(packed)], 1)
            hot = jnp.concatenate([hot_rows(cats, group * packed + i, levels) for i in range(packed)], 0)
            start = numeric_width + group * 128
            source[:, start : start + 128] = nn(weights, hot).T
        load_numeric.wait()
        source[:, :numeric_width] = nums[...]
        for i in range(rows // ROWS_MB):
            part = source[batch_rows(i), :]
            mean = column_sum(part) * (1.0 / ROWS_MB)
            local[0, i : i + 1, :] = mean
            local[1, i : i + 1, :] = column_sum((part - mean) * (part - mean))

    return pl.pallas_call(
        kernel,
        out_shape=(jax.ShapeDtypeStruct((rows, width), F32),
                   jax.ShapeDtypeStruct((2, rows // ROWS_MB, width), F32),
                   jax.ShapeDtypeStruct((2 * half, width), F32),
                   jax.ShapeDtypeStruct((2 * half, 2 * width), F32),
                   jax.ShapeDtypeStruct((2 * half, width), F32),
                   jax.ShapeDtypeStruct((2, 2, width), F32)),
        in_specs=[ANY, ANY] + [VM] * 11,
        out_specs=(VM,) * 6,
        scratch_shapes=[pltpu.VMEM((columns, rows), jnp.int32), pltpu.VMEM((rows, numeric_width), F32),
                        pltpu.SemaphoreType.DMA((2,))],
        compiler_params=pltpu.CompilerParams(vmem_limit_bytes=LIMIT),
        cost_estimate=pl.CostEstimate(flops=8 * rows * width * levels, transcendentals=0, bytes_accessed=8 * rows * width),
        name="embed",
    )(numeric, categories, table, *own, *other, *affine)


def feature_grads(gx, source, moments, totals, gain, categories, table_shape):
    rows, width = gx.shape
    embedded, levels = table_shape
    columns = categories.shape[0]
    each = embedded // columns
    numeric_width = width - embedded
    half = columns // 2

    def kernel(gx, source, moments, totals, gain, categories, numeric, sent, mine, cats, back, table, sem):
        load = load_columns(categories, cats, sem.at[0], rows)
        load.start()
        for i in range(rows // ROWS_MB):
            at = batch_rows(i)
            part = gx[at, :] - totals[0, i : i + 1, :] - xhat_rows(source, moments, i) * totals[1, i : i + 1, :]
            back[at, :] = gain[...] * moments[1, i : i + 1, :] * part
        numeric[...] = back[:, :numeric_width]
        load.wait()
        table[...] = jnp.zeros_like(table)
        for group in range(embedded // 128):
            start = numeric_width + group * 128
            grads = back[:, start : start + 128].astype(BF)
            lane = lax.broadcasted_iota(jnp.int32, (levels, 128), 1) // each
            blocks = jnp.zeros((levels, 128), F32)
            for i in range(128 // each):
                c = group * (128 // each) + i
                blocks = jnp.where(lane == i, nn(hot_rows(cats, c, levels), grads), blocks)
            turned = blocks.T
            for i in range(128 // each):
                c = group * (128 // each) + i
                for e in range(each):
                    at = i * each + e
                    table[c // half, c % half : c % half + 1, e * levels : (e + 1) * levels] = turned[at : at + 1, :]
        core = lax.axis_index("pipe") % 2
        sent[...] = table[1 - core].astype(BF)
        mine[...] = table[core].astype(BF)

    part = jax.ShapeDtypeStruct((16, each * levels), BF)
    return pl.pallas_call(
        kernel,
        out_shape=(jax.ShapeDtypeStruct((rows, numeric_width), F32), part, part),
        in_specs=[VM] * 5 + [ANY],
        out_specs=(VM, VM, VM),
        scratch_shapes=[pltpu.VMEM((columns, rows), jnp.int32), pltpu.VMEM((rows, width), F32),
                        pltpu.VMEM((2, 16, each * levels), F32), pltpu.SemaphoreType.DMA((1,))],
        compiler_params=pltpu.CompilerParams(vmem_limit_bytes=LIMIT),
        cost_estimate=pl.CostEstimate(flops=8 * rows * width * levels, transcendentals=0, bytes_accessed=16 * rows * width),
        name="feature_grads",
    )(gx, source, moments, totals, gain, categories)


def spare_totals(pieces, rows, used, logits, allow):
    count = len(pieces)
    spare, columns = pieces[0].shape[0] - rows, pieces[0].shape[1]
    half, width = logits.shape

    def kernel(logits, allow, *refs):
        pieces, (table, gate_b, cand_b, logit, gain, bias, parts, sems) = refs[:count], refs[count:]
        copies = [pltpu.make_async_copy(piece.at[pl.ds(rows, spare), :], parts.at[i], sems.at[i])
                  for i, piece in enumerate(pieces)]
        for copy in copies:
            copy.start()
        shares = feature_share(logits[...], allow[...])
        for copy in copies:
            copy.wait()
        spot = ring_place(count)
        added = jnp.zeros((spare, columns), F32)
        for place in range(count):
            added = added + parts[lax.rem(spot - place + count, count)].astype(F32)
        table[...] = added[:used, :]
        small = added[used:, : columns // 2] + added[used:, columns // 2 :]
        gate_b[...] = small[:half, : 2 * width]
        cand_b[...] = small[:half, 2 * width : 3 * width]
        scaled = width * small[:half, 3 * width :]
        logit[...] = shares * (scaled - jnp.sum(shares * scaled, axis=-1, keepdims=True))
        for layer in range(2):
            at = layer * width
            bias[layer : layer + 1, :] = small[half : half + 1, at : at + width]
            gain[layer : layer + 1, :] = small[half : half + 1, 2 * width + at : 3 * width + at]

    def out(*shape):
        return jax.ShapeDtypeStruct(shape, F32)

    return pl.pallas_call(
        kernel,
        out_shape=(out(used, columns), out(half, 2 * width), out(half, width), out(half, width), out(2, width),
                   out(2, width)),
        in_specs=[VM, VM] + [ANY] * count,
        out_specs=(VM,) * 6,
        scratch_shapes=[pltpu.VMEM((count, spare, columns), BF), pltpu.SemaphoreType.DMA((count,))],
        compiler_params=pltpu.CompilerParams(vmem_limit_bytes=LIMIT),
        name="spare_totals",
    )(logits, allow, *pieces)


def ring_place(places):
    place = lax.axis_index("dp")
    spot = jnp.where(place % 2 == 0, place // 2, places - 1 - place // 2)
    return jnp.where(lax.axis_index("pipe") % 2 == 0, spot, places - 1 - spot)


def blank_outputs(per_core, width):
    def kernel(gate, cand, zeros, sems):
        @pl.when(lax.axis_index("pipe") % 2 == 0)
        def _():
            zeros[...] = jnp.zeros_like(zeros)
            copies = [
                pltpu.make_async_copy(zeros, gate.at[0, pl.ds(0, width), :], sems.at[0]),
                pltpu.make_async_copy(zeros.at[:, pl.ds(0, width)],
                                      gate.at[0, pl.ds(width, width), pl.ds(width, width)], sems.at[1]),
                pltpu.make_async_copy(zeros.at[:, pl.ds(0, width)], cand.at[0, pl.ds(0, width), :], sems.at[2])]
            for copy in copies:
                copy.start()
            for copy in copies:
                copy.wait()

    return pl.pallas_call(
        kernel,
        out_shape=(jax.ShapeDtypeStruct((per_core, 2 * width, 2 * width), F32),
                   jax.ShapeDtypeStruct((per_core, 2 * width, width), F32)),
        out_specs=(ANY, ANY),
        scratch_shapes=[pltpu.VMEM((width, 2 * width), F32), pltpu.SemaphoreType.DMA((3,))],
        name="blank_outputs",
    )()


def place_block(step, blocks, mine, other, extra, gate, cand):
    rows, columns = other.shape
    per_core, width = gate.shape[0], cand.shape[2]
    given = () if extra is None else (extra,)

    def kernel(*refs):
        mine, other = refs[:2]
        extra = refs[2] if given else None
        gate, cand, onward, full, tail, sems = refs[4 + len(given) :]
        spot = ring_place(blocks)
        copies = []

        def copy(source, target, j, row, size):
            copies.append(pltpu.make_async_copy(
                source, target.at[j, pl.ds(row, rows), pl.ds(0, size)], sems.at[len(copies)]))
            copies[-1].start()

        def at(block):
            return pl.multiple_of(block * rows, rows)

        def put(own_half, first_layer):
            del copies[:]
            own_block = lax.rem(spot + 1 - step + blocks, blocks)
            other_block = lax.rem(2 * blocks - spot + step, blocks)
            if not first_layer and given:
                put_extra(spot, step - 1, blocks, extra, tail, cand, copies, sems)
            for piece, half, block in ((mine, own_half, own_block), (other, 1 - own_half, other_block)):
                full[half] = piece[:rows, :].astype(F32)
                for j in range(per_core):
                    start = (per_core - 1 - j) * 3 * width + (width if first_layer else 0)
                    source = full.at[half]
                    if first_layer and j == 0:
                        copy(source.at[:, pl.ds(start, width)], cand if half else gate, 0, width + at(block), width)
                        continue
                    copy(source.at[:, pl.ds(start, 2 * width)], gate, j, half * width + at(block), 2 * width)
                    if j or first_layer:
                        copy(source.at[:, pl.ds(start + 2 * width, width)], cand, j, half * width + at(block), width)
            if first_layer:
                onward[:rows, :] = mine[:rows, :width]
                onward[rows:, :] = other[:, :width]
            for item in copies:
                item.wait()

        core = lax.axis_index("pipe") % 2
        pl.when(core == 0)(functools.partial(put, 0, True))
        pl.when(core == 1)(functools.partial(put, 1, False))

    args = (mine, other, *given, gate, cand)
    return pl.pallas_call(
        kernel,
        out_shape=(jax.ShapeDtypeStruct(gate.shape, F32), jax.ShapeDtypeStruct(cand.shape, F32),
                   jax.ShapeDtypeStruct((2 * rows, width), BF)),
        in_specs=[VM] * (len(args) - 2) + [ANY] * 2,
        out_specs=(ANY, ANY, VM),
        input_output_aliases={len(args) - 2: 0, len(args) - 1: 1},
        scratch_shapes=[pltpu.VMEM((2, rows, columns), F32), pltpu.VMEM((2, rows, width), F32),
                        pltpu.SemaphoreType.DMA((4 * per_core,))],
        compiler_params=pltpu.CompilerParams(vmem_limit_bytes=LIMIT),
        name=f"place_block_{step}",
    )(*args)


def put_extra(spot, step, blocks, extra, tail, cand, copies, sems):
    rows, width = tail.shape[1:]
    for half, block in ((0, lax.rem(2 * blocks - spot - step, blocks)), (1, lax.rem(spot + 1 + step, blocks))):
        tail[half] = extra[half * rows : (half + 1) * rows, :].astype(F32)
        row = half * width + pl.multiple_of(block * rows, rows)
        copies.append(pltpu.make_async_copy(tail.at[half], cand.at[0, pl.ds(row, rows), :], sems.at[len(copies)]))
        copies[-1].start()


def place_extra(step, blocks, extra, cand):
    width = cand.shape[2]
    rows = extra.shape[0] // 2

    def kernel(extra, unused, cand, tail, sems):
        @pl.when(lax.axis_index("pipe") % 2 == 1)
        def _():
            copies = []
            put_extra(ring_place(blocks), step, blocks, extra, tail, cand, copies, sems)
            for item in copies:
                item.wait()

    return pl.pallas_call(
        kernel,
        out_shape=jax.ShapeDtypeStruct(cand.shape, F32),
        in_specs=[VM, ANY],
        out_specs=ANY,
        input_output_aliases={1: 0},
        scratch_shapes=[pltpu.VMEM((2, rows, width), F32), pltpu.SemaphoreType.DMA((2,))],
        compiler_params=pltpu.CompilerParams(vmem_limit_bytes=LIMIT),
        name="place_extra",
    )(extra, cand)


def tied(*values):
    return lax.optimization_barrier(values)


class Ring:
    def __init__(self, parts=None, held=None, unit=None, turn=None):
        self.turn = turn
        self.unit = unit
        self.places = lax.axis_size("dp")
        order = list(range(0, self.places, 2)) + list(range(1, self.places, 2))[::-1]
        lanes = lax.axis_size("pipe")
        self.pairs = []
        for lane in range(lanes):
            way = order if lane % 2 == 0 else order[::-1]
            self.pairs += [(way[i] * lanes + lane, way[(i + 1) % self.places] * lanes + lane)
                           for i in range(self.places)]
        self.spot = ring_place(self.places)
        self.parts = ()
        self.done = 0
        self.held = held
        if held is None:
            mine, received, first = parts
            self.rows = mine.shape[0] // self.places
            self.parts = (mine, received)
            self.held = (self.rows_of(mine, self.spot).astype(F32) + first.astype(F32)).astype(BF)

    def rows_of(self, part, number):
        at = lax.rem(number + self.places, self.places) * self.rows
        return lax.dynamic_slice_in_dim(part, at, self.rows, 0)

    def block(self, number):
        a, b = [self.rows_of(part, number) for part in self.parts]
        return a.astype(F32) + b.astype(F32)

    def step(self, sends=(), work=None, ends=None, wait=True):
        self.done += 1
        sent = len(sends)
        works = work if isinstance(work, list) else [work] if work else []
        held, *values = tied(self.held, *[value for _, value in sends], *[value for _, given in works for value in given])
        got = lax.ppermute(held, ("dp", "pipe"), self.pairs)
        given = [send(value) for (send, _), value in zip(sends, values)]
        outs, values = [], values[sent:]
        for function, arguments in works + ([ends] if ends else []):
            if function is not (ends or [None])[0]:
                arguments, values = values[: len(arguments)], values[len(arguments) :]
            result = function(*arguments)
            outs += list(result) if isinstance(result, (tuple, list)) else [result]
        if self.turn is not None:
            got, *_ = tied(got, *self.turn)
            self.turn[:] = [got]
        got, *outs = tied(got, *outs, *(given if wait else ()))
        if wait:
            given, outs = outs[len(outs) - sent :], outs[: len(outs) - sent]
        if self.unit is not None and self.done < self.places - 1:
            got = got * self.unit
        if self.parts:
            got = (self.block(self.spot - self.done) + got.astype(F32)).astype(BF)
        self.held = got
        return list(given) + outs


def on_device(numeric, categories, cardinalities, embed_table, bn_gain, bn_bias, mask_logits,
              feature_allow, gate_weight, gate_bias, cand_weight, cand_bias, out_grad):
    rank = lax.axis_index("pipe")
    core = rank % 2
    first_core = core == 0
    top = rank >= lax.axis_size("pipe") // 2
    width = out_grad.shape[1]
    numeric_width = numeric.shape[1]
    columns, levels, embed_width = embed_table.shape
    batches = MB // 2
    rows = batches * ROWS_MB
    counted = ROWS_MB * lax.axis_size("dp")

    def my_rows(array):
        return lax.dynamic_slice_in_dim(array, core * rows, rows, 0)

    def by_batch(array):
        return array.reshape(batches, ROWS_MB, array.shape[-1])

    half = gate_weight.shape[0]
    count = 2 * half
    flat_table = jnp.swapaxes(embed_table, 1, 2).reshape(columns * embed_width, levels)
    category_columns = categories.T
    own_small = (mask_logits, feature_allow, gate_bias, cand_bias)
    other_small = tuple(core_swap(value) for value in own_small)
    *other_small, own_gate, own_cand = tied(*other_small, gate_weight, cand_weight)
    weights = (gate_weight, core_swap(own_gate), cand_weight, core_swap(own_cand))
    source1, local1, scales, gate_b, cand_b, affine = embed(
        numeric, category_columns, flat_table, rows, own_small, other_small, (bn_gain, bn_bias))
    h1, local2, moments1 = layer1_forward(
        source1, last_pair(dp_moments(local1, ROWS_MB)), affine, scales, gate_b, cand_b, weights, False)
    source2 = to_layer(h1, True)
    local2 = dp_moments(local2, ROWS_MB)
    halves2 = last_pair_to_layer(local2, True)
    local2, source1 = lax.optimization_barrier((local2, source1))
    kept_states = layer1_forward(source1, moments1, affine, scales, gate_b, cand_b, weights, True)
    mean2, spread2 = merged(*last_pair(local2), counted // 2)
    moments2 = jnp.stack([mean2, lax.rsqrt(spread2 / counted + EPS)])
    h2, gx2, nsums2, sums2, operands, grads = layer2_both(
        source2, halves2, affine, scales, gate_b, cand_b, weights, out_grad)
    received = to_layer(gx2, False)
    totals2 = last_pair_to_layer(partial_total(nsums2), False)

    def layer_columns(value):
        share = value.shape[1] // 4
        pieces = value.reshape(rows, 2, 2, share)
        kept = jnp.where(first_core, pieces[:, :, 0], pieces[:, :, 1])
        got = core_swap(jnp.where(first_core, pieces[:, :, 1], pieces[:, :, 0]))
        both = jnp.where(first_core, jnp.stack([kept, got]), jnp.stack([got, kept]))
        return both.reshape(2 * rows, 2, share)

    def pick(a, b):
        return jnp.where(top, a, b)

    gx1, nsums1, sums1, sent_a, sent_b, mine_a, mine_b = layer1_backward(
        (received, h1, moments2, *totals2), source1, moments1, affine, scales, weights, kept_states, operands, grads)
    places = lax.axis_size("dp")

    def first_block(sent):
        rows = sent.shape[0] // places
        return core_swap(lax.dynamic_slice_in_dim(sent, (places - 1 - ring_place(places)) * rows, rows, 0))

    first_a, first_b = first_block(sent_a), first_block(sent_b)
    first_a, first_b, sent_a, sent_b = tied(first_a, first_b, sent_a, sent_b)
    upper = Ring((mine_a, core_swap(sent_a), first_a))
    lower = Ring((mine_b, core_swap(sent_b), first_b))
    pipes = lax.axis_size("pipe")

    levels_of_dp = [1 << i for i in range(places.bit_length() - 1)]

    def over_layers(value):
        return lax.ppermute(value, "pipe", [(i, (i + pipes // 2) % pipes) for i in range(pipes)])

    def small_sums(sums1, sums2, nsums1, nsums2):
        small = pick(sums2, sums1).reshape(count, 4 * width)
        kept, sent_sums = halves(small, ~first_core)
        sums = [nsums.sum(axis=1) for nsums in (nsums1, nsums2)]
        sums = jnp.stack([jnp.where(top, 0.0, sums[0]), jnp.where(top, sums[1], 0.0)], axis=1).reshape(-1, 4 * width)
        small = jnp.concatenate([kept, sums]) + core_swap(jnp.concatenate([sent_sums, sums]))
        return small

    def features(gx1, totals1):
        return feature_grads(gx1, source1, moments1, totals1, bn_gain[:1], category_columns, flat_table.shape)

    totals1 = nsums1
    used = columns // 2
    chain = [("",)] + [("sum", level) for level in levels_of_dp] + [("features",), ("cores",), ("layers",)]
    while lower.done < places - 1:
        act = chain.pop(0) if chain else ("",)
        if act[0] == "sum":
            got, = upper.step(((functools.partial(dp_swap, step=act[1]), totals1),))
            totals1 = totals1 + got
        elif act[0] == "features":
            numeric_back, table_sent, table = upper.step(work=(features, (gx1, totals1 / counted)))
        elif act[0] == "cores":
            got, = upper.step(((core_swap, table_sent),))
            table = plus(table, got)
        elif act[0] == "layers":
            got, got_sums = upper.step(((functools.partial(to_layer, up=True), table), (over_layers, small[half:])))
            high = lax.reduce_precision(jnp.concatenate([small[:half], small[half:] + got_sums]), 8, 7)
            low_part = jnp.concatenate([small[:half], small[half:] + got_sums]) - high
            table = jnp.concatenate([pick(got, table)[:used], jnp.concatenate([high, low_part], 1).astype(BF)])
        else:
            upper.step(ends=None if lower.done else (lambda held: held, (lower.held,)))
        if lower.done == 1:
            small, = lower.step(work=(small_sums, (sums1, sums2, nsums1, nsums2)))
        elif lower.done == 5:
            block, = lower.step(work=(layer_columns, (h2,)))
        elif lower.done == 6:
            numeric_part, = lower.step(work=(layer_columns, (numeric_back,)))
        elif lower.done == 2:
            gate_w, cand_w = lower.step(work=(lambda: blank_outputs(half, width), ()))
        else:
            lower.step()

    block_rows = upper.held.shape[0]
    unit = (1.0 + 0.0 * cardinalities[0].astype(F32)).astype(BF)
    turn = []
    own = Ring(held=jnp.concatenate([jnp.where(first_core, lower.held, upper.held), table]), unit=unit, turn=turn)
    other = Ring(held=core_swap(jnp.where(first_core, upper.held, lower.held)), unit=unit, turn=turn)
    mine, extra = [], None
    for s in range(places):
        mine.append(own.held)
        place = functools.partial(place_block, s, places)
        if extra is None:
            place = lambda a, b, *rest: place_block(0, places, a, b, None, *rest)
        values = (own.held, other.held, *(() if extra is None else (extra,)), gate_w, cand_w)
        if s == places - 1:
            gate_w, cand_w, extra = place(*values)
            break
        if s == places - 2:
            gate_w, cand_w, extra = own.step(ends=(place, values))
            extra = core_swap(extra)
            other.step()
            continue
        own.step()
        sends, ends, works = (), None, [(place, values)]
        if s == 1:
            sends = ((functools.partial(to_layer, up=False), block[:, 0]),
                     (functools.partial(to_layer, up=True), numeric_part[:, 1]))
        elif s == 5:
            works.append((lambda a, b, c, d: (pick(a, b), pick(c, d)),
                          (block[:, 1], got_block, got_numeric, numeric_part[:, 0])))
        outs = other.step(sends, works, ends, wait=False)
        if s == 1:
            got_block, got_numeric, *outs = outs
        gate_w, cand_w, extra, *outs = outs
        extra = core_swap(extra)
        if s == 5:
            block_out, numeric_grad = outs
    cand_w = place_extra(places - 1, places, core_swap(extra), cand_w)
    table, gate_b, cand_b, logit, gain, bias = spare_totals(mine, block_rows, used, mask_logits, feature_allow)
    table = joined(table, core_swap(table), ~first_core)
    table = jnp.swapaxes(table.reshape(columns, embed_width, levels), 1, 2)
    return (block_out, numeric_grad, table, gain, bias, logit,
            gate_w, gate_b, cand_w, cand_b)


def solution(mesh):
    in_specs = (P("dp", None), P("dp", None), P(), P(), P(), P(), P("pipe", None), P("pipe", None),
                P("pipe", None, None), P("pipe", None), P("pipe", None, None), P("pipe", None),
                P("dp", None))
    out_specs = (P("dp", "pipe"), P("dp", "pipe"), P(), P(), P(), P("pipe", None),
                 P("pipe", None, None), P("pipe", None), P("pipe", None, None), P("pipe", None))
    return jax.shard_map(on_device, mesh=mesh, in_specs=in_specs, out_specs=out_specs, check_vma=False)
```
